32 devices in a mesh: groups: 2 (over x), dom: 8 (over z, y), sub: 2 (over core).
Axes of the slice: x: 2, y: 2, z: 4, core: 2. Of those that a mesh axis runs over, the one named last changes fastest.
Arguments:
- node_latent: bfloat16 [98304, 128], P(('groups', 'dom', 'sub')), parts along dimension 0, may hold values from -6 to 6
- edge_latent: bfloat16 [589824, 128], P(('groups', 'dom', 'sub')), parts along dimension 0, may hold values from -6 to 6
- receivers: int32 [589824], P(('groups', 'dom', 'sub')), parts along dimension 0, may hold values from 0 to 49151, as said below
- senders: int32 [589824], P(('groups', 'dom', 'sub')), parts along dimension 0, may hold values from 0 to 49151, as said below
- coarse_map: int32 [98304], P(('groups', 'dom', 'sub')), parts along dimension 0, may hold values from 0 to 6143, as said below
- coarse_recv: int32 [73728], P(('groups', 'dom', 'sub')), parts along dimension 0, may hold values from 0 to 6143, as said below
- coarse_send: int32 [73728], P(('groups', 'dom', 'sub')), parts along dimension 0, may hold values from 0 to 6143, as said below
- edge_w1: bfloat16 [384, 128], replicated, may hold values from -0.3125 to 0.3125
- mod_u: bfloat16 [384, 32], replicated, may hold values from -0.3125 to 0.3125
- mod_v: bfloat16 [32, 128], replicated, may hold values from -1 to 1
- edge_w2: bfloat16 [128, 128], replicated, may hold values from -0.5 to 0.5
- edge_gain: float32 [128], replicated, may hold values from 0.5 to 1.5
- node_w1: bfloat16 [256, 128], replicated, may hold values from -0.375 to 0.375
- node_w2: bfloat16 [128, 128], replicated, may hold values from -0.5 to 0.5
- node_gain: float32 [128], replicated, may hold values from 0.5 to 1.5
- coarse_w1: bfloat16 [256, 128], replicated, may hold values from -0.375 to 0.375
- coarse_w2: bfloat16 [128, 128], replicated, may hold values from -0.5 to 0.5
- coarse_gain: float32 [128], replicated, may hold values from 0.5 to 1.5
Outputs:
- node_out: bfloat16 [98304, 128], P(('groups', 'dom', 'sub')), parts along dimension 0
- edge_out: bfloat16 [589824, 128], P(('groups', 'dom', 'sub')), parts along dimension 0
The draws below stay inside these ranges and needn't reach their ends.
There are 2 independent parts, one for each index of `groups`. The reference program is written for one: setup_inputs(seed, part) draws one part's arguments, and reference() takes and returns one part's arrays. A program takes and returns all parts, laid end to end along the dimension named above; an argument that names none is the same for every part. Nothing has to cross between parts.
Inputs may be any that keep to these rules, and one draw needn't show every extreme that they name: `receivers`: the edges form aligned blocks of 768; every edge of the k-th block has its receiver among nodes k * 128 to (k + 1) * 128 - 1. `senders`: each edge's sender differs from its receiver by at most 256. coarse_map[n] // 384 equals n // 3072. coarse_recv[k] // 384 equals k // 2304. With b = k // 2304, coarse_send[k] // 384 equals b or differs from b in exactly one bit.
All inputs are finite; a program needn't handle non-finite values.
Results may differ from the reference program's by a relative error of at most 0.0061.
Values may be sent and summed in bfloat16 or wider, within the bound.
No kernel may reach another device: no remote copies, remote signals or barrier semaphores. Data moves between devices by JAX's collectives and lax.ppermute only.
A program may use at most 128 MiB of HBM per device.

```python
import jax
import jax.numpy as jnp
from jax import lax

LAT = 128
RANK = 32
TILE = 128
BLOCKS = 24
DEG = 6
HALO = 256
CDEG = 6
COARSE_DEV = 384
NODES = 49152
EDGES = 294912
COARSE_ALL = 6144
LOGDEV = 4
N_DOM = 8
N_SUB = 2


def edge_pair(key):
    device_count = N_DOM * N_SUB
    node_rows = BLOCKS * TILE
    edge_rows = node_rows * DEG
    edge_total = device_count * edge_rows
    position = jnp.arange(edge_total, dtype=jnp.int32)
    owning_dev = position // edge_rows
    tile_index = position % edge_rows // (TILE * DEG)
    in_tile = position % (TILE * DEG)
    inside = jax.random.randint(jax.random.fold_in(key, 11), (edge_total,), 0, TILE, dtype=jnp.int32)
    inside = jnp.where(in_tile == 0, 0, jnp.where(in_tile == 1, TILE - 1, inside))
    recv_ids = owning_dev * node_rows + tile_index * TILE + inside
    offsets = jax.random.randint(jax.random.fold_in(key, 12), (edge_total,), -HALO, HALO + 1, dtype=jnp.int32)
    offsets = jnp.where(in_tile == 0, -HALO, jnp.where(in_tile == 1, HALO, offsets))
    send_ids = jnp.clip(recv_ids + offsets, 0, device_count * node_rows - 1)
    return (recv_ids, send_ids)


def coarse_pair(key):
    device_count = N_DOM * N_SUB
    edge_rows = COARSE_DEV * CDEG
    edge_total = device_count * edge_rows
    position = jnp.arange(edge_total, dtype=jnp.int32)
    owning_dev = position // edge_rows
    in_dev = position % edge_rows
    recv_inside = jax.random.randint(jax.random.fold_in(key, 21), (edge_total,), 0, COARSE_DEV, dtype=jnp.int32)
    recv_inside = jnp.where(in_dev == 0, 0, jnp.where(in_dev == 1, COARSE_DEV - 1, recv_inside))
    recv_ids = owning_dev * COARSE_DEV + recv_inside
    hop_pick = jax.random.randint(jax.random.fold_in(key, 22), (edge_total,), 0, LOGDEV + 1, dtype=jnp.int32)
    hop_pick = jnp.where(in_dev < 2, 0, hop_pick)
    flip_mask = jnp.where(hop_pick > 0, jnp.left_shift(jnp.ones_like(hop_pick), jnp.maximum(hop_pick - 1, 0)), 0)
    partner = jnp.bitwise_xor(owning_dev, flip_mask)
    send_inside = jax.random.randint(jax.random.fold_in(key, 23), (edge_total,), 0, COARSE_DEV, dtype=jnp.int32)
    send_inside = jnp.where(in_dev == 0, 0, jnp.where(in_dev == 1, COARSE_DEV - 1, send_inside))
    send_ids = partner * COARSE_DEV + send_inside
    return (recv_ids, send_ids)


def draw_receivers(key, part):
    shared = edge_pair(key)
    return shared[0]


def draw_senders(key, part):
    shared = edge_pair(key)
    return shared[1]


def draw_coarse_map(key, part):
    key = jax.random.fold_in(key, 3)
    node_rows = BLOCKS * TILE
    position = jnp.arange(NODES, dtype=jnp.int32)
    owning_dev = position // node_rows
    in_dev = position % node_rows
    inside = jax.random.randint(key, (NODES,), 0, COARSE_DEV, dtype=jnp.int32)
    inside = jnp.where(in_dev == 0, 0, jnp.where(in_dev == node_rows - 1, COARSE_DEV - 1, inside))
    return owning_dev * COARSE_DEV + inside


def draw_coarse_recv(key, part):
    shared = coarse_pair(key)
    return shared[0]


def draw_coarse_send(key, part):
    shared = coarse_pair(key)
    return shared[1]


def level_of(rng, extent, cuts, smallest, largest):
    def one(dim, blocks):
        draws = jax.random.uniform(jax.random.fold_in(jax.random.fold_in(rng, 6), dim), (blocks,), jnp.float32, smallest / len(cuts), largest / len(cuts))
        return jnp.repeat(jnp.exp(draws), extent[dim] // blocks).reshape((-1,) + (1,) * (len(extent) - dim - 1))

    gain = one(*cuts[0])
    for cut in cuts[1:]:
        gain = gain * one(*cut)
    return gain


def noise(rng, shape, deviation, bound, cuts=(), kind=jnp.bfloat16):
    drawn = deviation * jax.random.normal(rng, shape, jnp.float32)
    if cuts:
        drawn = drawn * level_of(rng, shape, cuts, -0.22, 0.18)
    return jnp.clip(drawn, -bound, bound).astype(kind)


def setup_inputs(seed: int = 0, part: int = 0) -> dict:
    key_list = jax.random.split(jax.random.key(seed), 19)
    own_keys = jax.random.split(jax.random.fold_in(key_list[18], part), 19)
    node_latent = noise(own_keys[0], (NODES, LAT), 1.0, 6.0, ((0, 16),))
    edge_latent = noise(own_keys[1], (EDGES, LAT), 1.0, 6.0, ((0, 16),))
    receivers = draw_receivers(jax.random.fold_in(jax.random.fold_in(key_list[18], part), 71), part)
    senders = draw_senders(jax.random.fold_in(jax.random.fold_in(key_list[18], part), 71), part)
    coarse_map = draw_coarse_map(jax.random.fold_in(jax.random.fold_in(key_list[18], part), 71), part)
    coarse_recv = draw_coarse_recv(jax.random.fold_in(jax.random.fold_in(key_list[18], part), 71), part)
    coarse_send = draw_coarse_send(jax.random.fold_in(jax.random.fold_in(key_list[18], part), 71), part)
    edge_w1 = noise(key_list[7], (3 * LAT, LAT), (3 * LAT) ** -0.5, 0.3125)
    mod_u = noise(key_list[8], (3 * LAT, RANK), (3 * LAT) ** -0.5, 0.3125)
    mod_v = noise(key_list[9], (RANK, LAT), RANK ** -0.5, 1.0)
    edge_w2 = noise(key_list[10], (LAT, LAT), LAT ** -0.5, 0.5)
    edge_gain = jnp.clip(1.0 + 0.1 * jax.random.normal(key_list[11], (LAT,), jnp.float32), 0.5, 1.5)
    node_w1 = noise(key_list[12], (2 * LAT, LAT), (2 * LAT) ** -0.5, 0.375)
    node_w2 = noise(key_list[13], (LAT, LAT), LAT ** -0.5, 0.5)
    node_gain = jnp.clip(1.0 + 0.1 * jax.random.normal(key_list[14], (LAT,), jnp.float32), 0.5, 1.5)
    coarse_w1 = noise(key_list[15], (2 * LAT, LAT), (2 * LAT) ** -0.5, 0.375)
    coarse_w2 = noise(key_list[16], (LAT, LAT), LAT ** -0.5, 0.5)
    coarse_gain = jnp.clip(1.0 + 0.1 * jax.random.normal(key_list[17], (LAT,), jnp.float32), 0.5, 1.5)
    return {"node_latent": node_latent, "edge_latent": edge_latent, "receivers": receivers, "senders": senders, "coarse_map": coarse_map, "coarse_recv": coarse_recv, "coarse_send": coarse_send, "edge_w1": edge_w1, "mod_u": mod_u, "mod_v": mod_v, "edge_w2": edge_w2, "edge_gain": edge_gain, "node_w1": node_w1, "node_w2": node_w2, "node_gain": node_gain, "coarse_w1": coarse_w1, "coarse_w2": coarse_w2, "coarse_gain": coarse_gain}


def layer_norm(values, gain_vec):
    average = lax.optimization_barrier(jnp.mean(values, axis=-1, keepdims=True))
    centred = values - average
    spread = lax.optimization_barrier(jnp.mean(centred * centred, axis=-1, keepdims=True))
    return centred * lax.rsqrt(spread + 1e-05) * gain_vec

def reference(node_latent, edge_latent, receivers, senders, coarse_map, coarse_recv, coarse_send, edge_w1, mod_u, mod_v, edge_w2, edge_gain, node_w1, node_w2, node_gain, coarse_w1, coarse_w2, coarse_gain):
    device_count = N_DOM * N_SUB
    edge_rows = BLOCKS * TILE * DEG

    def edge_block(operands):
        edges, recv_ids, send_ids = operands
        edge_in = jnp.concatenate([edges, node_latent[send_ids], node_latent[recv_ids]], axis=1)
        low_rank = jnp.dot(edge_in, mod_u, preferred_element_type=jnp.float32).astype(jnp.bfloat16)
        preact = jnp.dot(edge_in, edge_w1, preferred_element_type=jnp.float32) + jnp.dot(low_rank, mod_v, preferred_element_type=jnp.float32)
        edge_hidden = jax.nn.silu(preact).astype(jnp.bfloat16)
        update = jnp.dot(edge_hidden, edge_w2, preferred_element_type=jnp.float32)
        return (edges.astype(jnp.float32) + layer_norm(update, edge_gain)).astype(jnp.bfloat16)
    edge_out = lax.map(edge_block, (edge_latent.reshape(device_count, edge_rows, LAT), receivers.reshape(device_count, edge_rows), senders.reshape(device_count, edge_rows))).reshape(EDGES, LAT)
    incoming = jax.ops.segment_sum(edge_out.astype(jnp.float32), receivers, num_segments=NODES).astype(jnp.bfloat16)
    node_in = jnp.concatenate([node_latent, incoming], axis=1)
    node_hidden = jax.nn.silu(jnp.dot(node_in, node_w1, preferred_element_type=jnp.float32)).astype(jnp.bfloat16)
    node_update = jnp.dot(node_hidden, node_w2, preferred_element_type=jnp.float32)
    fine_new = (node_latent.astype(jnp.float32) + layer_norm(node_update, node_gain)).astype(jnp.bfloat16)
    coarse_sum = jax.ops.segment_sum(fine_new.astype(jnp.float32), coarse_map, num_segments=COARSE_ALL)
    counts = jax.ops.segment_sum(jnp.ones((NODES,), jnp.float32), coarse_map, num_segments=COARSE_ALL)
    coarse_latent = (coarse_sum / jnp.maximum(counts, 1.0)[:, None]).astype(jnp.bfloat16)
    coarse_in_rows = jnp.concatenate([coarse_latent[coarse_send], coarse_latent[coarse_recv]], axis=1)
    coarse_hidden = jax.nn.silu(jnp.dot(coarse_in_rows, coarse_w1, preferred_element_type=jnp.float32)).astype(jnp.bfloat16)
    coarse_msg = jnp.dot(coarse_hidden, coarse_w2, preferred_element_type=jnp.float32).astype(jnp.bfloat16)
    coarse_in = jax.ops.segment_sum(coarse_msg.astype(jnp.float32), coarse_recv, num_segments=COARSE_ALL)
    coarse_delta = layer_norm(coarse_latent.astype(jnp.float32) + coarse_in, coarse_gain).astype(jnp.bfloat16)
    node_out = (fine_new.astype(jnp.float32) + coarse_delta[coarse_map].astype(jnp.float32)).astype(jnp.bfloat16)
    return (node_out, edge_out)
```

```python
import functools

import jax
import jax.numpy as jnp
from jax import lax
from jax.experimental import pallas as pl
from jax.experimental.pallas import tpu as pltpu
from jax.sharding import PartitionSpec as P

TILE = 128
HALO = 256
COARSEN = 8
STEP = 4
BF = jnp.bfloat16
F32 = jnp.float32


def dot(a, b):
    return jnp.dot(a, b, preferred_element_type=F32)


def silu(x):
    y = 0.5 * x
    return y * jnp.tanh(y) + y


def one_hot(mask):
    return jnp.where(mask, 1.0, 0.0).astype(BF)


def centred_weight(w):
    w = w.astype(F32)
    return (w - jnp.mean(w, axis=1, keepdims=True)).astype(BF)


def twice(w):
    z = jnp.zeros_like(w)
    return jnp.concatenate(
        [jnp.concatenate([w, z], axis=1), jnp.concatenate([z, w], axis=1)], axis=0
    )


def pair_dot(x, w2):
    half = x.shape[0] // 2
    out = dot(jnp.concatenate([x[:half], x[half:]], axis=1), w2)
    n = out.shape[1] // 2
    return jnp.concatenate([out[:, :n], out[:, n:]], axis=0)


def fine_kernel(
    edge_ref, send_ref, recv_ref, before_ref, own_ref, after_ref, cmap_ref, base_ref,
    w1_ref, u_ref, v_ref, w2_ref, gain_ref, nw1_ref, nw2_ref, ngain_ref,
    edge_out_ref, fine_ref, coarse_ref,
    sent_s, recv_s, we_s, w2_s, nw2_s, ones_s, pool_s,
):
    step = pl.program_id(0)
    lat = own_ref.shape[1]
    rows = own_ref.shape[0]
    window = TILE + 2 * HALO
    groups = send_ref.shape[0] // STEP
    crows = coarse_ref.shape[0]

    @pl.when(step == 0)
    def _():
        w_eff = (w1_ref[...].astype(F32) + dot(u_ref[...], v_ref[...])).astype(BF)
        we_s[...] = twice(w_eff[:lat])
        ws = w_eff[lat : 2 * lat]
        sent_s[0:HALO] = dot(before_ref[...], ws).astype(BF)
        sent_s[HALO : HALO + rows] = dot(own_ref[...], ws).astype(BF)
        sent_s[HALO + rows :] = dot(after_ref[...], ws).astype(BF)
        recv_s[...] = dot(own_ref[...], w_eff[2 * lat :]).astype(BF)
        w2_s[...] = twice(centred_weight(w2_ref[...]))
        nw2_s[...] = twice(centred_weight(nw2_ref[...]))
        ones_s[...] = twice(jnp.full((lat, lat), 1.0 / lat, BF))
        pool_s[...] = jnp.zeros_like(pool_s)

    lane = lax.broadcasted_iota(jnp.int32, (TILE, TILE), 1)
    sub = lax.broadcasted_iota(jnp.int32, (TILE, TILE), 0)
    recv = recv_ref[...]
    loc = recv & (TILE - 1)
    off = send_ref[...] - (recv - loc) + HALO
    loc_t = loc.T
    off_t = off.T
    gain = gain_ref[...]
    incoming = []
    for k in range(STEP):
        start = pl.multiple_of((step * STEP + k) * TILE, TILE)
        rhs = jnp.concatenate(
            [sent_s[pl.ds(start, window)], recv_s[pl.ds(start, TILE)]], axis=0
        )
        lhs = []
        for j in range(groups):
            col = k * groups + j
            o = jnp.broadcast_to(off_t[:, col : col + 1], (TILE, TILE))
            r = jnp.broadcast_to(loc_t[:, col : col + 1], (TILE, TILE))
            parts = [one_hot(o == lane + c * TILE) for c in range(window // TILE)]
            parts.append(one_hot(r == lane))
            lhs.append(jnp.concatenate(parts, axis=1))
        lhs = jnp.concatenate(lhs, axis=0)
        e0 = k * groups * TILE
        edges = edge_ref[e0 : e0 + groups * TILE]
        preact = dot(lhs, rhs) + pair_dot(edges, we_s[...])
        hidden = silu(preact).astype(BF)
        c = pair_dot(hidden, w2_s[...])
        var = pair_dot((c * c).astype(BF), ones_s[...])
        new = (edges.astype(F32) + c * lax.rsqrt(var + 1e-05) * gain).astype(BF)
        edge_out_ref[e0 : e0 + groups * TILE] = new
        back = jnp.concatenate(
            [
                one_hot(loc[k * groups + j : k * groups + j + 1] == sub)
                for j in range(groups)
            ],
            axis=1,
        )
        incoming.append(dot(back, new).astype(BF))
    incoming = jnp.concatenate(incoming, axis=0)
    start = pl.multiple_of(step * STEP * TILE, STEP * TILE)
    own = own_ref[pl.ds(start, STEP * TILE)]
    hidden = silu(dot(jnp.concatenate([own, incoming], axis=1), nw1_ref[...])).astype(BF)
    c = pair_dot(hidden, nw2_s[...])
    var = pair_dot((c * c).astype(BF), ones_s[...])
    fine = (own.astype(F32) + c * lax.rsqrt(var + 1e-05) * ngain_ref[...]).astype(BF)
    fine_ref[...] = fine
    csub = lax.broadcasted_iota(jnp.int32, (crows, TILE), 0) + base_ref[0] * crows
    member = jnp.concatenate(
        [
            one_hot(cmap_ref[pl.ds(step * STEP + k, 1), :] == csub)
            for k in range(STEP)
        ],
        axis=1,
    )
    pool_s[...] += dot(member, jnp.concatenate([fine, jnp.ones_like(fine)], axis=1))

    @pl.when(step == pl.num_programs(0) - 1)
    def _():
        total = pool_s[...]
        coarse_ref[...] = (total[:, :lat] / jnp.maximum(total[:, lat:], 1.0)).astype(BF)


def coarse_kernel(
    base_ref, send_ref, recv_ref, cmap_ref, fine_ref, w1_ref, w2_ref, gain_ref, *rest
):
    tables, out_ref = rest[:-1], rest[-1]
    dev = base_ref[0]
    crows, lat = tables[0].shape
    rows = send_ref.shape[0]
    send = send_ref[...]
    owner = lax.div(send, jnp.full_like(send, crows))
    other = owner ^ dev
    slot = jnp.zeros_like(send)
    for j in range(len(tables) - 1):
        slot = jnp.where(other == (1 << j), j + 1, slot)
    off = send - owner * crows + slot * crows
    loc = recv_ref[...] - dev * crows
    ws = w1_ref[:lat]
    proj = [dot(t[...], ws).astype(BF) for t in tables]
    own = tables[0][...]
    proj.append(dot(own, w1_ref[lat:]).astype(BF))
    rhs = jnp.concatenate(proj, axis=0)
    lane = lax.broadcasted_iota(jnp.int32, (TILE, TILE), 1)
    off_t = off.T
    loc_t = loc.T
    chunks = crows // TILE
    csub = lax.broadcasted_iota(jnp.int32, (crows, TILE), 0)
    group = 6 if rows % 6 == 0 else 1
    total = own.astype(F32)
    for g in range(rows // group):
        lhs = []
        for j in range(group):
            col = g * group + j
            o = jnp.broadcast_to(off_t[:, col : col + 1], (TILE, TILE))
            r = jnp.broadcast_to(loc_t[:, col : col + 1], (TILE, TILE))
            parts = [one_hot(o == lane + c * TILE) for c in range(chunks * len(tables))]
            parts += [one_hot(r == lane + c * TILE) for c in range(chunks)]
            lhs.append(jnp.concatenate(parts, axis=1))
        hidden = silu(dot(jnp.concatenate(lhs, axis=0), rhs)).astype(BF)
        msg = dot(hidden, w2_ref[...]).astype(BF)
        back = jnp.concatenate(
            [one_hot(loc[g * group + j : g * group + j + 1] == csub) for j in range(group)],
            axis=1,
        )
        total = total + dot(back, msg)
    centred = total - jnp.mean(total, axis=1, keepdims=True)
    var = jnp.mean(centred * centred, axis=1, keepdims=True)
    delta = (centred * lax.rsqrt(var + 1e-05) * gain_ref[...]).astype(BF)
    cm_t = (cmap_ref[...] - dev * crows).T
    for t in range(cmap_ref.shape[0]):
        m = jnp.broadcast_to(cm_t[:, t : t + 1], (TILE, TILE))
        hot = jnp.concatenate([one_hot(m == lane + c * TILE) for c in range(chunks)], axis=1)
        sl = slice(t * TILE, (t + 1) * TILE)
        out_ref[sl] = (fine_ref[sl].astype(F32) + dot(hot, delta)).astype(BF)


def on_device(
    node_latent, edge_latent, receivers, senders, coarse_map, coarse_recv, coarse_send,
    edge_w1, mod_u, mod_v, edge_w2, edge_gain, node_w1, node_w2, node_gain,
    coarse_w1, coarse_w2, coarse_gain,
):
    axes = ("dom", "sub")
    size = lax.axis_size(axes)
    dev = lax.axis_index(axes).astype(jnp.int32).reshape(1)
    nodes, lat = node_latent.shape
    edges = edge_latent.shape[0]
    tiles = nodes // TILE
    per = edges // tiles
    crows = nodes // COARSEN
    steps = tiles // STEP
    up = [(i, i + 1) for i in range(size - 1)]
    down = [(j, i) for i, j in up]
    before = lax.ppermute(node_latent[nodes - HALO :], axes, up)
    after = lax.ppermute(node_latent[:HALO], axes, down)
    send2 = senders.reshape(edges // TILE, TILE)
    recv2 = receivers.reshape(edges // TILE, TILE)
    cmap2 = coarse_map.reshape(tiles, TILE)
    vm = pl.BlockSpec(memory_space=pltpu.VMEM)
    sm = pl.BlockSpec(memory_space=pltpu.SMEM)
    idx = pl.BlockSpec((STEP * per // TILE, TILE), lambda i: (i, 0))
    edge_out, fine, coarse = pl.pallas_call(
        fine_kernel,
        grid=(steps,),
        in_specs=[pl.BlockSpec((STEP * per, lat), lambda i: (i, 0)), idx, idx]
        + [vm] * 4 + [sm] + [vm] * 8,
        out_specs=[
            pl.BlockSpec((STEP * per, lat), lambda i: (i, 0)),
            pl.BlockSpec((STEP * TILE, lat), lambda i: (i, 0)),
            pl.BlockSpec((crows, lat), lambda i: (0, 0)),
        ],
        out_shape=[
            jax.ShapeDtypeStruct((edges, lat), BF),
            jax.ShapeDtypeStruct((nodes, lat), BF),
            jax.ShapeDtypeStruct((crows, lat), BF),
        ],
        scratch_shapes=[
            pltpu.VMEM((nodes + 2 * HALO, lat), BF),
            pltpu.VMEM((nodes, lat), BF),
            pltpu.VMEM((2 * lat, 2 * lat), BF),
            pltpu.VMEM((2 * lat, 2 * lat), BF),
            pltpu.VMEM((2 * lat, 2 * lat), BF),
            pltpu.VMEM((2 * lat, 2 * lat), BF),
            pltpu.VMEM((crows, 2 * lat), F32),
        ],
        compiler_params=pltpu.CompilerParams(
            dimension_semantics=("arbitrary",), vmem_limit_bytes=48 * 2**20
        ),
        name="fine",
    )(
        edge_latent, send2, recv2, before, node_latent, after, cmap2, dev,
        edge_w1, mod_u, mod_v, edge_w2, edge_gain.reshape(1, lat),
        node_w1, node_w2, node_gain.reshape(1, lat),
    )
    tables = [coarse]
    bit = 1
    while bit < size:
        tables.append(lax.ppermute(coarse, axes, [(i, i ^ bit) for i in range(size)]))
        bit *= 2
    cedges = coarse_send.shape[0]
    node_out = pl.pallas_call(
        coarse_kernel,
        in_specs=[sm] + [vm] * (7 + len(tables)),
        out_specs=vm,
        out_shape=jax.ShapeDtypeStruct((nodes, lat), BF),
        compiler_params=pltpu.CompilerParams(vmem_limit_bytes=48 * 2**20),
        name="coarse",
    )(
        dev, coarse_send.reshape(cedges // TILE, TILE), coarse_recv.reshape(cedges // TILE, TILE),
        cmap2, fine, coarse_w1, coarse_w2, coarse_gain.reshape(1, lat), *tables,
    )
    return (node_out, edge_out)


def solution(mesh):
    split = P(("groups", "dom", "sub"))
    wide = P(("groups", "dom", "sub"), None)
    return jax.shard_map(
        on_device,
        mesh=mesh,
        in_specs=(wide, wide) + (split,) * 5 + (P(),) * 11,
        out_specs=(wide, wide),
        check_vma=False,
    )
```

```python
import functools

import jax
import jax.numpy as jnp
from jax import lax
from jax.experimental import pallas as pl
from jax.experimental.pallas import tpu as pltpu
from jax.sharding import PartitionSpec as P

TILE = 128
HALO = 256
COARSEN = 8
STEP = 2
PARTS = 2
PAD = 16
BF = jnp.bfloat16
F32 = jnp.float32
I16 = jnp.int16


def dot(a, b):
    return jnp.dot(a, b, preferred_element_type=F32)


def one_hot(mask):
    return jnp.where(mask, jnp.ones((), BF), jnp.zeros((), BF))


def pick(off, lane, blocks):
    return [one_hot(off == lane + I16(c * TILE)) for c in range(blocks)]


def column(rows_t, col):
    return jnp.broadcast_to(rows_t[:, col : col + 1], (TILE, TILE))


def along_lanes(row, count):
    return jnp.broadcast_to(row, (count, TILE)).astype(I16)


def twice(w):
    z = jnp.zeros_like(w)
    return jnp.concatenate(
        [jnp.concatenate([w, z], axis=1), jnp.concatenate([z, w], axis=1)], axis=0
    )


def pair_dot(x, w2):
    half = x.shape[0] // 2
    out = dot(jnp.concatenate([x[:half], x[half:]], axis=1), w2)
    n = out.shape[1] // 2
    return jnp.concatenate([out[:, :n], out[:, n:]], axis=0)


def gained(w, gain):
    w = w.astype(F32)
    return twice(((w - jnp.mean(w, axis=1, keepdims=True)) * gain).astype(BF))


def mean_weight(gain):
    lat = gain.shape[1]
    return twice(jnp.broadcast_to(1.0 / (gain * gain * lat), (lat, lat)).T.astype(BF))


def norm(hidden, w, m):
    c = pair_dot(hidden, w)
    return c * lax.rsqrt(pair_dot((c * c).astype(BF), m) + 1e-05)


def half_silu(y):
    return (y * jnp.tanh(y) + y).astype(BF)


def fine_kernel(base_ref, edge_ref, last_ref, before_ref, after_ref, *refs):
    hbm, refs = refs[:12], refs[12:]
    (edge_out_ref, fine_ref, coarse_ref), refs = refs[:3], refs[3:]
    vmem, refs = refs[:12], refs[12:]
    own_ref, send_ref, recv_ref, cmap_ref, w1_ref, u_ref, v_ref = vmem[:7]
    edge_w2_ref, nw1_ref, node_w2_ref, gain_ref, ngain_ref = vmem[7:]
    sent_s, recv_s, we_s, w2_s, m_s, nw1_s, nw2_s, nm_s, code_s, loc_s, hid_s, inc_s, pool_s, sem = refs
    step = pl.program_id(0)
    steps = pl.num_programs(0) - 2
    rows, lat = own_ref.shape
    per = edge_ref.shape[0] // STEP
    groups = per // TILE
    idx_rows = STEP * groups
    crows = coarse_ref.shape[0]
    low_blocks = 3
    high_blocks = (TILE + 2 * HALO) // TILE - low_blocks

    @pl.when(step == 0)
    def _():
        copies = [pltpu.make_async_copy(a, b, sem.at[i]) for i, (a, b) in enumerate(zip(hbm, vmem))]
        for c in copies:
            c.start()
        for c in copies:
            c.wait()
        w_eff = w1_ref[...].astype(F32) + lax.dot_general(
            u_ref[...], v_ref[...], (((0,), (0,)), ((), ())), preferred_element_type=F32
        )
        w_eff = (0.5 * w_eff).astype(BF)
        we_s[...] = twice(w_eff[:lat])
        ws = w_eff[lat : 2 * lat]
        both = dot(own_ref[...], jnp.concatenate([ws, w_eff[2 * lat :]], axis=1)).astype(BF)
        sent_s[0:HALO] = dot(before_ref[...], ws).astype(BF)
        sent_s[HALO : HALO + rows] = both[:, :lat]
        sent_s[HALO + rows :] = dot(after_ref[...], ws).astype(BF)
        recv_s[...] = both[:, lat:]
        w2_s[...] = gained(edge_w2_ref[...], gain_ref[...])
        m_s[...] = mean_weight(gain_ref[...])
        nw2_s[...] = gained(node_w2_ref[...], ngain_ref[...])
        nm_s[...] = mean_weight(ngain_ref[...])
        nw1_s[...] = nw1_ref[...] * 0.5
        pool_s[...] = jnp.zeros_like(pool_s)
        recv = recv_ref[...]
        loc = recv & (TILE - 1)
        off = send_ref[...] - (recv - loc) + HALO
        hi = off >= low_blocks * TILE
        lo = jnp.where(hi, off - low_blocks * TILE, off)
        code = lo | (loc << 16) | jnp.where(hi, jnp.int32(-(2**31)), 0)
        for s in range(rows // TILE // STEP):
            sl = slice(s * idx_rows, (s + 1) * idx_rows)
            code_s[s, :, 0:idx_rows] = code[sl].T
            loc_s[s, 0:idx_rows] = loc[sl]

    this, prev, past = step, step - 1, step - 2
    part = per // PARTS
    lane = lax.broadcasted_iota(I16, (TILE, TILE), 1)
    sub = lax.broadcasted_iota(I16, (TILE, TILE), 0)
    csub = lax.broadcasted_iota(I16, (crows, TILE), 0)
    incoming = [[] for _ in range(STEP)]

    def weights(k):
        start = pl.multiple_of((this * STEP + k) * TILE, TILE)
        mine = recv_s[pl.ds(start, TILE)]
        low = jnp.concatenate([sent_s[pl.ds(start, low_blocks * TILE)], mine], axis=0)
        high = jnp.concatenate(
            [
                sent_s[pl.ds(start + low_blocks * TILE, high_blocks * TILE)],
                sent_s[pl.ds(start, (low_blocks - high_blocks) * TILE)],
                mine,
            ],
            axis=0,
        )
        return jnp.concatenate([low, high], axis=1)

    def first(k, q):
        at = slice(k * per + q * part, k * per + (q + 1) * part)
        code_t = code_s[this]
        lhs, upper = [], []
        for j in range(part // TILE):
            word = column(code_t, at.start // TILE + j)
            o = word.astype(I16) & I16(511)
            r = (word >> 16).astype(I16) & I16(TILE - 1)
            lhs.append(jnp.concatenate(pick(o, lane, low_blocks) + pick(r, lane, 1), axis=1))
            upper.append(word < 0)
        out = dot(jnp.concatenate(lhs, axis=0), weights(k))
        y = pair_dot(edge_ref[at], we_s[...])
        yield
        y = y + jnp.where(jnp.concatenate(upper, axis=0), out[:, lat:], out[:, :lat])
        hid_s[at] = half_silu(y)

    def second(k, q):
        at = slice(k * per + q * part, k * per + (q + 1) * part)
        c = pair_dot(hid_s[at], w2_s[...])
        yield
        var = pair_dot((c * c).astype(BF), m_s[...])
        yield
        new = (last_ref[at].astype(F32) + c * lax.rsqrt(var + 1e-05)).astype(BF)
        edge_out_ref[at] = new
        loc = loc_s[prev]
        back = [
            one_hot(along_lanes(loc[j : j + 1], TILE) == sub)
            for j in range(at.start // TILE, at.stop // TILE)
        ]
        incoming[k].append(dot(jnp.concatenate(back, axis=1), new))
        yield
        if q == PARTS - 1:
            inc_s[k * TILE : (k + 1) * TILE] = sum(incoming[k][1:], incoming[k][0]).astype(BF)

    def third():
        here = pl.ds(pl.multiple_of(past * STEP * TILE, STEP * TILE), STEP * TILE)
        own = own_ref[here]
        y = dot(jnp.concatenate([own, inc_s[...]], axis=1), nw1_s[...])
        yield
        c = pair_dot(half_silu(y), nw2_s[...])
        yield
        var = pair_dot((c * c).astype(BF), nm_s[...])
        yield
        fine = (own.astype(F32) + c * lax.rsqrt(var + 1e-05)).astype(BF)
        fine_ref[here] = fine
        member = []
        for k in range(STEP):
            local = cmap_ref[pl.ds(past * STEP + k, 1), :] - base_ref[0] * crows
            member.append(one_hot(along_lanes(local, crows) == csub))
        fine = jnp.concatenate([fine, jnp.ones_like(fine)], axis=1)
        pool_s[...] += dot(jnp.concatenate(member, axis=1), fine)

    def stages(one, two, three):
        for k in range(STEP):
            incoming[k].clear()
        active = [third()] if three else []
        todo = [(k, q) for k in range(STEP) for q in range(PARTS)] if one or two else []
        while active or todo:
            if todo:
                k, q = todo.pop(0)
                active = [second(k, q)] * two + [first(k, q)] * one + active
            alive = []
            for g in active:
                try:
                    next(g)
                    alive.append(g)
                except StopIteration:
                    pass
            active = alive

    full = (step >= 2) & (step < steps)
    for when, which in (
        (full, (True, True, True)),
        (step == 0, (True, False, False)),
        (step == 1, (True, True, False)),
        (step == steps, (False, True, True)),
        (step == steps + 1, (False, False, True)),
    ):
        pl.when(when)(functools.partial(stages, *which))

    @pl.when(step == steps + 1)
    def _():
        total = pool_s[...]
        coarse_ref[...] = (total[:, :lat] / jnp.maximum(total[:, lat:], 1.0)).astype(BF)


def coarse_kernel(
    base_ref, send_ref, recv_ref, cmap_ref, fine_ref, w1_ref, w2_ref, gain_ref, *refs
):
    tables, (out_ref, out_s, sem) = refs[:-3], refs[-3:]
    dev = base_ref[0]
    crows, lat = tables[0].shape
    rows = send_ref.shape[0]
    nodes = fine_ref.shape[0]
    chunks = crows // TILE
    blocks = chunks * len(tables)
    lows = (blocks + 1) // 2
    send = send_ref[...]
    owner = lax.div(send, jnp.full_like(send, crows))
    other = owner ^ dev
    slot = jnp.zeros_like(send)
    for j in range(len(tables) - 1):
        slot = jnp.where(other == (1 << j), j + 1, slot)
    off = send - owner * crows + slot * crows
    hi = off >= lows * TILE
    lo = jnp.where(hi, off - lows * TILE, off)
    loc = recv_ref[...] - dev * crows
    w1 = w1_ref[...] * 0.5
    proj = jnp.concatenate([dot(t[...], w1[:lat]).astype(BF) for t in tables], axis=0)
    own = tables[0][...]
    mine = dot(own, w1[lat:]).astype(BF)
    low = proj[: lows * TILE]
    high = proj[lows * TILE :]
    if high.shape[0] < low.shape[0]:
        high = jnp.concatenate([high, low[high.shape[0] :]], axis=0)
    rhs = jnp.concatenate(
        [jnp.concatenate([low, mine], axis=0), jnp.concatenate([high, mine], axis=0)], axis=1
    )
    lane = lax.broadcasted_iota(I16, (TILE, TILE), 1)
    lo_t, hi_t, loc_t = lo.T, hi.astype(jnp.int32).T, loc.T
    csub = lax.broadcasted_iota(I16, (crows, TILE), 0)
    w2 = twice(w2_ref[...])
    group = 6 if rows % 6 == 0 else 1
    total = own.astype(F32)
    for g in range(rows // group):
        lhs, upper, back = [], [], []
        for j in range(group):
            col = g * group + j
            o = column(lo_t, col).astype(I16)
            r = column(loc_t, col).astype(I16)
            lhs.append(jnp.concatenate(pick(o, lane, lows) + pick(r, lane, chunks), axis=1))
            upper.append(column(hi_t, col) > 0)
            back.append(one_hot(along_lanes(loc[col : col + 1], crows) == csub))
        out = dot(jnp.concatenate(lhs, axis=0), rhs)
        y = jnp.where(jnp.concatenate(upper, axis=0), out[:, lat:], out[:, :lat])
        msg = pair_dot(half_silu(y), w2).astype(BF)
        total = total + dot(jnp.concatenate(back, axis=1), msg)
    centred = total - jnp.mean(total, axis=1, keepdims=True)
    var = jnp.mean(centred * centred, axis=1, keepdims=True)
    delta = (centred * lax.rsqrt(var + 1e-05) * gain_ref[...]).astype(BF)
    half = (chunks + 1) // 2
    high = delta[half * TILE :]
    if high.shape[0] < half * TILE:
        high = jnp.concatenate([high, delta[high.shape[0] : half * TILE]], axis=0)
    rhs = jnp.concatenate([delta[: half * TILE], high], axis=1)
    cm = cmap_ref[...] - dev * crows
    hi = cm >= half * TILE
    lo_t = jnp.where(hi, cm - half * TILE, cm).T
    hi_t = hi.astype(jnp.int32).T
    tiles = nodes // TILE
    part = 6 if tiles % 6 == 0 else 1
    copies = []
    for p in range(tiles // part):
        hot, upper = [], []
        for t in range(p * part, (p + 1) * part):
            hot.append(jnp.concatenate(pick(column(lo_t, t).astype(I16), lane, half), axis=1))
            upper.append(column(hi_t, t) > 0)
        out = dot(jnp.concatenate(hot, axis=0), rhs)
        back = jnp.where(jnp.concatenate(upper, axis=0), out[:, lat:], out[:, :lat])
        sl = pl.ds(p * part * TILE, part * TILE)
        out_s[sl] = (fine_ref[sl].astype(F32) + back).astype(BF)
        copies.append(pltpu.make_async_copy(out_s.at[sl], out_ref.at[sl], sem.at[p]))
        copies[-1].start()
    for c in copies:
        c.wait()


def on_device(
    node_latent, edge_latent, receivers, senders, coarse_map, coarse_recv, coarse_send,
    edge_w1, mod_u, mod_v, edge_w2, edge_gain, node_w1, node_w2, node_gain,
    coarse_w1, coarse_w2, coarse_gain,
):
    axes = ("dom", "sub")
    size = lax.axis_size(axes)
    dev = lax.axis_index(axes).astype(jnp.int32).reshape(1)
    nodes, lat = node_latent.shape
    edges = edge_latent.shape[0]
    tiles = nodes // TILE
    per = edges // tiles
    crows = nodes // COARSEN
    steps = tiles // STEP
    up = [(i, i + 1) for i in range(size - 1)]
    down = [(j, i) for i, j in up]
    before = lax.ppermute(node_latent[nodes - HALO :], axes, up)
    after = lax.ppermute(node_latent[:HALO], axes, down)
    cmap2 = coarse_map.reshape(tiles, TILE)
    vm = pl.BlockSpec(memory_space=pltpu.VMEM)
    sm = pl.BlockSpec(memory_space=pltpu.SMEM)
    hb = pl.BlockSpec(memory_space=pltpu.HBM)
    hbm = (
        node_latent, senders.reshape(edges // TILE, TILE), receivers.reshape(edges // TILE, TILE),
        cmap2, edge_w1, mod_u.T, mod_v, edge_w2, node_w1, node_w2,
        edge_gain.reshape(1, lat), node_gain.reshape(1, lat),
    )
    big = (STEP * per, lat)
    index = pltpu.VMEM((steps, PAD, TILE), jnp.int32)
    square = pltpu.VMEM((2 * lat, 2 * lat), BF)
    far = pltpu.with_memory_space_constraint(edge_latent, pltpu.HBM)
    edge_out, fine, coarse = pl.pallas_call(
        fine_kernel,
        grid=(steps + 2,),
        in_specs=[
            sm,
            pl.BlockSpec(big, lambda i: (jnp.minimum(i, steps - 1), 0)),
            pl.BlockSpec(big, lambda i: (jnp.clip(i - 1, 0, steps - 1), 0)),
            vm, vm,
        ] + [hb] * len(hbm),
        out_specs=[pl.BlockSpec(big, lambda i: (jnp.clip(i - 1, 0, steps - 1), 0)), vm, vm],
        out_shape=[
            jax.ShapeDtypeStruct((edges, lat), BF),
            jax.ShapeDtypeStruct((nodes, lat), BF),
            jax.ShapeDtypeStruct((crows, lat), BF),
        ],
        scratch_shapes=[pltpu.VMEM(a.shape, a.dtype) for a in hbm] + [
            pltpu.VMEM((nodes + 2 * HALO, lat), BF),
            pltpu.VMEM((nodes, lat), BF),
            square, square, square,
            pltpu.VMEM((2 * lat, lat), BF),
            square, square,
            pltpu.VMEM((steps, TILE, PAD), jnp.int32),
            index,
            pltpu.VMEM(big, BF),
            pltpu.VMEM((STEP * TILE, lat), BF),
            pltpu.VMEM((crows, 2 * lat), F32),
            pltpu.SemaphoreType.DMA((len(hbm),)),
        ],
        compiler_params=pltpu.CompilerParams(
            dimension_semantics=("arbitrary",), vmem_limit_bytes=48 * 2**20
        ),
        name="fine",
    )(dev, far, far, before, after, *[pltpu.with_memory_space_constraint(a, pltpu.HBM) for a in hbm])
    tables = [coarse]
    bit = 1
    while bit < size:
        tables.append(lax.ppermute(coarse, axes, [(i, i ^ bit) for i in range(size)]))
        bit *= 2
    cedges = coarse_send.shape[0]
    node_out = pl.pallas_call(
        coarse_kernel,
        in_specs=[sm] + [vm] * (7 + len(tables)),
        out_specs=hb,
        out_shape=jax.ShapeDtypeStruct((nodes, lat), BF),
        scratch_shapes=[pltpu.VMEM((nodes, lat), BF), pltpu.SemaphoreType.DMA((tiles,))],
        compiler_params=pltpu.CompilerParams(vmem_limit_bytes=48 * 2**20),
        name="coarse",
    )(
        dev, coarse_send.reshape(cedges // TILE, TILE), coarse_recv.reshape(cedges // TILE, TILE),
        cmap2, fine, coarse_w1, coarse_w2, coarse_gain.reshape(1, lat), *tables,
    )
    return (node_out, edge_out)


def solution(mesh):
    split = P(("groups", "dom", "sub"))
    wide = P(("groups", "dom", "sub"), None)
    return jax.shard_map(
        on_device,
        mesh=mesh,
        in_specs=(wide, wide) + (split,) * 5 + (P(),) * 11,
        out_specs=(wide, wide),
        check_vma=False,
    )
```

```python
import functools

import jax
import jax.numpy as jnp
from jax import lax
from jax.experimental import pallas as pl
from jax.experimental.pallas import tpu as pltpu
from jax.sharding import PartitionSpec as P

TILE = 128
HALO = 256
COARSEN = 8
STEP = 2
PARTS = 2
PAD = 16
BF = jnp.bfloat16
F32 = jnp.float32
I16 = jnp.int16


def dot(a, b):
    return jnp.dot(a, b, preferred_element_type=F32)


def one_hot(mask):
    return jnp.where(mask, jnp.ones((), BF), jnp.zeros((), BF))


def pick(off, lane, blocks):
    return [one_hot(off == lane + I16(c * TILE)) for c in range(blocks)]


def column(rows_t, col):
    return jnp.broadcast_to(rows_t[:, col : col + 1], (TILE, TILE))


def along_lanes(row, count):
    return jnp.broadcast_to(row, (count, TILE)).astype(I16)


def twice(w):
    z = jnp.zeros_like(w)
    return jnp.concatenate(
        [jnp.concatenate([w, z], axis=1), jnp.concatenate([z, w], axis=1)], axis=0
    )


def pair_dot(x, w2):
    half = x.shape[0] // 2
    out = dot(jnp.concatenate([x[:half], x[half:]], axis=1), w2)
    n = out.shape[1] // 2
    return jnp.concatenate([out[:, :n], out[:, n:]], axis=0)


def gained(w, gain):
    w = w.astype(F32)
    return twice(((w - jnp.mean(w, axis=1, keepdims=True)) * gain).astype(BF))


def mean_weight(gain):
    lat = gain.shape[1]
    return twice(jnp.broadcast_to(1.0 / (gain * gain * lat), (lat, lat)).T.astype(BF))


def norm(hidden, w, m):
    c = pair_dot(hidden, w)
    return c * lax.rsqrt(pair_dot((c * c).astype(BF), m) + 1e-05)


def half_silu(y):
    return (y * jnp.tanh(y) + y).astype(BF)


def interleave(queue, active):
    queue = list(queue)
    while active or queue:
        if queue:
            active = list(queue.pop(0)) + active
        alive = []
        for part in active:
            try:
                next(part)
                alive.append(part)
            except StopIteration:
                pass
        active = alive


def fine_kernel(base_ref, edge_ref, last_ref, before_ref, after_ref, *refs):
    hbm, refs = refs[:12], refs[12:]
    (edge_out_ref, fine_ref, coarse_ref), refs = refs[:3], refs[3:]
    vmem, refs = refs[:12], refs[12:]
    own_ref, send_ref, recv_ref, cmap_ref, w1_ref, u_ref, v_ref = vmem[:7]
    edge_w2_ref, nw1_ref, node_w2_ref, gain_ref, ngain_ref = vmem[7:]
    sent_s, recv_s, we_s, w2_s, m_s, nw1_s, nw2_s, nm_s, code_s, loc_s, hid_s, inc_s, pool_s, sem = refs
    step = pl.program_id(0)
    steps = pl.num_programs(0) - 2
    rows, lat = own_ref.shape
    per = edge_ref.shape[0] // STEP
    groups = per // TILE
    idx_rows = STEP * groups
    crows = coarse_ref.shape[0]
    low_blocks = 3
    high_blocks = (TILE + 2 * HALO) // TILE - low_blocks

    @pl.when(step == 0)
    def _():
        copies = [pltpu.make_async_copy(a, b, sem.at[i]) for i, (a, b) in enumerate(zip(hbm, vmem))]
        for c in copies:
            c.start()
        for c in copies:
            c.wait()
        w_eff = w1_ref[...].astype(F32) + lax.dot_general(
            u_ref[...], v_ref[...], (((0,), (0,)), ((), ())), preferred_element_type=F32
        )
        w_eff = (0.5 * w_eff).astype(BF)
        we_s[...] = twice(w_eff[:lat])
        ws = w_eff[lat : 2 * lat]
        both = dot(own_ref[...], jnp.concatenate([ws, w_eff[2 * lat :]], axis=1)).astype(BF)
        sent_s[0:HALO] = dot(before_ref[...], ws).astype(BF)
        sent_s[HALO : HALO + rows] = both[:, :lat]
        sent_s[HALO + rows :] = dot(after_ref[...], ws).astype(BF)
        recv_s[...] = both[:, lat:]
        w2_s[...] = gained(edge_w2_ref[...], gain_ref[...])
        m_s[...] = mean_weight(gain_ref[...])
        nw2_s[...] = gained(node_w2_ref[...], ngain_ref[...])
        nm_s[...] = mean_weight(ngain_ref[...])
        nw1_s[...] = nw1_ref[...] * 0.5
        pool_s[...] = jnp.zeros_like(pool_s)
        recv = recv_ref[...]
        loc = recv & (TILE - 1)
        off = send_ref[...] - (recv - loc) + HALO
        hi = off >= low_blocks * TILE
        lo = jnp.where(hi, off - low_blocks * TILE, off)
        code = lo | (loc << 16) | jnp.where(hi, jnp.int32(-(2**31)), 0)
        for s in range(rows // TILE // STEP):
            sl = slice(s * idx_rows, (s + 1) * idx_rows)
            code_s[s, :, 0:idx_rows] = code[sl].T
            loc_s[s, 0:idx_rows] = loc[sl]

    this, prev, past = step, step - 1, step - 2
    part = per // PARTS
    lane = lax.broadcasted_iota(I16, (TILE, TILE), 1)
    sub = lax.broadcasted_iota(I16, (TILE, TILE), 0)
    csub = lax.broadcasted_iota(I16, (crows, TILE), 0)
    incoming = [[] for _ in range(STEP)]

    def weights(k):
        start = pl.multiple_of((this * STEP + k) * TILE, TILE)
        mine = recv_s[pl.ds(start, TILE)]
        low = jnp.concatenate([sent_s[pl.ds(start, low_blocks * TILE)], mine], axis=0)
        high = jnp.concatenate(
            [
                sent_s[pl.ds(start + low_blocks * TILE, high_blocks * TILE)],
                sent_s[pl.ds(start, (low_blocks - high_blocks) * TILE)],
                mine,
            ],
            axis=0,
        )
        return jnp.concatenate([low, high], axis=1)

    def first(k, q):
        at = slice(k * per + q * part, k * per + (q + 1) * part)
        code_t = code_s[this]
        lhs, upper = [], []
        for j in range(part // TILE):
            word = column(code_t, at.start // TILE + j)
            o = word.astype(I16) & I16(511)
            r = (word >> 16).astype(I16) & I16(TILE - 1)
            lhs.append(jnp.concatenate(pick(o, lane, low_blocks) + pick(r, lane, 1), axis=1))
            upper.append(word < 0)
        out = dot(jnp.concatenate(lhs, axis=0), weights(k))
        y = pair_dot(edge_ref[at], we_s[...])
        yield
        y = y + jnp.where(jnp.concatenate(upper, axis=0), out[:, lat:], out[:, :lat])
        hid_s[at] = half_silu(y)

    def second(k, q):
        at = slice(k * per + q * part, k * per + (q + 1) * part)
        c = pair_dot(hid_s[at], w2_s[...])
        yield
        var = pair_dot((c * c).astype(BF), m_s[...])
        yield
        new = (last_ref[at].astype(F32) + c * lax.rsqrt(var + 1e-05)).astype(BF)
        edge_out_ref[at] = new
        loc = loc_s[prev]
        back = [
            one_hot(along_lanes(loc[j : j + 1], TILE) == sub)
            for j in range(at.start // TILE, at.stop // TILE)
        ]
        incoming[k].append(dot(jnp.concatenate(back, axis=1), new))
        yield
        if q == PARTS - 1:
            inc_s[k * TILE : (k + 1) * TILE] = sum(incoming[k][1:], incoming[k][0]).astype(BF)

    def third():
        here = pl.ds(pl.multiple_of(past * STEP * TILE, STEP * TILE), STEP * TILE)
        own = own_ref[here]
        y = dot(jnp.concatenate([own, inc_s[...]], axis=1), nw1_s[...])
        yield
        c = pair_dot(half_silu(y), nw2_s[...])
        yield
        var = pair_dot((c * c).astype(BF), nm_s[...])
        yield
        fine = (own.astype(F32) + c * lax.rsqrt(var + 1e-05)).astype(BF)
        fine_ref[here] = fine
        member = []
        for k in range(STEP):
            local = cmap_ref[pl.ds(past * STEP + k, 1), :] - base_ref[0] * crows
            member.append(one_hot(along_lanes(local, crows) == csub))
        fine = jnp.concatenate([fine, jnp.ones_like(fine)], axis=1)
        pool_s[...] += dot(jnp.concatenate(member, axis=1), fine)

    def stages(one, two, three):
        for k in range(STEP):
            incoming[k].clear()
        todo = [(k, q) for k in range(STEP) for q in range(PARTS)] if one or two else []
        interleave(
            [[second(k, q)] * two + [first(k, q)] * one for k, q in todo],
            [third()] if three else [],
        )

    full = (step >= 2) & (step < steps)
    for when, which in (
        (full, (True, True, True)),
        (step == 0, (True, False, False)),
        (step == 1, (True, True, False)),
        (step == steps, (False, True, True)),
        (step == steps + 1, (False, False, True)),
    ):
        pl.when(when)(functools.partial(stages, *which))

    @pl.when(step == steps + 1)
    def _():
        total = pool_s[...]
        coarse_ref[...] = (total[:, :lat] / jnp.maximum(total[:, lat:], 1.0)).astype(BF)


def near_kernel(base_ref, send_ref, recv_ref, own_ref, w1_ref, pre_ref):
    crows, lat = own_ref.shape
    rows = send_ref.shape[0]
    first = base_ref[0] * crows
    blocks = crows // TILE
    send = send_ref[...] - first
    mine = (send >= 0) & (send < crows)
    code_t = (jnp.where(mine, send, crows) | ((recv_ref[...] - first) << 16)).T
    w1 = w1_ref[...] * 0.5
    rhs = dot(own_ref[...], jnp.concatenate([w1[:lat], w1[lat:]], axis=1)).astype(BF)
    rhs = jnp.concatenate([rhs[:, :lat], rhs[:, lat:]], axis=0)
    lane = lax.broadcasted_iota(I16, (TILE, TILE), 1)
    group = 3 if rows % 3 == 0 else 1

    def part(g):
        lhs = []
        for col in range(g, g + group):
            word = column(code_t, col)
            o, r = word.astype(I16), (word >> 16).astype(I16)
            lhs.append(jnp.concatenate(pick(o, lane, blocks) + pick(r, lane, blocks), axis=1))
        out = dot(jnp.concatenate(lhs, axis=0), rhs)
        yield
        pre_ref[g * TILE : (g + group) * TILE] = out

    interleave([[part(g)] for g in range(0, rows, group)], [])


def coarse_kernel(
    base_ref, send_ref, recv_ref, cmap_ref, fine_ref, pre_ref, w1_ref, w2_ref, gain_ref, *refs
):
    (own_ref, *tables), (out_ref, out_s, sem) = refs[:-3], refs[-3:]
    dev = base_ref[0]
    crows, lat = own_ref.shape
    rows = send_ref.shape[0]
    nodes = fine_ref.shape[0]
    chunks = crows // TILE
    blocks = chunks * len(tables)
    lows = (blocks + 1) // 2
    send = send_ref[...]
    owner = lax.div(send, jnp.full_like(send, crows))
    other = owner ^ dev
    slot = jnp.full_like(send, -1)
    for j in range(len(tables)):
        slot = jnp.where(other == (1 << j), j, slot)
    off = send - owner * crows + slot * crows
    hi = off >= lows * TILE
    lo = jnp.where(hi, off - lows * TILE, off)
    code_t = jnp.where(
        slot < 0, lows * TILE, lo | jnp.where(hi, jnp.int32(-(2**31)), 0)
    ).T
    loc = recv_ref[...] - dev * crows
    w1 = twice(w1_ref[:lat] * 0.5)
    proj = jnp.concatenate([pair_dot(t[...], w1).astype(BF) for t in tables], axis=0)
    low, high = proj[: lows * TILE], proj[lows * TILE :]
    if high.shape[0] < low.shape[0]:
        high = jnp.concatenate([high, low[high.shape[0] :]], axis=0)
    rhs = jnp.concatenate([low, high], axis=1)
    lane = lax.broadcasted_iota(I16, (TILE, TILE), 1)
    csub = lax.broadcasted_iota(I16, (crows, TILE), 0)
    w2 = twice(w2_ref[...])
    group = 2 if rows % 2 == 0 else 1
    total = [own_ref[...].astype(F32)]

    def part(g):
        lhs, upper = [], []
        for col in range(g, g + group):
            word = column(code_t, col)
            lhs.append(jnp.concatenate(pick(word.astype(I16), lane, lows), axis=1))
            upper.append(word < 0)
        out = dot(jnp.concatenate(lhs, axis=0), rhs)
        yield
        y = jnp.where(jnp.concatenate(upper, axis=0), out[:, lat:], out[:, :lat])
        y = half_silu(y + pre_ref[g * TILE : (g + group) * TILE])
        msg = pair_dot(y, w2)
        yield
        back = [one_hot(along_lanes(loc[col : col + 1], crows) == csub) for col in range(g, g + group)]
        total[0] = total[0] + dot(jnp.concatenate(back, axis=1), msg.astype(BF))

    interleave([[part(g)] for g in range(0, rows, group)], [])
    total = total[0]
    centred = total - jnp.mean(total, axis=1, keepdims=True)
    var = jnp.mean(centred * centred, axis=1, keepdims=True)
    delta = (centred * lax.rsqrt(var + 1e-05) * gain_ref[...]).astype(BF)
    half = (chunks + 1) // 2
    high = delta[half * TILE :]
    if high.shape[0] < half * TILE:
        high = jnp.concatenate([high, delta[high.shape[0] : half * TILE]], axis=0)
    rhs = jnp.concatenate([delta[: half * TILE], high], axis=1)
    cm = cmap_ref[...] - dev * crows
    hi = cm >= half * TILE
    cm_t = (jnp.where(hi, cm - half * TILE, cm) | jnp.where(hi, jnp.int32(-(2**31)), 0)).T
    tiles = nodes // TILE
    size = 4 if tiles % 4 == 0 else 1
    copies = []

    def spread(p):
        hot, upper = [], []
        for t in range(p, p + size):
            word = column(cm_t, t)
            hot.append(jnp.concatenate(pick(word.astype(I16), lane, half), axis=1))
            upper.append(word < 0)
        out = dot(jnp.concatenate(hot, axis=0), rhs)
        yield
        back = jnp.where(jnp.concatenate(upper, axis=0), out[:, lat:], out[:, :lat])
        sl = pl.ds(p * TILE, size * TILE)
        out_s[sl] = (fine_ref[sl].astype(F32) + back).astype(BF)
        copies.append(pltpu.make_async_copy(out_s.at[sl], out_ref.at[sl], sem.at[p]))
        copies[-1].start()

    interleave([[spread(p)] for p in range(0, tiles, size)], [])
    for c in copies:
        c.wait()


def on_device(
    node_latent, edge_latent, receivers, senders, coarse_map, coarse_recv, coarse_send,
    edge_w1, mod_u, mod_v, edge_w2, edge_gain, node_w1, node_w2, node_gain,
    coarse_w1, coarse_w2, coarse_gain,
):
    axes = ("dom", "sub")
    size = lax.axis_size(axes)
    dev = lax.axis_index(axes).astype(jnp.int32).reshape(1)
    nodes, lat = node_latent.shape
    edges = edge_latent.shape[0]
    tiles = nodes // TILE
    per = edges // tiles
    crows = nodes // COARSEN
    steps = tiles // STEP
    up = [(i, i + 1) for i in range(size - 1)]
    down = [(j, i) for i, j in up]
    before = lax.ppermute(node_latent[nodes - HALO :], axes, up)
    after = lax.ppermute(node_latent[:HALO], axes, down)
    cmap2 = coarse_map.reshape(tiles, TILE)
    vm = pl.BlockSpec(memory_space=pltpu.VMEM)
    sm = pl.BlockSpec(memory_space=pltpu.SMEM)
    hb = pl.BlockSpec(memory_space=pltpu.HBM)
    hbm = (
        node_latent, senders.reshape(edges // TILE, TILE), receivers.reshape(edges // TILE, TILE),
        cmap2, edge_w1, mod_u.T, mod_v, edge_w2, node_w1, node_w2,
        edge_gain.reshape(1, lat), node_gain.reshape(1, lat),
    )
    big = (STEP * per, lat)
    index = pltpu.VMEM((steps, PAD, TILE), jnp.int32)
    square = pltpu.VMEM((2 * lat, 2 * lat), BF)
    far = pltpu.with_memory_space_constraint(edge_latent, pltpu.HBM)
    edge_out, fine, coarse = pl.pallas_call(
        fine_kernel,
        grid=(steps + 2,),
        in_specs=[
            sm,
            pl.BlockSpec(big, lambda i: (jnp.minimum(i, steps - 1), 0)),
            pl.BlockSpec(big, lambda i: (jnp.clip(i - 1, 0, steps - 1), 0)),
            vm, vm,
        ] + [hb] * len(hbm),
        out_specs=[pl.BlockSpec(big, lambda i: (jnp.clip(i - 1, 0, steps - 1), 0)), vm, vm],
        out_shape=[
            jax.ShapeDtypeStruct((edges, lat), BF),
            jax.ShapeDtypeStruct((nodes, lat), BF),
            jax.ShapeDtypeStruct((crows, lat), BF),
        ],
        scratch_shapes=[pltpu.VMEM(a.shape, a.dtype) for a in hbm] + [
            pltpu.VMEM((nodes + 2 * HALO, lat), BF),
            pltpu.VMEM((nodes, lat), BF),
            square, square, square,
            pltpu.VMEM((2 * lat, lat), BF),
            square, square,
            pltpu.VMEM((steps, TILE, PAD), jnp.int32),
            index,
            pltpu.VMEM(big, BF),
            pltpu.VMEM((STEP * TILE, lat), BF),
            pltpu.VMEM((crows, 2 * lat), F32),
            pltpu.SemaphoreType.DMA((len(hbm),)),
        ],
        compiler_params=pltpu.CompilerParams(
            dimension_semantics=("arbitrary",), vmem_limit_bytes=48 * 2**20
        ),
        name="fine",
    )(dev, far, far, before, after, *[pltpu.with_memory_space_constraint(a, pltpu.HBM) for a in hbm])
    tables = [coarse]
    bit = 1
    while bit < size:
        tables.append(lax.ppermute(coarse, axes, [(i, i ^ bit) for i in range(size)]))
        bit *= 2
    cedges = coarse_send.shape[0]
    csend2 = coarse_send.reshape(cedges // TILE, TILE)
    crecv2 = coarse_recv.reshape(cedges // TILE, TILE)
    pre = pl.pallas_call(
        near_kernel,
        in_specs=[sm] + [vm] * 4,
        out_specs=vm,
        out_shape=jax.ShapeDtypeStruct((cedges, lat), F32),
        compiler_params=pltpu.CompilerParams(vmem_limit_bytes=32 * 2**20),
        name="near",
    )(dev, csend2, crecv2, coarse, coarse_w1)
    node_out = pl.pallas_call(
        coarse_kernel,
        in_specs=[sm] + [vm] * (8 + len(tables)),
        out_specs=hb,
        out_shape=jax.ShapeDtypeStruct((nodes, lat), BF),
        scratch_shapes=[pltpu.VMEM((nodes, lat), BF), pltpu.SemaphoreType.DMA((tiles,))],
        compiler_params=pltpu.CompilerParams(vmem_limit_bytes=32 * 2**20),
        name="coarse",
    )(
        dev, csend2, crecv2, cmap2, fine, pre, coarse_w1, coarse_w2, coarse_gain.reshape(1, lat),
        *tables,
    )
    return (node_out, edge_out)


def solution(mesh):
    split = P(("groups", "dom", "sub"))
    wide = P(("groups", "dom", "sub"), None)
    return jax.shard_map(
        on_device,
        mesh=mesh,
        in_specs=(wide, wide) + (split,) * 5 + (P(),) * 11,
        out_specs=(wide, wide),
        check_vma=False,
    )
```

```python
import functools

import jax
import jax.numpy as jnp
from jax import lax
from jax.experimental import pallas as pl
from jax.experimental.pallas import tpu as pltpu
from jax.sharding import PartitionSpec as P

TILE = 128
HALO = 256
COARSEN = 8
STEP = 2
PARTS = 2
LOW = 3
HIGH = (TILE + 2 * HALO) // TILE - LOW
PAD = 16
BF = jnp.bfloat16
F32 = jnp.float32
I16 = jnp.int16


def dot(a, b):
    return jnp.dot(a, b, preferred_element_type=F32)


def one_hot(mask):
    return jnp.where(mask, jnp.ones((), BF), jnp.zeros((), BF))


def pick(off, lane, blocks):
    return [one_hot(off == lane + I16(c * TILE)) for c in range(blocks)]


def aligned(row):
    return row if isinstance(row, int) else pl.multiple_of(row, TILE)


def column(rows_t, col):
    return jnp.broadcast_to(rows_t[:, col : col + 1], (TILE, TILE))


def along_lanes(row, count):
    return jnp.broadcast_to(row, (count, TILE)).astype(I16)


def twice(w):
    z = jnp.zeros_like(w)
    return jnp.concatenate(
        [jnp.concatenate([w, z], axis=1), jnp.concatenate([z, w], axis=1)], axis=0
    )


def pair_dot(x, w2):
    half = x.shape[0] // 2
    out = dot(jnp.concatenate([x[:half], x[half:]], axis=1), w2)
    n = out.shape[1] // 2
    return jnp.concatenate([out[:, :n], out[:, n:]], axis=0)


def gained(w, gain):
    w = w.astype(F32)
    return twice(((w - jnp.mean(w, axis=1, keepdims=True)) * gain).astype(BF))


def mean_weight(gain):
    return 1.0 / (gain * gain * gain.shape[1])


def mean_square(gain):
    lat = gain.shape[1]
    return twice(jnp.broadcast_to(mean_weight(gain), (lat, lat)).T.astype(BF))


def scaled(c, weight):
    return c * lax.rsqrt(jnp.sum(c * c * weight, axis=1, keepdims=True) + 1e-05)


def half_silu(y):
    return (y * jnp.tanh(y) + y).astype(BF)


def interleave(queue, active):
    queue = list(queue)
    while active or queue:
        if queue:
            active = list(queue.pop(0)) + active
        alive = []
        for part in active:
            try:
                next(part)
                alive.append(part)
            except StopIteration:
                pass
        active = alive


def make_stages(block, window, base, refs, base_ref):
    edge_ref, last_ref, edge_out_ref, own_ref, cmap_ref, fine_ref = refs[:6]
    sent_s, recv_s, we_s, w2_s, m_s, nw1_s, nw2_s, nm_s, code_s, loc_s = refs[6:16]
    hid_s, inc_s, pool_s, per = refs[16:]
    lat = sent_s.shape[1]
    crows = pool_s.shape[0]
    groups = per // TILE
    part = per // PARTS
    lane = lax.broadcasted_iota(I16, (TILE, TILE), 1)
    sub = lax.broadcasted_iota(I16, (TILE, TILE), 0)
    csub = lax.broadcasted_iota(I16, (crows, TILE), 0)
    incoming = {}

    def rows_of(s, k, q):
        start = (base(s) + k) * per + q * part
        return slice(start, start + part), (k * per + q * part) // TILE

    def weights(s, k):
        start = aligned(window(s) + k * TILE)
        at = aligned((block(s) * STEP + k) * TILE)
        mine = recv_s[pl.ds(at, TILE)]
        low = jnp.concatenate([sent_s[pl.ds(start, LOW * TILE)], mine], axis=0)
        high = jnp.concatenate(
            [
                sent_s[pl.ds(start + LOW * TILE, HIGH * TILE)],
                sent_s[pl.ds(start, (LOW - HIGH) * TILE)],
                mine,
            ],
            axis=0,
        )
        return jnp.concatenate([low, high], axis=1)

    def first(s, k, q):
        at, col0 = rows_of(s, k, q)
        code_t = code_s[block(s)]
        lhs, upper = [], []
        for j in range(part // TILE):
            word = column(code_t, col0 + j)
            o = word.astype(I16) & I16(511)
            r = (word >> 16).astype(I16) & I16(TILE - 1)
            lhs.append(jnp.concatenate(pick(o, lane, LOW) + pick(r, lane, 1), axis=1))
            upper.append(word < 0)
        y = pair_dot(edge_ref[at], we_s[...])
        out = dot(jnp.concatenate(lhs, axis=0), weights(s, k))
        yield
        y = y + jnp.where(jnp.concatenate(upper, axis=0), out[:, lat:], out[:, :lat])
        hid_s[at] = half_silu(y)

    def second(s, k, q):
        at, col0 = rows_of(s, k, q)
        c = pair_dot(hid_s[at], w2_s[...])
        yield
        new = (last_ref[at].astype(F32) + scaled(c, m_s[...])).astype(BF)
        edge_out_ref[at] = new
        loc = loc_s[block(s)]
        back = [
            one_hot(along_lanes(loc[j : j + 1], TILE) == sub)
            for j in range(col0, col0 + part // TILE)
        ]
        incoming.setdefault(k + base(s), []).append((back, new))
        yield
        if q == PARTS - 1:
            backs, news = zip(*incoming.pop(k + base(s)))
            row = (base(s) + k) * TILE
            inc_s[row : row + TILE] = dot(
                jnp.concatenate(sum(backs, []), axis=1), jnp.concatenate(news, axis=0)
            ).astype(BF)

    def third(s):
        here = pl.ds(aligned(block(s) * STEP * TILE), STEP * TILE)
        own = own_ref[here]
        got = inc_s[base(s) * TILE : (base(s) + STEP) * TILE]
        y = dot(jnp.concatenate([own, got], axis=1), nw1_s[...])
        yield
        c = pair_dot(half_silu(y), nw2_s[...])
        yield
        var = pair_dot((c * c).astype(BF), nm_s[...])
        yield
        fine = (own.astype(F32) + c * lax.rsqrt(var + 1e-05)).astype(BF)
        fine_ref[here] = fine
        member = []
        for k in range(STEP):
            local = cmap_ref[pl.ds(block(s) * STEP + k, 1), :] - base_ref[0] * crows
            member.append(one_hot(along_lanes(local, crows) == csub))
        fine = jnp.concatenate([fine, jnp.ones_like(fine)], axis=1)
        pool_s[...] += dot(jnp.concatenate(member, axis=1), fine)

    return first, second, third


def run_stages(step, count, stages):
    first, second, third = stages
    parts = [(k, q) for k in range(STEP) for q in range(PARTS)]

    def run(one, two, three):
        interleave(
            [
                [second(step - 1, k, q)] * two + [first(step, k, q)] * one
                for k, q in (parts if one or two else [])
            ],
            [third(step - 2)] if three else [],
        )

    for when, which in (
        ((step >= 2) & (step < count), (True, True, True)),
        (step == 0, (True, False, False)),
        (step == 1, (True, True, False)),
        (step == count, (False, True, True)),
        (step == count + 1, (False, False, True)),
    ):
        pl.when(when)(functools.partial(run, *which))


def inner_kernel(count, base_ref, edge_ref, last_ref, all_ref, *refs):
    hbm, refs = refs[:12], refs[12:]
    edge_out_ref, fine_ref, pool_ref, ws_ref, ends_ref, own_ref, cmap_ref = refs[:7]
    ready, refs = refs[7:17], refs[17:]
    vmem, (hid_s, inc_s, sem) = refs[:10], refs[10:]
    send_ref, recv_ref, w1_ref, u_ref, v_ref = vmem[:5]
    edge_w2_ref, node_w1_ref, node_w2_ref, gain_ref, ngain_ref = vmem[5:]
    vmem = (own_ref, cmap_ref) + vmem
    sent_s, recv_s, we_s, w2_s, m_s, nw1_s, nw2_s, nm_s, code_s, loc_s = ready
    step = pl.program_id(0)
    rows, lat = own_ref.shape
    size = edge_ref.shape[0]
    idx_rows = size // TILE
    ends = [
        pltpu.make_async_copy(
            all_ref.at[pl.ds(at * size, size)], ends_ref.at[pl.ds(n * size, size)],
            sem.at[len(hbm) + n],
        )
        for n, at in enumerate((0, count + 1))
    ]

    @pl.when(step == 0)
    def _():
        copies = [pltpu.make_async_copy(a, b, sem.at[i]) for i, (a, b) in enumerate(zip(hbm, vmem))]
        for c in copies + ends:
            c.start()
        for c in copies:
            c.wait()
        w_eff = w1_ref[...].astype(F32) + lax.dot_general(
            u_ref[...], v_ref[...], (((0,), (0,)), ((), ())), preferred_element_type=F32
        )
        w_eff = (0.5 * w_eff).astype(BF)
        we_s[...] = twice(w_eff[:lat])
        ws = w_eff[lat : 2 * lat]
        ws_ref[...] = ws
        both = dot(own_ref[...], jnp.concatenate([ws, w_eff[2 * lat :]], axis=1)).astype(BF)
        sent_s[...] = both[:, :lat]
        recv_s[...] = both[:, lat:]
        w2_s[...] = gained(edge_w2_ref[...], gain_ref[...])
        m_s[...] = mean_weight(gain_ref[...])
        nw1_s[...] = node_w1_ref[...] * 0.5
        nw2_s[...] = gained(node_w2_ref[...], ngain_ref[...])
        nm_s[...] = mean_square(ngain_ref[...])
        pool_ref[...] = jnp.zeros_like(pool_ref)
        recv = recv_ref[...]
        loc = recv & (TILE - 1)
        off = send_ref[...] - (recv - loc) + HALO
        hi = off >= LOW * TILE
        lo = jnp.where(hi, off - LOW * TILE, off)
        code = lo | (loc << 16) | jnp.where(hi, jnp.int32(-(2**31)), 0)
        for s in range(rows // TILE // STEP):
            sl = slice(s * idx_rows, (s + 1) * idx_rows)
            code_s[s, :, 0:idx_rows] = code[sl].T
            loc_s[s, 0:idx_rows] = loc[sl]

    run_stages(
        step, count,
        make_stages(
            lambda s: s + 1, lambda s: (s + 1) * STEP * TILE - HALO, lambda s: 0,
            (edge_ref, last_ref, edge_out_ref, own_ref, cmap_ref, fine_ref) + ready
            + (hid_s, inc_s, pool_ref, size // STEP),
            base_ref,
        ),
    )

    @pl.when(step == count + 1)
    def _():
        for c in ends:
            c.wait()


def border_kernel(
    last_block, base_ref, ends_ref, own_ref, across_ref, within_ref, cmap_ref, pool_ref,
    ws_ref, *refs
):
    ready, refs = refs[:10], refs[12:]
    edge_out_ref, fine_ref, coarse_ref, win_s, out_s, hid_s, inc_s, pool_s, sem = refs
    sent_ref = ready[0]
    rows, lat = sent_ref.shape
    size = ends_ref.shape[0] // 2
    span = STEP * TILE + 2 * HALO
    inside = span - HALO
    even = base_ref[0] % 2 == 0
    across, within = across_ref[...], within_ref[...]
    ws = ws_ref[...]
    win_s[:HALO] = dot(jnp.where(even, across, within), ws).astype(BF)
    win_s[HALO:span] = sent_ref[:inside]
    win_s[span : span + inside] = sent_ref[rows - inside :]
    win_s[span + inside :] = dot(jnp.where(even, within, across), ws).astype(BF)
    pool_s[...] = pool_ref[...]
    first, second, third = make_stages(
        lambda s: s * last_block, lambda s: s * span, lambda s: s * STEP,
        (ends_ref, ends_ref, out_s, own_ref, cmap_ref, fine_ref, win_s) + ready[1:]
        + (hid_s, inc_s, pool_s, size // STEP),
        base_ref,
    )
    copies = []

    def send(s):
        copies.append(
            pltpu.make_async_copy(
                out_s.at[pl.ds(s * size, size)],
                edge_out_ref.at[pl.ds(s * last_block * size, size)],
                sem.at[s],
            )
        )
        copies[-1].start()
        yield

    parts = [(s, k, q) for s in range(2) for k in range(STEP) for q in range(PARTS)]
    half = STEP * PARTS
    ticks = [[] for _ in range(2 * half + 8)]
    for n, p in enumerate(parts):
        ticks[n].append(first(*p))
        ticks[n + 2].insert(0, second(*p))
    for s in range(2):
        done = (s + 1) * half + 1 + 3
        ticks[done] += [send(s), third(s)]
    interleave(ticks, [])
    total = pool_s[...]
    coarse_ref[...] = (total[:, :lat] / jnp.maximum(total[:, lat:], 1.0)).astype(BF)
    for c in copies:
        c.wait()


def near_kernel(base_ref, send_ref, recv_ref, own_ref, w1_ref, pre_ref):
    crows, lat = own_ref.shape
    rows = send_ref.shape[0]
    first = base_ref[0] * crows
    blocks = crows // TILE
    send = send_ref[...] - first
    mine = (send >= 0) & (send < crows)
    code_t = (jnp.where(mine, send, crows) | ((recv_ref[...] - first) << 16)).T
    w1 = w1_ref[...] * 0.5
    rhs = dot(own_ref[...], jnp.concatenate([w1[:lat], w1[lat:]], axis=1)).astype(BF)
    rhs = jnp.concatenate([rhs[:, :lat], rhs[:, lat:]], axis=0)
    lane = lax.broadcasted_iota(I16, (TILE, TILE), 1)
    group = 3 if rows % 3 == 0 else 1

    def part(g):
        lhs = []
        for col in range(g, g + group):
            word = column(code_t, col)
            o, r = word.astype(I16), (word >> 16).astype(I16)
            lhs.append(jnp.concatenate(pick(o, lane, blocks) + pick(r, lane, blocks), axis=1))
        out = dot(jnp.concatenate(lhs, axis=0), rhs)
        yield
        pre_ref[g * TILE : (g + group) * TILE] = out

    interleave([[part(g)] for g in range(0, rows, group)], [])


def coarse_kernel(
    base_ref, send_ref, recv_ref, cmap_ref, fine_ref, pre_ref, w1_ref, w2_ref, gain_ref, *refs
):
    (own_ref, *tables), (out_ref, out_s, sem) = refs[:-3], refs[-3:]
    dev = base_ref[0]
    crows, lat = own_ref.shape
    rows = send_ref.shape[0]
    nodes = fine_ref.shape[0]
    chunks = crows // TILE
    blocks = chunks * len(tables)
    lows = (blocks + 1) // 2
    send = send_ref[...]
    owner = lax.div(send, jnp.full_like(send, crows))
    other = owner ^ dev
    slot = jnp.full_like(send, -1)
    for j in range(len(tables)):
        slot = jnp.where(other == (1 << j), j, slot)
    off = send - owner * crows + slot * crows
    hi = off >= lows * TILE
    lo = jnp.where(hi, off - lows * TILE, off)
    code_t = jnp.where(
        slot < 0, lows * TILE, lo | jnp.where(hi, jnp.int32(-(2**31)), 0)
    ).T
    loc = recv_ref[...] - dev * crows
    w1 = twice(w1_ref[:lat] * 0.5)
    proj = jnp.concatenate([pair_dot(t[...], w1).astype(BF) for t in tables], axis=0)
    low, high = proj[: lows * TILE], proj[lows * TILE :]
    if high.shape[0] < low.shape[0]:
        high = jnp.concatenate([high, low[high.shape[0] :]], axis=0)
    rhs = jnp.concatenate([low, high], axis=1)
    lane = lax.broadcasted_iota(I16, (TILE, TILE), 1)
    csub = lax.broadcasted_iota(I16, (crows, TILE), 0)
    w2 = twice(w2_ref[...])
    group = 2 if rows % 2 == 0 else 1
    total = [own_ref[...].astype(F32)]

    def part(g):
        lhs, upper = [], []
        for col in range(g, g + group):
            word = column(code_t, col)
            lhs.append(jnp.concatenate(pick(word.astype(I16), lane, lows), axis=1))
            upper.append(word < 0)
        out = dot(jnp.concatenate(lhs, axis=0), rhs)
        yield
        y = jnp.where(jnp.concatenate(upper, axis=0), out[:, lat:], out[:, :lat])
        y = half_silu(y + pre_ref[g * TILE : (g + group) * TILE])
        msg = pair_dot(y, w2)
        yield
        back = [one_hot(along_lanes(loc[col : col + 1], crows) == csub) for col in range(g, g + group)]
        total[0] = total[0] + dot(jnp.concatenate(back, axis=1), msg.astype(BF))

    interleave([[part(g)] for g in range(0, rows, group)], [])
    total = total[0]
    centred = total - jnp.mean(total, axis=1, keepdims=True)
    var = jnp.mean(centred * centred, axis=1, keepdims=True)
    delta = (centred * lax.rsqrt(var + 1e-05) * gain_ref[...]).astype(BF)
    half = (chunks + 1) // 2
    high = delta[half * TILE :]
    if high.shape[0] < half * TILE:
        high = jnp.concatenate([high, delta[high.shape[0] : half * TILE]], axis=0)
    rhs = jnp.concatenate([delta[: half * TILE], high], axis=1)
    cm = cmap_ref[...] - dev * crows
    hi = cm >= half * TILE
    cm_t = (jnp.where(hi, cm - half * TILE, cm) | jnp.where(hi, jnp.int32(-(2**31)), 0)).T
    tiles = nodes // TILE
    size = 4 if tiles % 4 == 0 else 1
    copies = []

    def spread(p):
        hot, upper = [], []
        for t in range(p, p + size):
            word = column(cm_t, t)
            hot.append(jnp.concatenate(pick(word.astype(I16), lane, half), axis=1))
            upper.append(word < 0)
        out = dot(jnp.concatenate(hot, axis=0), rhs)
        yield
        back = jnp.where(jnp.concatenate(upper, axis=0), out[:, lat:], out[:, :lat])
        sl = pl.ds(p * TILE, size * TILE)
        out_s[sl] = (fine_ref[sl].astype(F32) + back).astype(BF)
        copies.append(pltpu.make_async_copy(out_s.at[sl], out_ref.at[sl], sem.at[p]))
        copies[-1].start()

    interleave([[spread(p)] for p in range(0, tiles, size)], [])
    for c in copies:
        c.wait()


def on_device(
    node_latent, edge_latent, receivers, senders, coarse_map, coarse_recv, coarse_send,
    edge_w1, mod_u, mod_v, edge_w2, edge_gain, node_w1, node_w2, node_gain,
    coarse_w1, coarse_w2, coarse_gain,
):
    axes = ("dom", "sub")
    size = lax.axis_size(axes)
    dev = lax.axis_index(axes).astype(jnp.int32).reshape(1)
    nodes, lat = node_latent.shape
    edges = edge_latent.shape[0]
    tiles = nodes // TILE
    per = edges // tiles
    crows = nodes // COARSEN
    steps = tiles // STEP
    even = dev[0] % 2 == 0
    ends = (node_latent[:HALO], node_latent[nodes - HALO :])
    across = [(i, i + 1) for i in range(1, size - 1, 2)]
    within = [(i, i + 1) for i in range(0, size, 2)]
    across = lax.ppermute(
        jnp.where(even, ends[0], ends[1]), axes, across + [(j, i) for i, j in across]
    )
    within = lax.ppermute(
        jnp.where(even, ends[1], ends[0]), axes, within + [(j, i) for i, j in within]
    )
    cmap2 = coarse_map.reshape(tiles, TILE)
    vm = pl.BlockSpec(memory_space=pltpu.VMEM)
    sm = pl.BlockSpec(memory_space=pltpu.SMEM)
    hb = pl.BlockSpec(memory_space=pltpu.HBM)
    hbm = (
        node_latent, cmap2, senders.reshape(edges // TILE, TILE),
        receivers.reshape(edges // TILE, TILE), edge_w1, mod_u.T, mod_v, edge_w2, node_w1,
        node_w2, edge_gain.reshape(1, lat), node_gain.reshape(1, lat),
    )
    big = (STEP * per, lat)
    apart = lambda a: pltpu.with_memory_space_constraint(a, pltpu.HBM)
    far = apart(edge_latent)
    count = steps - 2
    full = jax.ShapeDtypeStruct((edges, lat), BF)
    inner_block = lambda i: (jnp.clip(i, 0, count - 1) + 1, 0)
    ready = [
        jax.ShapeDtypeStruct(shape, dtype)
        for shape, dtype in [((nodes, lat), BF)] * 2
        + [((2 * lat, 2 * lat), BF)] * 2
        + [((1, lat), F32), ((2 * lat, lat), BF), ((2 * lat, 2 * lat), BF), ((2 * lat, 2 * lat), BF)]
        + [((steps, TILE, PAD), jnp.int32), ((steps, PAD, TILE), jnp.int32)]
    ]
    edge_out, fine, pool, ws, ends, own, cmap2, *ready = pl.pallas_call(
        functools.partial(inner_kernel, count),
        grid=(count + 2,),
        in_specs=[
            sm,
            pl.BlockSpec(big, inner_block),
            pl.BlockSpec(big, lambda i: inner_block(i - 1)),
        ] + [hb] * (1 + len(hbm)),
        out_specs=[pl.BlockSpec(big, lambda i: inner_block(i - 1))] + [vm] * (6 + len(ready)),
        out_shape=[
            full,
            jax.ShapeDtypeStruct((nodes, lat), BF),
            jax.ShapeDtypeStruct((crows, 2 * lat), F32),
            jax.ShapeDtypeStruct((lat, lat), BF),
            jax.ShapeDtypeStruct((2 * STEP * per, lat), BF),
            jax.ShapeDtypeStruct((nodes, lat), BF),
            jax.ShapeDtypeStruct(cmap2.shape, cmap2.dtype),
        ] + ready,
        scratch_shapes=[pltpu.VMEM(a.shape, a.dtype) for a in hbm[2:]]
        + [pltpu.VMEM(big, BF), pltpu.VMEM((STEP * TILE, lat), BF)]
        + [pltpu.SemaphoreType.DMA((len(hbm) + 2,))],
        compiler_params=pltpu.CompilerParams(
            dimension_semantics=("arbitrary",), vmem_limit_bytes=24 * 2**20
        ),
        name="inner",
    )(dev, far, far, far, *[apart(a) for a in hbm])
    edge_out, fine, coarse = pl.pallas_call(
        functools.partial(border_kernel, steps - 1),
        in_specs=[sm] + [vm] * (7 + len(ready)) + [hb, vm],
        out_specs=[hb, vm, vm],
        out_shape=[
            full,
            jax.ShapeDtypeStruct((nodes, lat), BF),
            jax.ShapeDtypeStruct((crows, lat), BF),
        ],
        input_output_aliases={8 + len(ready): 0, 9 + len(ready): 1},
        scratch_shapes=[
            pltpu.VMEM((2 * (STEP * TILE + 2 * HALO), lat), BF),
            pltpu.VMEM((2 * STEP * per, lat), BF),
            pltpu.VMEM((2 * STEP * per, lat), BF),
            pltpu.VMEM((2 * STEP * TILE, lat), BF),
            pltpu.VMEM((crows, 2 * lat), F32),
            pltpu.SemaphoreType.DMA((2,)),
        ],
        compiler_params=pltpu.CompilerParams(vmem_limit_bytes=24 * 2**20),
        name="border",
    )(dev, ends, own, across, within, cmap2, pool, ws, *ready, edge_out, fine)
    tables = [coarse]
    bit = 1
    while bit < size:
        tables.append(lax.ppermute(coarse, axes, [(i, i ^ bit) for i in range(size)]))
        bit *= 2
    cedges = coarse_send.shape[0]
    csend2 = coarse_send.reshape(cedges // TILE, TILE)
    crecv2 = coarse_recv.reshape(cedges // TILE, TILE)
    pre = pl.pallas_call(
        near_kernel,
        in_specs=[sm] + [vm] * 4,
        out_specs=vm,
        out_shape=jax.ShapeDtypeStruct((cedges, lat), F32),
        compiler_params=pltpu.CompilerParams(vmem_limit_bytes=32 * 2**20),
        name="near",
    )(dev, csend2, crecv2, coarse, coarse_w1)
    node_out = pl.pallas_call(
        coarse_kernel,
        in_specs=[sm] + [vm] * (8 + len(tables)),
        out_specs=hb,
        out_shape=jax.ShapeDtypeStruct((nodes, lat), BF),
        scratch_shapes=[pltpu.VMEM((nodes, lat), BF), pltpu.SemaphoreType.DMA((tiles,))],
        compiler_params=pltpu.CompilerParams(vmem_limit_bytes=32 * 2**20),
        name="coarse",
    )(
        dev, csend2, crecv2, cmap2, fine, pre, coarse_w1, coarse_w2, coarse_gain.reshape(1, lat),
        *tables,
    )
    return (node_out, edge_out)


def solution(mesh):
    split = P(("groups", "dom", "sub"))
    wide = P(("groups", "dom", "sub"), None)
    return jax.shard_map(
        on_device,
        mesh=mesh,
        in_specs=(wide, wide) + (split,) * 5 + (P(),) * 11,
        out_specs=(wide, wide),
        check_vma=False,
    )
```

```python
import functools

import jax
import jax.numpy as jnp
from jax import lax
from jax.experimental import pallas as pl
from jax.experimental.pallas import tpu as pltpu
from jax.sharding import PartitionSpec as P

TILE = 128
HALO = 256
COARSEN = 8
STEP = 2
PARTS = 2
LOW = 3
HIGH = (TILE + 2 * HALO) // TILE - LOW
PAD = 16
BF = jnp.bfloat16
F32 = jnp.float32
I16 = jnp.int16


def dot(a, b):
    return jnp.dot(a, b, preferred_element_type=F32)


def one_hot(mask):
    return jnp.where(mask, jnp.ones((), BF), jnp.zeros((), BF))


def pick(off, lane, blocks):
    return [one_hot(off == lane + I16(c * TILE)) for c in range(blocks)]


def aligned(row):
    return row if isinstance(row, int) else pl.multiple_of(row, TILE)


def column(rows_t, col):
    return jnp.broadcast_to(rows_t[:, col : col + 1], (TILE, TILE))


def along_lanes(row, count):
    return jnp.broadcast_to(row, (count, TILE)).astype(I16)


def twice(w):
    z = jnp.zeros_like(w)
    return jnp.concatenate(
        [jnp.concatenate([w, z], axis=1), jnp.concatenate([z, w], axis=1)], axis=0
    )


def pair_dot(x, w2):
    half = x.shape[0] // 2
    out = dot(jnp.concatenate([x[:half], x[half:]], axis=1), w2)
    n = out.shape[1] // 2
    return jnp.concatenate([out[:, :n], out[:, n:]], axis=0)


def gained(w, gain):
    w = w.astype(F32)
    return twice(((w - jnp.mean(w, axis=1, keepdims=True)) * gain).astype(BF))


def mean_weight(gain):
    return 1.0 / (gain * gain * gain.shape[1])


def mean_square(gain):
    lat = gain.shape[1]
    return twice(jnp.broadcast_to(mean_weight(gain), (lat, lat)).T.astype(BF))


def scaled(c, weight):
    return c * lax.rsqrt(jnp.sum(c * c * weight, axis=1, keepdims=True) + 1e-05)


def half_silu(y):
    return (y * jnp.tanh(y) + y).astype(BF)


def interleave(queue, active):
    queue = list(queue)
    while active or queue:
        if queue:
            active = list(queue.pop(0)) + active
        alive = []
        for part in active:
            try:
                next(part)
                alive.append(part)
            except StopIteration:
                pass
        active = alive


def make_stages(block, window, base, held, refs, base_ref):
    edge_ref, own_ref, cmap_ref, fine_ref = refs[:4]
    sent_s, recv_s, we_s, w2_s, m_s, nw1_s, nw2_s, nm_s, code_s, loc_s = refs[4:14]
    hid_s, inc_s, pool_s, per = refs[14:]
    lat = sent_s.shape[1]
    crows = pool_s.shape[0]
    groups = per // TILE
    part = per // PARTS
    lane = lax.broadcasted_iota(I16, (TILE, TILE), 1)
    sub = lax.broadcasted_iota(I16, (TILE, TILE), 0)
    csub = lax.broadcasted_iota(I16, (crows, TILE), 0)
    incoming = {}

    def rows_of(s, k, q):
        start = k * per + q * part
        row = held(s) * per + start
        at = pl.ds(aligned(base(s) * per + start), part)
        return at, slice(row, row + part), start // TILE

    def weights(s, k):
        start = aligned(window(s) + k * TILE)
        at = aligned((block(s) * STEP + k) * TILE)
        mine = recv_s[pl.ds(at, TILE)]
        low = jnp.concatenate([sent_s[pl.ds(start, LOW * TILE)], mine], axis=0)
        high = jnp.concatenate(
            [
                sent_s[pl.ds(start + LOW * TILE, HIGH * TILE)],
                sent_s[pl.ds(start, (LOW - HIGH) * TILE)],
                mine,
            ],
            axis=0,
        )
        return jnp.concatenate([low, high], axis=1)

    def first(s, k, q):
        at, held_at, col0 = rows_of(s, k, q)
        code_t = code_s[block(s)]
        lhs, upper = [], []
        for j in range(part // TILE):
            word = column(code_t, col0 + j)
            o = word.astype(I16) & I16(511)
            r = (word >> 16).astype(I16) & I16(TILE - 1)
            lhs.append(jnp.concatenate(pick(o, lane, LOW) + pick(r, lane, 1), axis=1))
            upper.append(word < 0)
        y = pair_dot(edge_ref[at], we_s[...])
        out = dot(jnp.concatenate(lhs, axis=0), weights(s, k))
        yield
        y = y + jnp.where(jnp.concatenate(upper, axis=0), out[:, lat:], out[:, :lat])
        hid_s[held_at] = half_silu(y)

    def second(s, k, q):
        at, held_at, col0 = rows_of(s, k, q)
        c = pair_dot(hid_s[held_at], w2_s[...])
        yield
        new = (edge_ref[at].astype(F32) + scaled(c, m_s[...])).astype(BF)
        edge_ref[at] = new
        loc = loc_s[block(s)]
        back = [
            one_hot(along_lanes(loc[j : j + 1], TILE) == sub)
            for j in range(col0, col0 + part // TILE)
        ]
        incoming.setdefault(k + held(s), []).append((back, new))
        yield
        if q == PARTS - 1:
            backs, news = zip(*incoming.pop(k + held(s)))
            row = (held(s) + k) * TILE
            inc_s[row : row + TILE] = dot(
                jnp.concatenate(sum(backs, []), axis=1), jnp.concatenate(news, axis=0)
            ).astype(BF)

    def third(s):
        here = pl.ds(aligned(block(s) * STEP * TILE), STEP * TILE)
        own = own_ref[here]
        got = inc_s[held(s) * TILE : (held(s) + STEP) * TILE]
        y = dot(jnp.concatenate([own, got], axis=1), nw1_s[...])
        yield
        c = pair_dot(half_silu(y), nw2_s[...])
        yield
        var = pair_dot((c * c).astype(BF), nm_s[...])
        yield
        fine = (own.astype(F32) + c * lax.rsqrt(var + 1e-05)).astype(BF)
        fine_ref[here] = fine
        member = []
        for k in range(STEP):
            local = cmap_ref[pl.ds(block(s) * STEP + k, 1), :] - base_ref[0] * crows
            member.append(one_hot(along_lanes(local, crows) == csub))
        fine = jnp.concatenate([fine, jnp.ones_like(fine)], axis=1)
        pool_s[...] += dot(jnp.concatenate(member, axis=1), fine)

    return first, second, third


def run_stages(step, count, stages):
    first, second, third = stages
    parts = [(k, q) for k in range(STEP) for q in range(PARTS)]

    def run(one, two, three):
        interleave(
            [
                [second(step - 1, k, q)] * two + [first(step, k, q)] * one
                for k, q in (parts if one or two else [])
            ],
            [third(step - 2)] if three else [],
        )

    for when, which in (
        ((step >= 2) & (step < count), (True, True, True)),
        (step == 0, (True, False, False)),
        (step == 1, (True, True, False)),
        (step == count, (False, True, True)),
        (step == count + 1, (False, False, True)),
    ):
        pl.when(when)(functools.partial(run, *which))


def ready_kernel(base_ref, edge_ref, *refs):
    hbm, refs = refs[:12], refs[12:]
    (across_ref, within_ref, ws_ref, edges_ref, own_ref, cmap_ref), refs = refs[:6], refs[6:]
    ready, vmem, sem = refs[:10], refs[10:20], refs[20]
    send_ref, recv_ref, w1_ref, u_ref, v_ref = vmem[:5]
    edge_w2_ref, node_w1_ref, node_w2_ref, gain_ref, ngain_ref = vmem[5:]
    vmem = (own_ref, cmap_ref) + vmem
    sent_s, recv_s, we_s, w2_s, m_s, nw1_s, nw2_s, nm_s, code_s, loc_s = ready
    rows, lat = own_ref.shape
    idx_rows = send_ref.shape[0] // (rows // TILE) * STEP
    size = idx_rows * TILE
    copies = [pltpu.make_async_copy(a, b, sem.at[i]) for i, (a, b) in enumerate(zip(hbm, vmem))]
    order = [4, 5, 6, 0, 10, 11, 7, 9, 3, 2, 8, 1]
    for i in order:
        copies[i].start()
    early = pltpu.make_async_copy(
        edge_ref.at[pl.ds(size, size)], edges_ref.at[pl.ds(0, size)], sem.at[len(hbm)]
    )
    early.start()
    for i in order[:3]:
        copies[i].wait()
    w_eff = w1_ref[...].astype(F32) + lax.dot_general(
        u_ref[...], v_ref[...], (((0,), (0,)), ((), ())), preferred_element_type=F32
    )
    w_eff = (0.5 * w_eff).astype(BF)
    we_s[...] = twice(w_eff[:lat])
    ws = w_eff[lat : 2 * lat]
    ws_ref[...] = ws
    for i in order[3:]:
        copies[i].wait()
    even = base_ref[0] % 2 == 0
    head, tail = own_ref[:HALO], own_ref[rows - HALO :]
    across_ref[...] = jnp.where(even, head, tail)
    within_ref[...] = jnp.where(even, tail, head)
    both = dot(own_ref[...], jnp.concatenate([ws, w_eff[2 * lat :]], axis=1)).astype(BF)
    sent_s[...] = both[:, :lat]
    recv_s[...] = both[:, lat:]
    w2_s[...] = gained(edge_w2_ref[...], gain_ref[...])
    m_s[...] = mean_weight(gain_ref[...])
    nw1_s[...] = node_w1_ref[...] * 0.5
    nw2_s[...] = gained(node_w2_ref[...], ngain_ref[...])
    nm_s[...] = mean_square(ngain_ref[...])
    recv = recv_ref[...]
    loc = recv & (TILE - 1)
    off = send_ref[...] - (recv - loc) + HALO
    hi = off >= LOW * TILE
    lo = jnp.where(hi, off - LOW * TILE, off)
    code = lo | (loc << 16) | jnp.where(hi, jnp.int32(-(2**31)), 0)
    for s in range(rows // TILE // STEP):
        sl = slice(s * idx_rows, (s + 1) * idx_rows)
        code_s[s, :, 0:idx_rows] = code[sl].T
        loc_s[s, 0:idx_rows] = loc[sl]
    early.wait()


def inner_kernel(count, base_ref, all_ref, own_ref, cmap_ref, *refs):
    ready, refs = refs[:10], refs[11:]
    edges_ref, edge_out_ref, fine_ref, pool_ref, ends_ref, hid_s, inc_s, sem_in, sem_out = refs
    step = pl.program_id(0)
    size = hid_s.shape[0]

    def fetch(n):
        return pltpu.make_async_copy(
            all_ref.at[pl.ds((n + 1) * size, size)], edges_ref.at[pl.ds(n * size, size)],
            sem_in.at[n],
        )

    def store(n):
        return pltpu.make_async_copy(
            edges_ref.at[pl.ds(n * size, size)], edge_out_ref.at[pl.ds((n + 1) * size, size)],
            sem_out.at[n],
        )

    ends = [
        pltpu.make_async_copy(
            all_ref.at[pl.ds(at * size, size)], ends_ref.at[pl.ds(n * size, size)],
            sem_in.at[count + n],
        )
        for n, at in enumerate((0, count + 1))
    ]

    @pl.when(step == 0)
    def _():
        for n in range(1, count):
            fetch(n).start()
        for c in ends:
            c.start()
        pool_ref[...] = jnp.zeros_like(pool_ref)

    @pl.when((step > 0) & (step < count))
    def _():
        fetch(step).wait()

    run_stages(
        step, count,
        make_stages(
            lambda s: s + 1, lambda s: (s + 1) * STEP * TILE - HALO, lambda s: s * STEP,
            lambda s: 0,
            (edges_ref, own_ref, cmap_ref, fine_ref) + ready
            + (hid_s, inc_s, pool_ref, size // STEP),
            base_ref,
        ),
    )

    @pl.when((step > 0) & (step < count))
    def _():
        store(step - 1).start()

    @pl.when(step == count + 1)
    def _():
        for n in range(count - 1):
            store(n).wait()
        for c in ends:
            c.wait()


def border_kernel(
    last_block, base_ref, own_ref, across_ref, within_ref, cmap_ref, pool_ref, ws_ref, *refs
):
    ready, refs = refs[:10], refs[12:]
    ends_ref, fine_ref, coarse_ref, win_s, hid_s, inc_s, pool_s = refs
    sent_ref = ready[0]
    rows, lat = sent_ref.shape
    size = ends_ref.shape[0] // 2
    span = STEP * TILE + 2 * HALO
    inside = span - HALO
    even = base_ref[0] % 2 == 0
    across, within = across_ref[...], within_ref[...]
    ws = ws_ref[...]
    win_s[:HALO] = dot(jnp.where(even, across, within), ws).astype(BF)
    win_s[HALO:span] = sent_ref[:inside]
    win_s[span : span + inside] = sent_ref[rows - inside :]
    win_s[span + inside :] = dot(jnp.where(even, within, across), ws).astype(BF)
    pool_s[...] = pool_ref[...]
    first, second, third = make_stages(
        lambda s: s * last_block, lambda s: s * span, lambda s: s * STEP, lambda s: s * STEP,
        (ends_ref, own_ref, cmap_ref, fine_ref, win_s) + ready[1:]
        + (hid_s, inc_s, pool_s, size // STEP),
        base_ref,
    )
    parts = [(s, k, q) for s in range(2) for k in range(STEP) for q in range(PARTS)]
    half = STEP * PARTS
    ticks = [[] for _ in range(2 * half + 8)]
    for n, p in enumerate(parts):
        ticks[n].append(first(*p))
        ticks[n + 2].insert(0, second(*p))
    for s in range(2):
        done = (s + 1) * half + 1 + 3
        ticks[done].append(third(s))
    interleave(ticks, [])
    total = pool_s[...]
    coarse_ref[...] = (total[:, :lat] / jnp.maximum(total[:, lat:], 1.0)).astype(BF)


def near_kernel(
    last_block, base_ref, send_ref, recv_ref, own_ref, w1_ref, edges_ref, ends_ref, _, pre_ref,
    edge_out_ref, sem
):
    size = ends_ref.shape[0] // 2
    copies = [
        pltpu.make_async_copy(
            source.at[pl.ds(row, size)], edge_out_ref.at[pl.ds(at * size, size)], sem.at[n]
        )
        for n, (source, row, at) in enumerate(
            (
                (ends_ref, 0, 0),
                (ends_ref, size, last_block),
                (edges_ref, edges_ref.shape[0] - size, last_block - 1),
            )
        )
    ]
    for c in copies:
        c.start()
    crows, lat = own_ref.shape
    rows = send_ref.shape[0]
    first = base_ref[0] * crows
    blocks = crows // TILE
    send = send_ref[...] - first
    mine = (send >= 0) & (send < crows)
    code_t = (jnp.where(mine, send, crows) | ((recv_ref[...] - first) << 16)).T
    w1 = w1_ref[...] * 0.5
    rhs = dot(own_ref[...], jnp.concatenate([w1[:lat], w1[lat:]], axis=1)).astype(BF)
    rhs = jnp.concatenate([rhs[:, :lat], rhs[:, lat:]], axis=0)
    lane = lax.broadcasted_iota(I16, (TILE, TILE), 1)
    group = 3 if rows % 3 == 0 else 1

    def part(g):
        lhs = []
        for col in range(g, g + group):
            word = column(code_t, col)
            o, r = word.astype(I16), (word >> 16).astype(I16)
            lhs.append(jnp.concatenate(pick(o, lane, blocks) + pick(r, lane, blocks), axis=1))
        out = dot(jnp.concatenate(lhs, axis=0), rhs)
        yield
        pre_ref[g * TILE : (g + group) * TILE] = out

    interleave([[part(g)] for g in range(0, rows, group)], [])
    for c in copies:
        c.wait()


def coarse_kernel(
    base_ref, send_ref, recv_ref, cmap_ref, fine_ref, pre_ref, w1_ref, w2_ref, gain_ref, *refs
):
    (own_ref, *tables), (out_ref, out_s, sem) = refs[:-3], refs[-3:]
    dev = base_ref[0]
    crows, lat = own_ref.shape
    rows = send_ref.shape[0]
    nodes = fine_ref.shape[0]
    chunks = crows // TILE
    blocks = chunks * len(tables)
    lows = (blocks + 1) // 2
    send = send_ref[...]
    owner = lax.div(send, jnp.full_like(send, crows))
    other = owner ^ dev
    slot = jnp.full_like(send, -1)
    for j in range(len(tables)):
        slot = jnp.where(other == (1 << j), j, slot)
    off = send - owner * crows + slot * crows
    hi = off >= lows * TILE
    lo = jnp.where(hi, off - lows * TILE, off)
    code_t = jnp.where(
        slot < 0, lows * TILE, lo | jnp.where(hi, jnp.int32(-(2**31)), 0)
    ).T
    loc = recv_ref[...] - dev * crows
    w1 = twice(w1_ref[:lat] * 0.5)
    proj = jnp.concatenate([pair_dot(t[...], w1).astype(BF) for t in tables], axis=0)
    low, high = proj[: lows * TILE], proj[lows * TILE :]
    if high.shape[0] < low.shape[0]:
        high = jnp.concatenate([high, low[high.shape[0] :]], axis=0)
    rhs = jnp.concatenate([low, high], axis=1)
    lane = lax.broadcasted_iota(I16, (TILE, TILE), 1)
    csub = lax.broadcasted_iota(I16, (crows, TILE), 0)
    w2 = twice(w2_ref[...])
    group = 2 if rows % 2 == 0 else 1
    total = [own_ref[...].astype(F32)]

    def part(g):
        lhs, upper = [], []
        for col in range(g, g + group):
            word = column(code_t, col)
            lhs.append(jnp.concatenate(pick(word.astype(I16), lane, lows), axis=1))
            upper.append(word < 0)
        out = dot(jnp.concatenate(lhs, axis=0), rhs)
        yield
        y = jnp.where(jnp.concatenate(upper, axis=0), out[:, lat:], out[:, :lat])
        y = half_silu(y + pre_ref[g * TILE : (g + group) * TILE])
        msg = pair_dot(y, w2)
        yield
        back = [one_hot(along_lanes(loc[col : col + 1], crows) == csub) for col in range(g, g + group)]
        total[0] = total[0] + dot(jnp.concatenate(back, axis=1), msg.astype(BF))

    interleave([[part(g)] for g in range(0, rows, group)], [])
    total = total[0]
    centred = total - jnp.mean(total, axis=1, keepdims=True)
    var = jnp.mean(centred * centred, axis=1, keepdims=True)
    delta = (centred * lax.rsqrt(var + 1e-05) * gain_ref[...]).astype(BF)
    half = (chunks + 1) // 2
    high = delta[half * TILE :]
    if high.shape[0] < half * TILE:
        high = jnp.concatenate([high, delta[high.shape[0] : half * TILE]], axis=0)
    rhs = jnp.concatenate([delta[: half * TILE], high], axis=1)
    cm = cmap_ref[...] - dev * crows
    hi = cm >= half * TILE
    cm_t = (jnp.where(hi, cm - half * TILE, cm) | jnp.where(hi, jnp.int32(-(2**31)), 0)).T
    tiles = nodes // TILE
    size = 4 if tiles % 4 == 0 else 1
    copies = []

    def spread(p):
        hot, upper = [], []
        for t in range(p, p + size):
            word = column(cm_t, t)
            hot.append(jnp.concatenate(pick(word.astype(I16), lane, half), axis=1))
            upper.append(word < 0)
        out = dot(jnp.concatenate(hot, axis=0), rhs)
        yield
        back = jnp.where(jnp.concatenate(upper, axis=0), out[:, lat:], out[:, :lat])
        sl = pl.ds(p * TILE, size * TILE)
        out_s[sl] = (fine_ref[sl].astype(F32) + back).astype(BF)
        copies.append(pltpu.make_async_copy(out_s.at[sl], out_ref.at[sl], sem.at[p]))
        copies[-1].start()

    interleave([[spread(p)] for p in range(0, tiles, size)], [])
    for c in copies:
        c.wait()


def on_device(
    node_latent, edge_latent, receivers, senders, coarse_map, coarse_recv, coarse_send,
    edge_w1, mod_u, mod_v, edge_w2, edge_gain, node_w1, node_w2, node_gain,
    coarse_w1, coarse_w2, coarse_gain,
):
    axes = ("dom", "sub")
    size = lax.axis_size(axes)
    dev = lax.axis_index(axes).astype(jnp.int32).reshape(1)
    nodes, lat = node_latent.shape
    edges = edge_latent.shape[0]
    tiles = nodes // TILE
    per = edges // tiles
    crows = nodes // COARSEN
    steps = tiles // STEP
    cmap2 = coarse_map.reshape(tiles, TILE)
    vm = pl.BlockSpec(memory_space=pltpu.VMEM)
    sm = pl.BlockSpec(memory_space=pltpu.SMEM)
    hb = pl.BlockSpec(memory_space=pltpu.HBM)
    hbm = (
        node_latent, cmap2, senders.reshape(edges // TILE, TILE),
        receivers.reshape(edges // TILE, TILE), edge_w1, mod_u.T, mod_v, edge_w2, node_w1,
        node_w2, edge_gain.reshape(1, lat), node_gain.reshape(1, lat),
    )
    big = (STEP * per, lat)
    apart = lambda a: pltpu.with_memory_space_constraint(a, pltpu.HBM)
    far = apart(edge_latent)
    count = steps - 2
    full = jax.ShapeDtypeStruct((edges, lat), BF)
    ready = [
        jax.ShapeDtypeStruct(shape, dtype)
        for shape, dtype in [((nodes, lat), BF)] * 2
        + [((2 * lat, 2 * lat), BF)] * 2
        + [((1, lat), F32), ((2 * lat, lat), BF), ((2 * lat, 2 * lat), BF), ((2 * lat, 2 * lat), BF)]
        + [((steps, TILE, PAD), jnp.int32), ((steps, PAD, TILE), jnp.int32)]
    ]
    shape = jax.ShapeDtypeStruct
    params = pltpu.CompilerParams(vmem_limit_bytes=24 * 2**20)
    rows = STEP * per
    across, within, ws, inner_edges, own, cmap2, *ready = pl.pallas_call(
        ready_kernel,
        in_specs=[sm] + [hb] * (1 + len(hbm)),
        out_specs=[vm] * (6 + len(ready)),
        out_shape=[
            shape((HALO, lat), BF),
            shape((HALO, lat), BF),
            shape((lat, lat), BF),
            shape((count * rows, lat), BF),
            shape((nodes, lat), BF),
            shape(cmap2.shape, cmap2.dtype),
        ] + ready,
        scratch_shapes=[pltpu.VMEM(a.shape, a.dtype) for a in hbm[2:]]
        + [pltpu.SemaphoreType.DMA((len(hbm) + 1,))],
        compiler_params=params,
        name="ready",
    )(dev, far, *[apart(a) for a in hbm])
    pairs = [(i, i + 1) for i in range(1, size - 1, 2)]
    across = lax.ppermute(across, axes, pairs + [(j, i) for i, j in pairs])
    pairs = [(i, i + 1) for i in range(0, size, 2)]
    within = lax.ppermute(within, axes, pairs + [(j, i) for i, j in pairs])
    inner_edges, edge_out, fine, pool, ends = pl.pallas_call(
        functools.partial(inner_kernel, count),
        grid=(count + 2,),
        in_specs=[sm, hb] + [vm] * (3 + len(ready)),
        out_specs=[vm, hb, vm, vm, vm],
        out_shape=[
            shape((count * rows, lat), BF),
            full,
            shape((nodes, lat), BF),
            shape((crows, 2 * lat), F32),
            shape((2 * rows, lat), BF),
        ],
        input_output_aliases={4 + len(ready): 0},
        scratch_shapes=[
            pltpu.VMEM((rows, lat), BF),
            pltpu.VMEM((STEP * TILE, lat), BF),
            pltpu.SemaphoreType.DMA((count + 2,)),
            pltpu.SemaphoreType.DMA((count,)),
        ],
        compiler_params=pltpu.CompilerParams(
            dimension_semantics=("arbitrary",), vmem_limit_bytes=24 * 2**20
        ),
        name="inner",
    )(dev, far, own, cmap2, *ready, inner_edges)
    ends, fine, coarse = pl.pallas_call(
        functools.partial(border_kernel, steps - 1),
        in_specs=[sm] + [vm] * (8 + len(ready)),
        out_specs=[vm] * 3,
        out_shape=[shape((2 * rows, lat), BF), shape((nodes, lat), BF), shape((crows, lat), BF)],
        input_output_aliases={7 + len(ready): 0, 8 + len(ready): 1},
        scratch_shapes=[
            pltpu.VMEM((2 * (STEP * TILE + 2 * HALO), lat), BF),
            pltpu.VMEM((2 * rows, lat), BF),
            pltpu.VMEM((2 * STEP * TILE, lat), BF),
            pltpu.VMEM((crows, 2 * lat), F32),
        ],
        compiler_params=params,
        name="border",
    )(dev, own, across, within, cmap2, pool, ws, *ready, ends, fine)
    tables = [coarse]
    bit = 1
    while bit < size:
        tables.append(lax.ppermute(coarse, axes, [(i, i ^ bit) for i in range(size)]))
        bit *= 2
    cedges = coarse_send.shape[0]
    csend2 = coarse_send.reshape(cedges // TILE, TILE)
    crecv2 = coarse_recv.reshape(cedges // TILE, TILE)
    pre, edge_out = pl.pallas_call(
        functools.partial(near_kernel, steps - 1),
        in_specs=[sm] + [vm] * 6 + [hb],
        out_specs=[vm, hb],
        out_shape=[shape((cedges, lat), F32), full],
        input_output_aliases={7: 1},
        scratch_shapes=[pltpu.SemaphoreType.DMA((3,))],
        compiler_params=params,
        name="near",
    )(dev, csend2, crecv2, coarse, coarse_w1, inner_edges, ends, edge_out)
    node_out = pl.pallas_call(
        coarse_kernel,
        in_specs=[sm] + [vm] * (8 + len(tables)),
        out_specs=hb,
        out_shape=jax.ShapeDtypeStruct((nodes, lat), BF),
        scratch_shapes=[pltpu.VMEM((nodes, lat), BF), pltpu.SemaphoreType.DMA((tiles,))],
        compiler_params=pltpu.CompilerParams(vmem_limit_bytes=32 * 2**20),
        name="coarse",
    )(
        dev, csend2, crecv2, cmap2, fine, pre, coarse_w1, coarse_w2, coarse_gain.reshape(1, lat),
        *tables,
    )
    return (node_out, edge_out)


def solution(mesh):
    split = P(("groups", "dom", "sub"))
    wide = P(("groups", "dom", "sub"), None)
    return jax.shard_map(
        on_device,
        mesh=mesh,
        in_specs=(wide, wide) + (split,) * 5 + (P(),) * 11,
        out_specs=(wide, wide),
        check_vma=False,
    )
```

```python
import functools

import jax
import jax.numpy as jnp
from jax import lax
from jax.experimental import pallas as pl
from jax.experimental.pallas import tpu as pltpu
from jax.sharding import PartitionSpec as P

TILE = 128
HALO = 256
COARSEN = 8
STEP = 2
PARTS = 2
LOW = 3
HIGH = (TILE + 2 * HALO) // TILE - LOW
PAD = 16
BF = jnp.bfloat16
F32 = jnp.float32
I16 = jnp.int16


def dot(a, b):
    return jnp.dot(a, b, preferred_element_type=F32)


def one_hot(mask):
    return jnp.where(mask, jnp.ones((), BF), jnp.zeros((), BF))


def pick(off, lane, blocks):
    return [one_hot(off == lane + I16(c * TILE)) for c in range(blocks)]


def aligned(row):
    return row if isinstance(row, int) else pl.multiple_of(row, TILE)


def column(rows_t, col):
    return jnp.broadcast_to(rows_t[:, col : col + 1], (TILE, TILE))


def along_lanes(row, count):
    return jnp.broadcast_to(row, (count, TILE)).astype(I16)


def twice(w):
    z = jnp.zeros_like(w)
    return jnp.concatenate(
        [jnp.concatenate([w, z], axis=1), jnp.concatenate([z, w], axis=1)], axis=0
    )


def pair_dot(x, w2):
    half = x.shape[0] // 2
    out = dot(jnp.concatenate([x[:half], x[half:]], axis=1), w2)
    n = out.shape[1] // 2
    return jnp.concatenate([out[:, :n], out[:, n:]], axis=0)


def gained(w, gain):
    w = w.astype(F32)
    return twice(((w - jnp.mean(w, axis=1, keepdims=True)) * gain).astype(BF))


def mean_weight(gain):
    return 1.0 / (gain * gain * gain.shape[1])


def mean_square(gain):
    lat = gain.shape[1]
    return twice(jnp.broadcast_to(mean_weight(gain), (lat, lat)).T.astype(BF))


def scaled(c, weight):
    return c * lax.rsqrt(jnp.sum(c * c * weight, axis=1, keepdims=True) + 1e-05)


def half_silu(y):
    return (y * jnp.tanh(y) + y).astype(BF)


def interleave(queue, active):
    queue = list(queue)
    while active or queue:
        if queue:
            active = list(queue.pop(0)) + active
        alive = []
        for part in active:
            try:
                next(part)
                alive.append(part)
            except StopIteration:
                pass
        active = alive


def make_stages(block, window, base, held, refs, base_ref):
    edge_ref, own_ref, cmap_ref, fine_ref = refs[:4]
    sent_s, recv_s, we_s, w2_s, m_s, nw1_s, nw2_s, nm_s, code_s, loc_s = refs[4:14]
    hid_s, inc_s, pool_s, per = refs[14:]
    lat = sent_s.shape[1]
    crows = pool_s.shape[0]
    groups = per // TILE
    part = per // PARTS
    lane = lax.broadcasted_iota(I16, (TILE, TILE), 1)
    sub = lax.broadcasted_iota(I16, (TILE, TILE), 0)
    csub = lax.broadcasted_iota(I16, (crows, TILE), 0)
    incoming = {}

    def rows_of(s, k, q):
        start = k * per + q * part
        row = held(s) * per + start
        at = pl.ds(aligned(base(s) * per + start), part)
        return at, slice(row, row + part), start // TILE

    def weights(s, k):
        start = aligned(window(s) + k * TILE)
        at = aligned((block(s) * STEP + k) * TILE)
        mine = recv_s[pl.ds(at, TILE)]
        low = jnp.concatenate([sent_s[pl.ds(start, LOW * TILE)], mine], axis=0)
        high = jnp.concatenate(
            [
                sent_s[pl.ds(start + LOW * TILE, HIGH * TILE)],
                sent_s[pl.ds(start, (LOW - HIGH) * TILE)],
                mine,
            ],
            axis=0,
        )
        return jnp.concatenate([low, high], axis=1)

    def first(s, k, q):
        at, held_at, col0 = rows_of(s, k, q)
        code_t = code_s[block(s)]
        lhs, upper = [], []
        for j in range(part // TILE):
            word = column(code_t, col0 + j)
            o = word.astype(I16) & I16(511)
            r = (word >> 16).astype(I16) & I16(TILE - 1)
            lhs.append(jnp.concatenate(pick(o, lane, LOW) + pick(r, lane, 1), axis=1))
            upper.append(word < 0)
        y = pair_dot(edge_ref[at], we_s[...])
        out = dot(jnp.concatenate(lhs, axis=0), weights(s, k))
        yield
        y = y + jnp.where(jnp.concatenate(upper, axis=0), out[:, lat:], out[:, :lat])
        hid_s[held_at] = half_silu(y)

    def second(s, k, q):
        at, held_at, col0 = rows_of(s, k, q)
        c = pair_dot(hid_s[held_at], w2_s[...])
        yield
        new = (edge_ref[at].astype(F32) + scaled(c, m_s[...])).astype(BF)
        edge_ref[at] = new
        loc = loc_s[block(s)]
        back = [
            one_hot(along_lanes(loc[j : j + 1], TILE) == sub)
            for j in range(col0, col0 + part // TILE)
        ]
        incoming.setdefault(k + held(s), []).append((back, new))
        yield
        if q == PARTS - 1:
            backs, news = zip(*incoming.pop(k + held(s)))
            row = (held(s) + k) * TILE
            inc_s[row : row + TILE] = dot(
                jnp.concatenate(sum(backs, []), axis=1), jnp.concatenate(news, axis=0)
            ).astype(BF)

    def third(s):
        here = pl.ds(aligned(block(s) * STEP * TILE), STEP * TILE)
        own = own_ref[here]
        got = inc_s[held(s) * TILE : (held(s) + STEP) * TILE]
        y = dot(jnp.concatenate([own, got], axis=1), nw1_s[...])
        yield
        c = pair_dot(half_silu(y), nw2_s[...])
        yield
        var = pair_dot((c * c).astype(BF), nm_s[...])
        yield
        fine = (own.astype(F32) + c * lax.rsqrt(var + 1e-05)).astype(BF)
        fine_ref[here] = fine
        member = []
        for k in range(STEP):
            local = cmap_ref[pl.ds(block(s) * STEP + k, 1), :] - base_ref[0] * crows
            member.append(one_hot(along_lanes(local, crows) == csub))
        fine = jnp.concatenate([fine, jnp.ones_like(fine)], axis=1)
        pool_s[...] += dot(jnp.concatenate(member, axis=1), fine)

    return first, second, third


def run_stages(step, count, stages):
    first, second, third = stages
    parts = [(k, q) for k in range(STEP) for q in range(PARTS)]

    def run(one, two, three):
        interleave(
            [
                [second(step - 1, k, q)] * two + [first(step, k, q)] * one
                for k, q in (parts if one or two else [])
            ],
            [third(step - 2)] if three else [],
        )

    for when, which in (
        ((step >= 2) & (step < count), (True, True, True)),
        (step == 0, (True, False, False)),
        (step == 1, (True, True, False)),
        (step == count, (False, True, True)),
        (step == count + 1, (False, False, True)),
    ):
        pl.when(when)(functools.partial(run, *which))


def ready_kernel(base_ref, edge_ref, *refs):
    hbm, refs = refs[:12], refs[12:]
    (across_ref, within_ref, ws_ref, edges_ref, own_ref, cmap_ref), refs = refs[:6], refs[6:]
    ready, vmem, sem = refs[:10], refs[10:20], refs[20]
    send_ref, recv_ref, w1_ref, u_ref, v_ref = vmem[:5]
    edge_w2_ref, node_w1_ref, node_w2_ref, gain_ref, ngain_ref = vmem[5:]
    vmem = (own_ref, cmap_ref) + vmem
    sent_s, recv_s, we_s, w2_s, m_s, nw1_s, nw2_s, nm_s, code_s, loc_s = ready
    rows, lat = own_ref.shape
    idx_rows = send_ref.shape[0] // (rows // TILE) * STEP
    size = idx_rows * TILE
    copies = [pltpu.make_async_copy(a, b, sem.at[i]) for i, (a, b) in enumerate(zip(hbm, vmem))]
    order = [4, 5, 6, 0, 10, 11, 7, 9, 3, 2, 8, 1]
    for i in order:
        copies[i].start()
    early = pltpu.make_async_copy(
        edge_ref.at[pl.ds(size, size)], edges_ref.at[pl.ds(0, size)], sem.at[len(hbm)]
    )
    early.start()
    for i in order[:3]:
        copies[i].wait()
    w_eff = w1_ref[...].astype(F32) + lax.dot_general(
        u_ref[...], v_ref[...], (((0,), (0,)), ((), ())), preferred_element_type=F32
    )
    w_eff = (0.5 * w_eff).astype(BF)
    we_s[...] = twice(w_eff[:lat])
    ws = w_eff[lat : 2 * lat]
    ws_ref[...] = ws
    for i in order[3:]:
        copies[i].wait()
    even = base_ref[0] % 2 == 0
    head, tail = own_ref[:HALO], own_ref[rows - HALO :]
    across_ref[...] = jnp.where(even, head, tail)
    within_ref[...] = jnp.where(even, tail, head)
    both = dot(own_ref[...], jnp.concatenate([ws, w_eff[2 * lat :]], axis=1)).astype(BF)
    sent_s[...] = both[:, :lat]
    recv_s[...] = both[:, lat:]
    w2_s[...] = gained(edge_w2_ref[...], gain_ref[...])
    m_s[...] = mean_weight(gain_ref[...])
    nw1_s[...] = node_w1_ref[...] * 0.5
    nw2_s[...] = gained(node_w2_ref[...], ngain_ref[...])
    nm_s[...] = mean_square(ngain_ref[...])
    recv = recv_ref[...]
    loc = recv & (TILE - 1)
    off = send_ref[...] - (recv - loc) + HALO
    hi = off >= LOW * TILE
    lo = jnp.where(hi, off - LOW * TILE, off)
    code = lo | (loc << 16) | jnp.where(hi, jnp.int32(-(2**31)), 0)
    for s in range(rows // TILE // STEP):
        sl = slice(s * idx_rows, (s + 1) * idx_rows)
        code_s[s, :, 0:idx_rows] = code[sl].T
        loc_s[s, 0:idx_rows] = loc[sl]
    early.wait()


def inner_kernel(count, base_ref, all_ref, own_ref, cmap_ref, *refs):
    ready, refs = refs[:10], refs[11:]
    edges_ref, edge_out_ref, fine_ref, pool_ref, ends_ref, hid_s, inc_s, sem_in, sem_out = refs
    step = pl.program_id(0)
    size = hid_s.shape[0]

    def fetch(n):
        return pltpu.make_async_copy(
            all_ref.at[pl.ds((n + 1) * size, size)], edges_ref.at[pl.ds(n * size, size)],
            sem_in.at[n],
        )

    def store(n):
        return pltpu.make_async_copy(
            edges_ref.at[pl.ds(n * size, size)], edge_out_ref.at[pl.ds((n + 1) * size, size)],
            sem_out.at[n],
        )

    ends = [
        pltpu.make_async_copy(
            all_ref.at[pl.ds(at * size, size)], ends_ref.at[pl.ds(n * size, size)],
            sem_in.at[count + n],
        )
        for n, at in enumerate((0, count + 1))
    ]

    @pl.when(step == 0)
    def _():
        for n in range(1, count):
            fetch(n).start()
        for c in ends:
            c.start()
        pool_ref[...] = jnp.zeros_like(pool_ref)

    @pl.when((step > 0) & (step < count))
    def _():
        fetch(step).wait()

    run_stages(
        step, count,
        make_stages(
            lambda s: s + 1, lambda s: (s + 1) * STEP * TILE - HALO, lambda s: s * STEP,
            lambda s: 0,
            (edges_ref, own_ref, cmap_ref, fine_ref) + ready
            + (hid_s, inc_s, pool_ref, size // STEP),
            base_ref,
        ),
    )

    @pl.when((step > 0) & (step < count))
    def _():
        store(step - 1).start()

    @pl.when(step == count + 1)
    def _():
        for n in range(count - 1):
            store(n).wait()
        for c in ends:
            c.wait()


def border_kernel(
    last_block, base_ref, own_ref, across_ref, within_ref, cmap_ref, pool_ref, ws_ref, *refs
):
    ready, refs = refs[:10], refs[12:]
    ends_ref, fine_ref, coarse_ref, win_s, hid_s, inc_s, pool_s = refs
    sent_ref = ready[0]
    rows, lat = sent_ref.shape
    size = ends_ref.shape[0] // 2
    span = STEP * TILE + 2 * HALO
    inside = span - HALO
    even = base_ref[0] % 2 == 0
    across, within = across_ref[...], within_ref[...]
    ws = ws_ref[...]
    win_s[:HALO] = dot(jnp.where(even, across, within), ws).astype(BF)
    win_s[HALO:span] = sent_ref[:inside]
    win_s[span : span + inside] = sent_ref[rows - inside :]
    win_s[span + inside :] = dot(jnp.where(even, within, across), ws).astype(BF)
    pool_s[...] = pool_ref[...]
    first, second, third = make_stages(
        lambda s: s * last_block, lambda s: s * span, lambda s: s * STEP, lambda s: s * STEP,
        (ends_ref, own_ref, cmap_ref, fine_ref, win_s) + ready[1:]
        + (hid_s, inc_s, pool_s, size // STEP),
        base_ref,
    )
    parts = [(s, k, q) for s in range(2) for k in range(STEP) for q in range(PARTS)]
    half = STEP * PARTS
    ticks = [[] for _ in range(2 * half + 8)]
    for n, p in enumerate(parts):
        ticks[n].append(first(*p))
        ticks[n + 3].insert(0, second(*p))
    for s in range(2):
        done = (s + 1) * half + 5
        ticks[done].append(third(s))
    interleave(ticks, [])
    total = pool_s[...]
    coarse_ref[...] = (total[:, :lat] / jnp.maximum(total[:, lat:], 1.0)).astype(BF)


def half_blocks(blocks):
    return (blocks + 1) // 2


def in_halves(row, half):
    hi = row >= half * TILE
    return jnp.where(hi, (row - half * TILE) | jnp.int32(-(2**31)), row)


def near_kernel(
    last_block, partners, base_ref, send_ref, recv_ref, cmap_ref, own_ref, w1_ref, edges_ref,
    ends_ref, _, pre_ref, edge_out_ref, far_ref, spread_ref, sem
):
    size = ends_ref.shape[0] // 2
    copies = [
        pltpu.make_async_copy(
            source.at[pl.ds(row, size)], edge_out_ref.at[pl.ds(at * size, size)], sem.at[n]
        )
        for n, (source, row, at) in enumerate(
            (
                (ends_ref, 0, 0),
                (ends_ref, size, last_block),
                (edges_ref, edges_ref.shape[0] - size, last_block - 1),
            )
        )
    ]
    for c in copies:
        c.start()
    crows, lat = own_ref.shape
    rows = send_ref.shape[0]
    tiles = cmap_ref.shape[0]
    first = base_ref[0] * crows
    blocks = crows // TILE
    half, lows = half_blocks(blocks), half_blocks(blocks * partners)
    send = send_ref[...]
    owner = lax.div(send, jnp.full_like(send, crows))
    other = owner ^ base_ref[0]
    slot = jnp.full_like(send, -1)
    for j in range(partners):
        slot = jnp.where(other == (1 << j), j, slot)
    far = in_halves(jnp.where(slot < 0, 2 * lows * TILE, send - owner * crows + slot * crows), lows)
    far_t = far.T
    spread_t = in_halves(cmap_ref[...] - first, half).T
    send = send - first
    mine = (send >= 0) & (send < crows)
    code_t = (jnp.where(mine, send, crows) | ((recv_ref[...] - first) << 16)).T
    w1 = w1_ref[...] * 0.5
    rhs = dot(own_ref[...], jnp.concatenate([w1[:lat], w1[lat:]], axis=1)).astype(BF)
    rhs = jnp.concatenate([rhs[:, :lat], rhs[:, lat:]], axis=0)
    lane = lax.broadcasted_iota(I16, (TILE, TILE), 1)
    group = 3 if rows % 3 == 0 else 1

    def part(g):
        lhs = []
        for col in range(g, g + group):
            word = column(code_t, col)
            o, r = word.astype(I16), (word >> 16).astype(I16)
            lhs.append(jnp.concatenate(pick(o, lane, blocks) + pick(r, lane, blocks), axis=1))
        out = dot(jnp.concatenate(lhs, axis=0), rhs)
        yield
        pre_ref[g * TILE : (g + group) * TILE] = out
        for col in range(g, g + group):
            far_ref[col * TILE : (col + 1) * TILE] = column(far_t, col)
        for col in range(g * tiles // rows, (g + group) * tiles // rows):
            spread_ref[col * TILE : (col + 1) * TILE] = column(spread_t, col)

    interleave([[part(g)] for g in range(0, rows, group)], [])
    for c in copies:
        c.wait()


def coarse_kernel(
    base_ref, recv_ref, far_ref, spread_ref, fine_ref, pre_ref, w1_ref, w2_ref, gain_ref, *refs
):
    (own_ref, *tables), (out_ref, out_s, sem) = refs[:-3], refs[-3:]
    dev = base_ref[0]
    crows, lat = own_ref.shape
    rows = recv_ref.shape[0]
    nodes = fine_ref.shape[0]
    chunks = crows // TILE
    lows = half_blocks(chunks * len(tables))
    loc = recv_ref[...] - dev * crows
    w1 = twice(w1_ref[:lat] * 0.5)
    proj = jnp.concatenate([pair_dot(t[...], w1).astype(BF) for t in tables], axis=0)
    low, high = proj[: lows * TILE], proj[lows * TILE :]
    if high.shape[0] < low.shape[0]:
        high = jnp.concatenate([high, low[high.shape[0] :]], axis=0)
    rhs = jnp.concatenate([low, high], axis=1)
    lane = lax.broadcasted_iota(I16, (TILE, TILE), 1)
    csub = lax.broadcasted_iota(I16, (crows, TILE), 0)
    w2 = twice(w2_ref[...])
    group = 6 if rows % 6 == 0 else 1
    total = [own_ref[...].astype(F32)]

    def part(g):
        lhs, upper = [], []
        for col in range(g, g + group):
            word = far_ref[col * TILE : (col + 1) * TILE]
            lhs.append(jnp.concatenate(pick(word.astype(I16), lane, lows), axis=1))
            upper.append(word < 0)
        out = dot(jnp.concatenate(lhs, axis=0), rhs)
        yield
        y = jnp.where(jnp.concatenate(upper, axis=0), out[:, lat:], out[:, :lat])
        y = half_silu(y + pre_ref[g * TILE : (g + group) * TILE])
        msg = pair_dot(y, w2)
        yield
        back = [one_hot(along_lanes(loc[col : col + 1], crows) == csub) for col in range(g, g + group)]
        total[0] = total[0] + dot(jnp.concatenate(back, axis=1), msg.astype(BF))

    interleave([[part(g)] for g in range(0, rows, group)], [])
    total = total[0]
    centred = total - jnp.mean(total, axis=1, keepdims=True)
    var = jnp.mean(centred * centred, axis=1, keepdims=True)
    delta = (centred * lax.rsqrt(var + 1e-05) * gain_ref[...]).astype(BF)
    half = half_blocks(chunks)
    high = delta[half * TILE :]
    if high.shape[0] < half * TILE:
        high = jnp.concatenate([high, delta[high.shape[0] : half * TILE]], axis=0)
    rhs = jnp.concatenate([delta[: half * TILE], high], axis=1)
    tiles = nodes // TILE
    size = 4 if tiles % 4 == 0 else 1
    copies = []

    def spread(p):
        hot, upper = [], []
        for t in range(p, p + size):
            word = spread_ref[t * TILE : (t + 1) * TILE]
            hot.append(jnp.concatenate(pick(word.astype(I16), lane, half), axis=1))
            upper.append(word < 0)
        out = dot(jnp.concatenate(hot, axis=0), rhs)
        yield
        back = jnp.where(jnp.concatenate(upper, axis=0), out[:, lat:], out[:, :lat])
        sl = pl.ds(p * TILE, size * TILE)
        out_s[sl] = (fine_ref[sl].astype(F32) + back).astype(BF)
        copies.append(pltpu.make_async_copy(out_s.at[sl], out_ref.at[sl], sem.at[p]))
        copies[-1].start()

    interleave([[spread(p)] for p in range(0, tiles, size)], [])
    for c in copies:
        c.wait()


def on_device(
    node_latent, edge_latent, receivers, senders, coarse_map, coarse_recv, coarse_send,
    edge_w1, mod_u, mod_v, edge_w2, edge_gain, node_w1, node_w2, node_gain,
    coarse_w1, coarse_w2, coarse_gain,
):
    axes = ("dom", "sub")
    size = lax.axis_size(axes)
    dev = lax.axis_index(axes).astype(jnp.int32).reshape(1)
    nodes, lat = node_latent.shape
    edges = edge_latent.shape[0]
    tiles = nodes // TILE
    per = edges // tiles
    crows = nodes // COARSEN
    steps = tiles // STEP
    cmap2 = coarse_map.reshape(tiles, TILE)
    vm = pl.BlockSpec(memory_space=pltpu.VMEM)
    sm = pl.BlockSpec(memory_space=pltpu.SMEM)
    hb = pl.BlockSpec(memory_space=pltpu.HBM)
    hbm = (
        node_latent, cmap2, senders.reshape(edges // TILE, TILE),
        receivers.reshape(edges // TILE, TILE), edge_w1, mod_u.T, mod_v, edge_w2, node_w1,
        node_w2, edge_gain.reshape(1, lat), node_gain.reshape(1, lat),
    )
    big = (STEP * per, lat)
    apart = lambda a: pltpu.with_memory_space_constraint(a, pltpu.HBM)
    far = apart(edge_latent)
    count = steps - 2
    full = jax.ShapeDtypeStruct((edges, lat), BF)
    ready = [
        jax.ShapeDtypeStruct(shape, dtype)
        for shape, dtype in [((nodes, lat), BF)] * 2
        + [((2 * lat, 2 * lat), BF)] * 2
        + [((1, lat), F32), ((2 * lat, lat), BF), ((2 * lat, 2 * lat), BF), ((2 * lat, 2 * lat), BF)]
        + [((steps, TILE, PAD), jnp.int32), ((steps, PAD, TILE), jnp.int32)]
    ]
    shape = jax.ShapeDtypeStruct
    params = pltpu.CompilerParams(vmem_limit_bytes=24 * 2**20)
    rows = STEP * per
    across, within, ws, inner_edges, own, cmap2, *ready = pl.pallas_call(
        ready_kernel,
        in_specs=[sm] + [hb] * (1 + len(hbm)),
        out_specs=[vm] * (6 + len(ready)),
        out_shape=[
            shape((HALO, lat), BF),
            shape((HALO, lat), BF),
            shape((lat, lat), BF),
            shape((count * rows, lat), BF),
            shape((nodes, lat), BF),
            shape(cmap2.shape, cmap2.dtype),
        ] + ready,
        scratch_shapes=[pltpu.VMEM(a.shape, a.dtype) for a in hbm[2:]]
        + [pltpu.SemaphoreType.DMA((len(hbm) + 1,))],
        compiler_params=params,
        name="ready",
    )(dev, far, *[apart(a) for a in hbm])
    pairs = [(i, i + 1) for i in range(1, size - 1, 2)]
    across = lax.ppermute(across, axes, pairs + [(j, i) for i, j in pairs])
    pairs = [(i, i + 1) for i in range(0, size, 2)]
    within = lax.ppermute(within, axes, pairs + [(j, i) for i, j in pairs])
    inner_edges, edge_out, fine, pool, ends = pl.pallas_call(
        functools.partial(inner_kernel, count),
        grid=(count + 2,),
        in_specs=[sm, hb] + [vm] * (3 + len(ready)),
        out_specs=[vm, hb, vm, vm, vm],
        out_shape=[
            shape((count * rows, lat), BF),
            full,
            shape((nodes, lat), BF),
            shape((crows, 2 * lat), F32),
            shape((2 * rows, lat), BF),
        ],
        input_output_aliases={4 + len(ready): 0},
        scratch_shapes=[
            pltpu.VMEM((rows, lat), BF),
            pltpu.VMEM((STEP * TILE, lat), BF),
            pltpu.SemaphoreType.DMA((count + 2,)),
            pltpu.SemaphoreType.DMA((count,)),
        ],
        compiler_params=pltpu.CompilerParams(
            dimension_semantics=("arbitrary",), vmem_limit_bytes=24 * 2**20
        ),
        name="inner",
    )(dev, far, own, cmap2, *ready, inner_edges)
    ends, fine, coarse = pl.pallas_call(
        functools.partial(border_kernel, steps - 1),
        in_specs=[sm] + [vm] * (8 + len(ready)),
        out_specs=[vm] * 3,
        out_shape=[shape((2 * rows, lat), BF), shape((nodes, lat), BF), shape((crows, lat), BF)],
        input_output_aliases={7 + len(ready): 0, 8 + len(ready): 1},
        scratch_shapes=[
            pltpu.VMEM((2 * (STEP * TILE + 2 * HALO), lat), BF),
            pltpu.VMEM((2 * rows, lat), BF),
            pltpu.VMEM((2 * STEP * TILE, lat), BF),
            pltpu.VMEM((crows, 2 * lat), F32),
        ],
        compiler_params=params,
        name="border",
    )(dev, own, across, within, cmap2, pool, ws, *ready, ends, fine)
    tables = [coarse]
    bit = 1
    while bit < size:
        tables.append(lax.ppermute(coarse, axes, [(i, i ^ bit) for i in range(size)]))
        bit *= 2
    cedges = coarse_send.shape[0]
    csend2 = coarse_send.reshape(cedges // TILE, TILE)
    crecv2 = coarse_recv.reshape(cedges // TILE, TILE)
    pre, edge_out, far_words, spread_words = pl.pallas_call(
        functools.partial(near_kernel, steps - 1, len(tables) - 1),
        in_specs=[sm] + [vm] * 7 + [hb],
        out_specs=[vm, hb, vm, vm],
        out_shape=[
            shape((cedges, lat), F32),
            full,
            shape((cedges, TILE), jnp.int32),
            shape((nodes, TILE), jnp.int32),
        ],
        input_output_aliases={8: 1},
        scratch_shapes=[pltpu.SemaphoreType.DMA((3,))],
        compiler_params=params,
        name="near",
    )(dev, csend2, crecv2, cmap2, coarse, coarse_w1, inner_edges, ends, edge_out)
    node_out = pl.pallas_call(
        coarse_kernel,
        in_specs=[sm] + [vm] * (8 + len(tables)),
        out_specs=hb,
        out_shape=jax.ShapeDtypeStruct((nodes, lat), BF),
        scratch_shapes=[pltpu.VMEM((nodes, lat), BF), pltpu.SemaphoreType.DMA((tiles,))],
        compiler_params=pltpu.CompilerParams(vmem_limit_bytes=32 * 2**20),
        name="coarse",
    )(
        dev, crecv2, far_words, spread_words, fine, pre, coarse_w1, coarse_w2, coarse_gain.reshape(1, lat),
        *tables,
    )
    return (node_out, edge_out)


def solution(mesh):
    split = P(("groups", "dom", "sub"))
    wide = P(("groups", "dom", "sub"), None)
    return jax.shard_map(
        on_device,
        mesh=mesh,
        in_specs=(wide, wide) + (split,) * 5 + (P(),) * 11,
        out_specs=(wide, wide),
        check_vma=False,
    )
```

```python
import functools

import jax
import jax.numpy as jnp
from jax import lax
from jax.experimental import pallas as pl
from jax.experimental.pallas import tpu as pltpu
from jax.sharding import PartitionSpec as P

TILE = 128
HALO = 256
COARSEN = 8
STEP = 2
PARTS = 2
LOW = 3
HIGH = (TILE + 2 * HALO) // TILE - LOW
PAD = 16
BF = jnp.bfloat16
F32 = jnp.float32
I16 = jnp.int16


def dot(a, b):
    return jnp.dot(a, b, preferred_element_type=F32)


def one_hot(mask):
    return jnp.where(mask, jnp.ones((), BF), jnp.zeros((), BF))


def pick(off, lane, blocks):
    return [one_hot(off == lane + I16(c * TILE)) for c in range(blocks)]


def aligned(row):
    return row if isinstance(row, int) else pl.multiple_of(row, TILE)


def column(rows_t, col):
    return jnp.broadcast_to(rows_t[:, col : col + 1], (TILE, TILE))


def along_lanes(row, count):
    return jnp.broadcast_to(row, (count, TILE)).astype(I16)


def twice(w):
    z = jnp.zeros_like(w)
    return jnp.concatenate(
        [jnp.concatenate([w, z], axis=1), jnp.concatenate([z, w], axis=1)], axis=0
    )


def pair_dot(x, w2):
    half = x.shape[0] // 2
    out = dot(jnp.concatenate([x[:half], x[half:]], axis=1), w2)
    n = out.shape[1] // 2
    return jnp.concatenate([out[:, :n], out[:, n:]], axis=0)


def gained(w, gain):
    w = w.astype(F32)
    return twice(((w - jnp.mean(w, axis=1, keepdims=True)) * gain).astype(BF))


def mean_weight(gain):
    return 1.0 / (gain * gain * gain.shape[1])


def mean_square(gain):
    lat = gain.shape[1]
    return twice(jnp.broadcast_to(mean_weight(gain), (lat, lat)).T.astype(BF))


def scaled(c, weight):
    return c * lax.rsqrt(jnp.sum(c * c * weight, axis=1, keepdims=True) + 1e-05)


def half_silu(y):
    return (y * jnp.tanh(y) + y).astype(BF)


def interleave(queue, active):
    queue = list(queue)
    while active or queue:
        if queue:
            active = list(queue.pop(0)) + active
        alive = []
        for part in active:
            try:
                next(part)
                alive.append(part)
            except StopIteration:
                pass
        active = alive


def make_stages(block, window, base, held, refs, base_ref):
    edge_ref, own_ref, cmap_ref, fine_ref = refs[:4]
    sent_s, recv_s, we_s, w2_s, m_s, nw1_s, nw2_s, nm_s, code_s, loc_s = refs[4:14]
    hid_s, inc_s, pool_s, per = refs[14:]
    lat = sent_s.shape[1]
    crows = pool_s.shape[0]
    groups = per // TILE
    part = per // PARTS
    lane = lax.broadcasted_iota(I16, (TILE, TILE), 1)
    sub = lax.broadcasted_iota(I16, (TILE, TILE), 0)
    csub = lax.broadcasted_iota(I16, (crows, TILE), 0)
    incoming = {}

    def rows_of(s, k, q):
        start = k * per + q * part
        row = held(s) * per + start
        at = pl.ds(aligned(base(s) * per + start), part)
        return at, slice(row, row + part), start // TILE

    def weights(s, k):
        start = aligned(window(s) + k * TILE)
        at = aligned((block(s) * STEP + k) * TILE)
        mine = recv_s[pl.ds(at, TILE)]
        low = jnp.concatenate([sent_s[pl.ds(start, LOW * TILE)], mine], axis=0)
        high = jnp.concatenate(
            [
                sent_s[pl.ds(start + LOW * TILE, HIGH * TILE)],
                sent_s[pl.ds(start, (LOW - HIGH) * TILE)],
                mine,
            ],
            axis=0,
        )
        return jnp.concatenate([low, high], axis=1)

    def first(s, k, q):
        at, held_at, col0 = rows_of(s, k, q)
        code_t = code_s[block(s)]
        lhs, upper = [], []
        for j in range(part // TILE):
            word = column(code_t, col0 + j)
            o = word.astype(I16) & I16(511)
            r = (word >> 16).astype(I16) & I16(TILE - 1)
            lhs.append(jnp.concatenate(pick(o, lane, LOW) + pick(r, lane, 1), axis=1))
            upper.append(word < 0)
        y = pair_dot(edge_ref[at], we_s[...])
        out = dot(jnp.concatenate(lhs, axis=0), weights(s, k))
        yield
        y = y + jnp.where(jnp.concatenate(upper, axis=0), out[:, lat:], out[:, :lat])
        hid_s[held_at] = half_silu(y)

    def second(s, k, q):
        at, held_at, col0 = rows_of(s, k, q)
        c = pair_dot(hid_s[held_at], w2_s[...])
        yield
        new = (edge_ref[at].astype(F32) + scaled(c, m_s[...])).astype(BF)
        edge_ref[at] = new
        loc = loc_s[block(s)]
        back = [
            one_hot(along_lanes(loc[j : j + 1], TILE) == sub)
            for j in range(col0, col0 + part // TILE)
        ]
        incoming.setdefault(k + held(s), []).append((back, new))
        yield
        if q == PARTS - 1:
            backs, news = zip(*incoming.pop(k + held(s)))
            row = (held(s) + k) * TILE
            inc_s[row : row + TILE] = dot(
                jnp.concatenate(sum(backs, []), axis=1), jnp.concatenate(news, axis=0)
            ).astype(BF)

    def third(s):
        here = pl.ds(aligned(block(s) * STEP * TILE), STEP * TILE)
        own = own_ref[here]
        got = inc_s[held(s) * TILE : (held(s) + STEP) * TILE]
        y = dot(jnp.concatenate([own, got], axis=1), nw1_s[...])
        yield
        c = pair_dot(half_silu(y), nw2_s[...])
        yield
        var = pair_dot((c * c).astype(BF), nm_s[...])
        yield
        fine = (own.astype(F32) + c * lax.rsqrt(var + 1e-05)).astype(BF)
        fine_ref[here] = fine
        member = []
        for k in range(STEP):
            local = cmap_ref[pl.ds(block(s) * STEP + k, 1), :] - base_ref[0] * crows
            member.append(one_hot(along_lanes(local, crows) == csub))
        fine = jnp.concatenate([fine, jnp.ones_like(fine)], axis=1)
        pool_s[...] += dot(jnp.concatenate(member, axis=1), fine)

    return first, second, third


def run_stages(step, count, stages):
    first, second, third = stages
    parts = [(k, q) for k in range(STEP) for q in range(PARTS)]

    def run(one, two, three):
        interleave(
            [
                [second(step - 1, k, q)] * two + [first(step, k, q)] * one
                for k, q in (parts if one or two else [])
            ],
            [third(step - 2)] if three else [],
        )

    for when, which in (
        ((step >= 2) & (step < count), (True, True, True)),
        (step == 0, (True, False, False)),
        (step == 1, (True, True, False)),
        (step == count, (False, True, True)),
        (step == count + 1, (False, False, True)),
    ):
        pl.when(when)(functools.partial(run, *which))


def ready_kernel(base_ref, edge_ref, *refs):
    hbm, refs = refs[:12], refs[12:]
    (across_ref, within_ref, ws_ref, edges_ref, own_ref, cmap_ref), refs = refs[:6], refs[6:]
    ready, vmem, sem = refs[:10], refs[10:20], refs[20]
    send_ref, recv_ref, w1_ref, u_ref, v_ref = vmem[:5]
    edge_w2_ref, node_w1_ref, node_w2_ref, gain_ref, ngain_ref = vmem[5:]
    vmem = (own_ref, cmap_ref) + vmem
    sent_s, recv_s, we_s, w2_s, m_s, nw1_s, nw2_s, nm_s, code_s, loc_s = ready
    rows, lat = own_ref.shape
    idx_rows = send_ref.shape[0] // (rows // TILE) * STEP
    size = idx_rows * TILE
    copies = [pltpu.make_async_copy(a, b, sem.at[i]) for i, (a, b) in enumerate(zip(hbm, vmem))]
    order = [4, 5, 6, 0, 10, 11, 7, 9, 3, 2, 8, 1]
    for i in order:
        copies[i].start()
    early = pltpu.make_async_copy(
        edge_ref.at[pl.ds(size, size)], edges_ref.at[pl.ds(0, size)], sem.at[len(hbm)]
    )
    early.start()
    for i in order[:3]:
        copies[i].wait()
    w_eff = w1_ref[...].astype(F32) + lax.dot_general(
        u_ref[...], v_ref[...], (((0,), (0,)), ((), ())), preferred_element_type=F32
    )
    w_eff = (0.5 * w_eff).astype(BF)
    we_s[...] = twice(w_eff[:lat])
    ws = w_eff[lat : 2 * lat]
    ws_ref[...] = ws
    for i in order[3:]:
        copies[i].wait()
    even = base_ref[0] % 2 == 0
    head, tail = own_ref[:HALO], own_ref[rows - HALO :]
    across_ref[...] = jnp.where(even, head, tail)
    within_ref[...] = jnp.where(even, tail, head)
    both = dot(own_ref[...], jnp.concatenate([ws, w_eff[2 * lat :]], axis=1)).astype(BF)
    sent_s[...] = both[:, :lat]
    recv_s[...] = both[:, lat:]
    w2_s[...] = gained(edge_w2_ref[...], gain_ref[...])
    m_s[...] = mean_weight(gain_ref[...])
    nw1_s[...] = node_w1_ref[...] * 0.5
    nw2_s[...] = gained(node_w2_ref[...], ngain_ref[...])
    nm_s[...] = mean_square(ngain_ref[...])
    recv = recv_ref[...]
    loc = recv & (TILE - 1)
    off = send_ref[...] - (recv - loc) + HALO
    hi = off >= LOW * TILE
    lo = jnp.where(hi, off - LOW * TILE, off)
    code = lo | (loc << 16) | jnp.where(hi, jnp.int32(-(2**31)), 0)
    for s in range(rows // TILE // STEP):
        sl = slice(s * idx_rows, (s + 1) * idx_rows)
        code_s[s, :, 0:idx_rows] = code[sl].T
        loc_s[s, 0:idx_rows] = loc[sl]
    early.wait()


def inner_kernel(count, base_ref, all_ref, own_ref, cmap_ref, *refs):
    ready, refs = refs[:10], refs[11:]
    edges_ref, edge_out_ref, fine_ref, pool_ref, ends_ref, hid_s, inc_s, sem_in, sem_out = refs
    step = pl.program_id(0)
    size = hid_s.shape[0]

    def fetch(n):
        return pltpu.make_async_copy(
            all_ref.at[pl.ds((n + 1) * size, size)], edges_ref.at[pl.ds(n * size, size)],
            sem_in.at[n],
        )

    def store(n):
        return pltpu.make_async_copy(
            edges_ref.at[pl.ds(n * size, size)], edge_out_ref.at[pl.ds((n + 1) * size, size)],
            sem_out.at[n],
        )

    ends = [
        pltpu.make_async_copy(
            all_ref.at[pl.ds(at * size, size)], ends_ref.at[pl.ds(n * size, size)],
            sem_in.at[count + n],
        )
        for n, at in enumerate((0, count + 1))
    ]

    @pl.when(step == 0)
    def _():
        for n in range(1, count):
            fetch(n).start()
        for c in ends:
            c.start()
        pool_ref[...] = jnp.zeros_like(pool_ref)

    @pl.when((step > 0) & (step < count))
    def _():
        fetch(step).wait()

    run_stages(
        step, count,
        make_stages(
            lambda s: s + 1, lambda s: (s + 1) * STEP * TILE - HALO, lambda s: s * STEP,
            lambda s: 0,
            (edges_ref, own_ref, cmap_ref, fine_ref) + ready
            + (hid_s, inc_s, pool_ref, size // STEP),
            base_ref,
        ),
    )

    @pl.when((step > 0) & (step < count))
    def _():
        store(step - 1).start()

    @pl.when(step == count + 1)
    def _():
        for n in range(count - 1):
            store(n).wait()
        for c in ends:
            c.wait()


def border_kernel(
    last_block, base_ref, own_ref, across_ref, within_ref, cmap_ref, pool_ref, ws_ref, *refs
):
    ready, refs = refs[:10], refs[12:]
    ends_ref, fine_ref, coarse_ref, win_s, hid_s, inc_s, pool_s = refs
    sent_ref = ready[0]
    rows, lat = sent_ref.shape
    size = ends_ref.shape[0] // 2
    span = STEP * TILE + 2 * HALO
    inside = span - HALO
    even = base_ref[0] % 2 == 0
    across, within = across_ref[...], within_ref[...]
    ws = ws_ref[...]
    win_s[:HALO] = dot(jnp.where(even, across, within), ws).astype(BF)
    win_s[HALO:span] = sent_ref[:inside]
    win_s[span : span + inside] = sent_ref[rows - inside :]
    win_s[span + inside :] = dot(jnp.where(even, within, across), ws).astype(BF)
    pool_s[...] = pool_ref[...]
    first, second, third = make_stages(
        lambda s: s * last_block, lambda s: s * span, lambda s: s * STEP, lambda s: s * STEP,
        (ends_ref, own_ref, cmap_ref, fine_ref, win_s) + ready[1:]
        + (hid_s, inc_s, pool_s, size // STEP),
        base_ref,
    )
    parts = [(s, k, q) for s in range(2) for k in range(STEP) for q in range(PARTS)]
    half = STEP * PARTS
    ticks = [[] for _ in range(2 * half + 8)]
    for n, p in enumerate(parts):
        ticks[n].append(first(*p))
        ticks[n + 3].insert(0, second(*p))
    for s in range(2):
        done = (s + 1) * half + 5
        ticks[done].append(third(s))
    interleave(ticks, [])
    total = pool_s[...]
    coarse_ref[...] = (total[:, :lat] / jnp.maximum(total[:, lat:], 1.0)).astype(BF)


def half_blocks(blocks):
    return (blocks + 1) // 2


def in_halves(row, half):
    hi = row >= half * TILE
    return jnp.where(hi, (row - half * TILE) | jnp.int32(-(2**31)), row)


def near_kernel(
    last_block, partners, base_ref, send_ref, recv_ref, cmap_ref, own_ref, w1_ref, edges_ref,
    ends_ref, _, pre_ref, edge_out_ref, far_ref, spread_ref, sem
):
    size = ends_ref.shape[0] // 2
    copies = [
        pltpu.make_async_copy(
            source.at[pl.ds(row, size)], edge_out_ref.at[pl.ds(at * size, size)], sem.at[n]
        )
        for n, (source, row, at) in enumerate(
            (
                (ends_ref, 0, 0),
                (ends_ref, size, last_block),
                (edges_ref, edges_ref.shape[0] - size, last_block - 1),
            )
        )
    ]
    for c in copies:
        c.start()
    crows, lat = own_ref.shape
    rows = send_ref.shape[0]
    tiles = cmap_ref.shape[0]
    first = base_ref[0] * crows
    blocks = crows // TILE
    half, lows = half_blocks(blocks), half_blocks(blocks * partners)
    send = send_ref[...]
    owner = lax.div(send, jnp.full_like(send, crows))
    other = owner ^ base_ref[0]
    slot = jnp.full_like(send, -1)
    for j in range(partners):
        slot = jnp.where(other == (1 << j), j, slot)
    far = in_halves(jnp.where(slot < 0, 2 * lows * TILE, send - owner * crows + slot * crows), lows)
    far_t = far.T
    spread_t = in_halves(cmap_ref[...] - first, half).T
    send = send - first
    mine = (send >= 0) & (send < crows)
    code_t = (jnp.where(mine, send, crows) | ((recv_ref[...] - first) << 16)).T
    w1 = w1_ref[...] * 0.5
    rhs = dot(own_ref[...], jnp.concatenate([w1[:lat], w1[lat:]], axis=1)).astype(BF)
    rhs = jnp.concatenate([rhs[:, :lat], rhs[:, lat:]], axis=0)
    lane = lax.broadcasted_iota(I16, (TILE, TILE), 1)
    group = 3 if rows % 3 == 0 else 1

    def part(g):
        lhs = []
        for col in range(g, g + group):
            word = column(code_t, col)
            o, r = word.astype(I16), (word >> 16).astype(I16)
            lhs.append(jnp.concatenate(pick(o, lane, blocks) + pick(r, lane, blocks), axis=1))
        out = dot(jnp.concatenate(lhs, axis=0), rhs)
        yield
        pre_ref[g * TILE : (g + group) * TILE] = out
        for col in range(g, g + group):
            far_ref[col * TILE : (col + 1) * TILE] = column(far_t, col)
        for col in range(g * tiles // rows, (g + group) * tiles // rows):
            spread_ref[col * TILE : (col + 1) * TILE] = column(spread_t, col)

    interleave([[part(g)] for g in range(0, rows, group)], [])
    for c in copies:
        c.wait()


def coarse_kernel(
    base_ref, recv_ref, far_ref, spread_ref, fine_ref, pre_ref, w1_ref, w2_ref, gain_ref, *refs
):
    (own_ref, *tables), (out_ref, out_s, sem) = refs[:-3], refs[-3:]
    dev = base_ref[0]
    crows, lat = own_ref.shape
    rows = recv_ref.shape[0]
    nodes = fine_ref.shape[0]
    chunks = crows // TILE
    lows = half_blocks(chunks * len(tables))
    loc = recv_ref[...] - dev * crows
    w1 = twice(w1_ref[:lat] * 0.5)
    proj = jnp.concatenate([pair_dot(t[...], w1).astype(BF) for t in tables], axis=0)
    low, high = proj[: lows * TILE], proj[lows * TILE :]
    if high.shape[0] < low.shape[0]:
        high = jnp.concatenate([high, low[high.shape[0] :]], axis=0)
    rhs = jnp.concatenate([low, high], axis=1)
    lane = lax.broadcasted_iota(I16, (TILE, TILE), 1)
    csub = lax.broadcasted_iota(I16, (crows, TILE), 0)
    w2 = twice(w2_ref[...])
    group = next(g for g in (9, 6, 3, 2, 1) if rows % g == 0)
    total = [own_ref[...].astype(F32)]

    def part(g):
        lhs, upper = [], []
        for col in range(g, g + group):
            word = far_ref[col * TILE : (col + 1) * TILE]
            lhs.append(jnp.concatenate(pick(word.astype(I16), lane, lows), axis=1))
            upper.append(word < 0)
        out = dot(jnp.concatenate(lhs, axis=0), rhs)
        yield
        y = jnp.where(jnp.concatenate(upper, axis=0), out[:, lat:], out[:, :lat])
        y = half_silu(y + pre_ref[g * TILE : (g + group) * TILE])
        msg = pair_dot(y, w2)
        yield
        back = [one_hot(along_lanes(loc[col : col + 1], crows) == csub) for col in range(g, g + group)]
        total[0] = total[0] + dot(jnp.concatenate(back, axis=1), msg.astype(BF))

    interleave([[part(g)] for g in range(0, rows, group)], [])
    total = total[0]
    centred = total - jnp.mean(total, axis=1, keepdims=True)
    var = jnp.mean(centred * centred, axis=1, keepdims=True)
    delta = (centred * lax.rsqrt(var + 1e-05) * gain_ref[...]).astype(BF)
    half = half_blocks(chunks)
    high = delta[half * TILE :]
    if high.shape[0] < half * TILE:
        high = jnp.concatenate([high, delta[high.shape[0] : half * TILE]], axis=0)
    rhs = jnp.concatenate([delta[: half * TILE], high], axis=1)
    tiles = nodes // TILE
    size = 4 if tiles % 4 == 0 else 1
    copies = []

    def spread(p):
        hot, upper = [], []
        for t in range(p, p + size):
            word = spread_ref[t * TILE : (t + 1) * TILE]
            hot.append(jnp.concatenate(pick(word.astype(I16), lane, half), axis=1))
            upper.append(word < 0)
        out = dot(jnp.concatenate(hot, axis=0), rhs)
        yield
        back = jnp.where(jnp.concatenate(upper, axis=0), out[:, lat:], out[:, :lat])
        sl = pl.ds(p * TILE, size * TILE)
        out_s[sl] = (fine_ref[sl].astype(F32) + back).astype(BF)
        copies.append(pltpu.make_async_copy(out_s.at[sl], out_ref.at[sl], sem.at[p]))
        copies[-1].start()

    interleave([[spread(p)] for p in range(0, tiles, size)], [])
    for c in copies:
        c.wait()


def on_device(
    node_latent, edge_latent, receivers, senders, coarse_map, coarse_recv, coarse_send,
    edge_w1, mod_u, mod_v, edge_w2, edge_gain, node_w1, node_w2, node_gain,
    coarse_w1, coarse_w2, coarse_gain,
):
    axes = ("dom", "sub")
    size = lax.axis_size(axes)
    dev = lax.axis_index(axes).astype(jnp.int32).reshape(1)
    nodes, lat = node_latent.shape
    edges = edge_latent.shape[0]
    tiles = nodes // TILE
    per = edges // tiles
    crows = nodes // COARSEN
    steps = tiles // STEP
    cmap2 = coarse_map.reshape(tiles, TILE)
    vm = pl.BlockSpec(memory_space=pltpu.VMEM)
    sm = pl.BlockSpec(memory_space=pltpu.SMEM)
    hb = pl.BlockSpec(memory_space=pltpu.HBM)
    hbm = (
        node_latent, cmap2, senders.reshape(edges // TILE, TILE),
        receivers.reshape(edges // TILE, TILE), edge_w1, mod_u.T, mod_v, edge_w2, node_w1,
        node_w2, edge_gain.reshape(1, lat), node_gain.reshape(1, lat),
    )
    big = (STEP * per, lat)
    apart = lambda a: pltpu.with_memory_space_constraint(a, pltpu.HBM)
    far = apart(edge_latent)
    count = steps - 2
    full = jax.ShapeDtypeStruct((edges, lat), BF)
    ready = [
        jax.ShapeDtypeStruct(shape, dtype)
        for shape, dtype in [((nodes, lat), BF)] * 2
        + [((2 * lat, 2 * lat), BF)] * 2
        + [((1, lat), F32), ((2 * lat, lat), BF), ((2 * lat, 2 * lat), BF), ((2 * lat, 2 * lat), BF)]
        + [((steps, TILE, PAD), jnp.int32), ((steps, PAD, TILE), jnp.int32)]
    ]
    shape = jax.ShapeDtypeStruct
    params = pltpu.CompilerParams(vmem_limit_bytes=24 * 2**20)
    rows = STEP * per
    across, within, ws, inner_edges, own, cmap2, *ready = pl.pallas_call(
        ready_kernel,
        in_specs=[sm] + [hb] * (1 + len(hbm)),
        out_specs=[vm] * (6 + len(ready)),
        out_shape=[
            shape((HALO, lat), BF),
            shape((HALO, lat), BF),
            shape((lat, lat), BF),
            shape((count * rows, lat), BF),
            shape((nodes, lat), BF),
            shape(cmap2.shape, cmap2.dtype),
        ] + ready,
        scratch_shapes=[pltpu.VMEM(a.shape, a.dtype) for a in hbm[2:]]
        + [pltpu.SemaphoreType.DMA((len(hbm) + 1,))],
        compiler_params=params,
        name="ready",
    )(dev, far, *[apart(a) for a in hbm])
    pairs = [(i, i + 1) for i in range(1, size - 1, 2)]
    across = lax.ppermute(across, axes, pairs + [(j, i) for i, j in pairs])
    pairs = [(i, i + 1) for i in range(0, size, 2)]
    within = lax.ppermute(within, axes, pairs + [(j, i) for i, j in pairs])
    inner_edges, edge_out, fine, pool, ends = pl.pallas_call(
        functools.partial(inner_kernel, count),
        grid=(count + 2,),
        in_specs=[sm, hb] + [vm] * (3 + len(ready)),
        out_specs=[vm, hb, vm, vm, vm],
        out_shape=[
            shape((count * rows, lat), BF),
            full,
            shape((nodes, lat), BF),
            shape((crows, 2 * lat), F32),
            shape((2 * rows, lat), BF),
        ],
        input_output_aliases={4 + len(ready): 0},
        scratch_shapes=[
            pltpu.VMEM((rows, lat), BF),
            pltpu.VMEM((STEP * TILE, lat), BF),
            pltpu.SemaphoreType.DMA((count + 2,)),
            pltpu.SemaphoreType.DMA((count,)),
        ],
        compiler_params=pltpu.CompilerParams(
            dimension_semantics=("arbitrary",), vmem_limit_bytes=24 * 2**20
        ),
        name="inner",
    )(dev, far, own, cmap2, *ready, inner_edges)
    ends, fine, coarse = pl.pallas_call(
        functools.partial(border_kernel, steps - 1),
        in_specs=[sm] + [vm] * (8 + len(ready)),
        out_specs=[vm] * 3,
        out_shape=[shape((2 * rows, lat), BF), shape((nodes, lat), BF), shape((crows, lat), BF)],
        input_output_aliases={7 + len(ready): 0, 8 + len(ready): 1},
        scratch_shapes=[
            pltpu.VMEM((2 * (STEP * TILE + 2 * HALO), lat), BF),
            pltpu.VMEM((2 * rows, lat), BF),
            pltpu.VMEM((2 * STEP * TILE, lat), BF),
            pltpu.VMEM((crows, 2 * lat), F32),
        ],
        compiler_params=params,
        name="border",
    )(dev, own, across, within, cmap2, pool, ws, *ready, ends, fine)
    tables = [coarse]
    bit = 1
    while bit < size:
        tables.append(lax.ppermute(coarse, axes, [(i, i ^ bit) for i in range(size)]))
        bit *= 2
    cedges = coarse_send.shape[0]
    csend2 = coarse_send.reshape(cedges // TILE, TILE)
    crecv2 = coarse_recv.reshape(cedges // TILE, TILE)
    pre, edge_out, far_words, spread_words = pl.pallas_call(
        functools.partial(near_kernel, steps - 1, len(tables) - 1),
        in_specs=[sm] + [vm] * 7 + [hb],
        out_specs=[vm, hb, vm, vm],
        out_shape=[
            shape((cedges, lat), F32),
            full,
            shape((cedges, TILE), jnp.int32),
            shape((nodes, TILE), jnp.int32),
        ],
        input_output_aliases={8: 1},
        scratch_shapes=[pltpu.SemaphoreType.DMA((3,))],
        compiler_params=params,
        name="near",
    )(dev, csend2, crecv2, cmap2, coarse, coarse_w1, inner_edges, ends, edge_out)
    node_out = pl.pallas_call(
        coarse_kernel,
        in_specs=[sm] + [vm] * (8 + len(tables)),
        out_specs=hb,
        out_shape=jax.ShapeDtypeStruct((nodes, lat), BF),
        scratch_shapes=[pltpu.VMEM((nodes, lat), BF), pltpu.SemaphoreType.DMA((tiles,))],
        compiler_params=pltpu.CompilerParams(vmem_limit_bytes=32 * 2**20),
        name="coarse",
    )(
        dev, crecv2, far_words, spread_words, fine, pre, coarse_w1, coarse_w2, coarse_gain.reshape(1, lat),
        *tables,
    )
    return (node_out, edge_out)


def solution(mesh):
    split = P(("groups", "dom", "sub"))
    wide = P(("groups", "dom", "sub"), None)
    return jax.shard_map(
        on_device,
        mesh=mesh,
        in_specs=(wide, wide) + (split,) * 5 + (P(),) * 11,
        out_specs=(wide, wide),
        check_vma=False,
    )
```

```python
import functools

import jax
import jax.numpy as jnp
from jax import lax
from jax.experimental import pallas as pl
from jax.experimental.pallas import tpu as pltpu
from jax.sharding import PartitionSpec as P

TILE = 128
HALO = 256
COARSEN = 8
STEP = 2
PARTS = 2
LOW = 3
HIGH = (TILE + 2 * HALO) // TILE - LOW
PAD = 16
BF = jnp.bfloat16
F32 = jnp.float32
I16 = jnp.int16


def dot(a, b):
    return jnp.dot(a, b, preferred_element_type=F32)


def one_hot(mask):
    return jnp.where(mask, jnp.ones((), BF), jnp.zeros((), BF))


def pick(off, lane, blocks):
    return [one_hot(off == lane + I16(c * TILE)) for c in range(blocks)]


def aligned(row):
    return row if isinstance(row, int) else pl.multiple_of(row, TILE)


def column(rows_t, col):
    return jnp.broadcast_to(rows_t[:, col : col + 1], (TILE, TILE))


def along_lanes(row, count):
    return jnp.broadcast_to(row, (count, TILE)).astype(I16)


def twice(w):
    z = jnp.zeros_like(w)
    return jnp.concatenate(
        [jnp.concatenate([w, z], axis=1), jnp.concatenate([z, w], axis=1)], axis=0
    )


def pair_dot(x, w2):
    half = x.shape[0] // 2
    out = dot(jnp.concatenate([x[:half], x[half:]], axis=1), w2)
    n = out.shape[1] // 2
    return jnp.concatenate([out[:, :n], out[:, n:]], axis=0)


def gained(w, gain):
    w = w.astype(F32)
    return twice(((w - jnp.mean(w, axis=1, keepdims=True)) * gain).astype(BF))


def mean_weight(gain):
    return 1.0 / (gain * gain * gain.shape[1])


def mean_square(gain):
    lat = gain.shape[1]
    return twice(jnp.broadcast_to(mean_weight(gain), (lat, lat)).T.astype(BF))


def scaled(c, weight):
    return c * lax.rsqrt(jnp.sum(c * c * weight, axis=1, keepdims=True) + 1e-05)


def half_silu(y):
    return (y * jnp.tanh(y) + y).astype(BF)


def interleave(queue, active):
    queue = list(queue)
    while active or queue:
        if queue:
            active = list(queue.pop(0)) + active
        alive = []
        for part in active:
            try:
                next(part)
                alive.append(part)
            except StopIteration:
                pass
        active = alive


def make_stages(block, window, base, held, refs, base_ref):
    edge_ref, own_ref, cmap_ref, fine_ref = refs[:4]
    sent_s, recv_s, we_s, w2_s, m_s, nw1_s, nw2_s, nm_s, code_s, loc_s = refs[4:14]
    hid_s, inc_s, pool_s, per = refs[14:]
    lat = sent_s.shape[1]
    crows = pool_s.shape[0]
    groups = per // TILE
    part = per // PARTS
    lane = lax.broadcasted_iota(I16, (TILE, TILE), 1)
    sub = lax.broadcasted_iota(I16, (TILE, TILE), 0)
    csub = lax.broadcasted_iota(I16, (crows, TILE), 0)
    incoming = {}

    def rows_of(s, k, q):
        start = k * per + q * part
        row = held(s) * per + start
        at = pl.ds(aligned(base(s) * per + start), part)
        return at, slice(row, row + part), start // TILE

    def weights(s, k):
        start = aligned(window(s) + k * TILE)
        at = aligned((block(s) * STEP + k) * TILE)
        mine = recv_s[pl.ds(at, TILE)]
        low = jnp.concatenate([sent_s[pl.ds(start, LOW * TILE)], mine], axis=0)
        high = jnp.concatenate(
            [
                sent_s[pl.ds(start + LOW * TILE, HIGH * TILE)],
                sent_s[pl.ds(start, (LOW - HIGH) * TILE)],
                mine,
            ],
            axis=0,
        )
        return jnp.concatenate([low, high], axis=1)

    def first(s, k, q):
        at, held_at, col0 = rows_of(s, k, q)
        code_t = code_s[block(s)]
        lhs, upper = [], []
        for j in range(part // TILE):
            word = column(code_t, col0 + j)
            o = word.astype(I16) & I16(511)
            r = (word >> 16).astype(I16) & I16(TILE - 1)
            lhs.append(jnp.concatenate(pick(o, lane, LOW) + pick(r, lane, 1), axis=1))
            upper.append(word < 0)
        y = pair_dot(edge_ref[at], we_s[...])
        out = dot(jnp.concatenate(lhs, axis=0), weights(s, k))
        yield
        y = y + jnp.where(jnp.concatenate(upper, axis=0), out[:, lat:], out[:, :lat])
        hid_s[held_at] = half_silu(y)

    def second(s, k, q):
        at, held_at, col0 = rows_of(s, k, q)
        c = pair_dot(hid_s[held_at], w2_s[...])
        yield
        new = (edge_ref[at].astype(F32) + scaled(c, m_s[...])).astype(BF)
        edge_ref[at] = new
        loc = loc_s[block(s)]
        back = [
            one_hot(along_lanes(loc[j : j + 1], TILE) == sub)
            for j in range(col0, col0 + part // TILE)
        ]
        incoming.setdefault(k + held(s), []).append((back, new))
        yield
        if q == PARTS - 1:
            backs, news = zip(*incoming.pop(k + held(s)))
            row = (held(s) + k) * TILE
            inc_s[row : row + TILE] = dot(
                jnp.concatenate(sum(backs, []), axis=1), jnp.concatenate(news, axis=0)
            ).astype(BF)

    def third(s):
        here = pl.ds(aligned(block(s) * STEP * TILE), STEP * TILE)
        own = own_ref[here]
        got = inc_s[held(s) * TILE : (held(s) + STEP) * TILE]
        y = dot(jnp.concatenate([own, got], axis=1), nw1_s[...])
        yield
        c = pair_dot(half_silu(y), nw2_s[...])
        yield
        var = pair_dot((c * c).astype(BF), nm_s[...])
        yield
        fine = (own.astype(F32) + c * lax.rsqrt(var + 1e-05)).astype(BF)
        fine_ref[here] = fine
        member = []
        for k in range(STEP):
            local = cmap_ref[pl.ds(block(s) * STEP + k, 1), :] - base_ref[0] * crows
            member.append(one_hot(along_lanes(local, crows) == csub))
        fine = jnp.concatenate([fine, jnp.ones_like(fine)], axis=1)
        pool_s[...] += dot(jnp.concatenate(member, axis=1), fine)

    return first, second, third


def run_stages(step, count, stages):
    first, second, third = stages
    parts = [(k, q) for k in range(STEP) for q in range(PARTS)]

    def run(one, two, three):
        interleave(
            [
                [second(step - 1, k, q)] * two + [first(step, k, q)] * one
                for k, q in (parts if one or two else [])
            ],
            [third(step - 2)] if three else [],
        )

    for when, which in (
        ((step >= 2) & (step < count), (True, True, True)),
        (step == 0, (True, False, False)),
        (step == 1, (True, True, False)),
        (step == count, (False, True, True)),
        (step == count + 1, (False, False, True)),
    ):
        pl.when(when)(functools.partial(run, *which))


def ready_kernel(base_ref, edge_ref, *refs):
    hbm, refs = refs[:12], refs[12:]
    (across_ref, within_ref, ws_ref, edges_ref, own_ref, cmap_ref), refs = refs[:6], refs[6:]
    ready, vmem, sem = refs[:10], refs[10:20], refs[20]
    send_ref, recv_ref, w1_ref, u_ref, v_ref = vmem[:5]
    edge_w2_ref, node_w1_ref, node_w2_ref, gain_ref, ngain_ref = vmem[5:]
    vmem = (own_ref, cmap_ref) + vmem
    sent_s, recv_s, we_s, w2_s, m_s, nw1_s, nw2_s, nm_s, code_s, loc_s = ready
    rows, lat = own_ref.shape
    idx_rows = send_ref.shape[0] // (rows // TILE) * STEP
    size = idx_rows * TILE
    copies = [pltpu.make_async_copy(a, b, sem.at[i]) for i, (a, b) in enumerate(zip(hbm, vmem))]
    order = [4, 5, 6, 0, 10, 11, 7, 9, 3, 2, 8, 1]
    for i in order:
        copies[i].start()
    early = pltpu.make_async_copy(
        edge_ref.at[pl.ds(size, size)], edges_ref.at[pl.ds(0, size)], sem.at[len(hbm)]
    )
    early.start()
    for i in order[:3]:
        copies[i].wait()
    w_eff = w1_ref[...].astype(F32) + lax.dot_general(
        u_ref[...], v_ref[...], (((0,), (0,)), ((), ())), preferred_element_type=F32
    )
    w_eff = (0.5 * w_eff).astype(BF)
    we_s[...] = twice(w_eff[:lat])
    ws = w_eff[lat : 2 * lat]
    ws_ref[...] = ws
    for i in order[3:]:
        copies[i].wait()
    even = base_ref[0] % 2 == 0
    head, tail = own_ref[:HALO], own_ref[rows - HALO :]
    across_ref[...] = jnp.where(even, head, tail)
    within_ref[...] = jnp.where(even, tail, head)
    both = dot(own_ref[...], jnp.concatenate([ws, w_eff[2 * lat :]], axis=1)).astype(BF)
    sent_s[...] = both[:, :lat]
    recv_s[...] = both[:, lat:]
    w2_s[...] = gained(edge_w2_ref[...], gain_ref[...])
    m_s[...] = mean_weight(gain_ref[...])
    nw1_s[...] = node_w1_ref[...] * 0.5
    nw2_s[...] = gained(node_w2_ref[...], ngain_ref[...])
    nm_s[...] = mean_square(ngain_ref[...])
    recv = recv_ref[...]
    loc = recv & (TILE - 1)
    off = send_ref[...] - (recv - loc) + HALO
    hi = off >= LOW * TILE
    lo = jnp.where(hi, off - LOW * TILE, off)
    code = lo | (loc << 16) | jnp.where(hi, jnp.int32(-(2**31)), 0)
    for s in range(rows // TILE // STEP):
        sl = slice(s * idx_rows, (s + 1) * idx_rows)
        code_s[s, :, 0:idx_rows] = code[sl].T
        loc_s[s, 0:idx_rows] = loc[sl]
    early.wait()


def inner_kernel(count, base_ref, all_ref, own_ref, cmap_ref, *refs):
    ready, refs = refs[:10], refs[11:]
    edges_ref, edge_out_ref, fine_ref, pool_ref, ends_ref, hid_s, inc_s, sem_in, sem_out = refs
    step = pl.program_id(0)
    size = hid_s.shape[0]

    def fetch(n):
        return pltpu.make_async_copy(
            all_ref.at[pl.ds((n + 1) * size, size)], edges_ref.at[pl.ds(n * size, size)],
            sem_in.at[n],
        )

    def store(n):
        return pltpu.make_async_copy(
            edges_ref.at[pl.ds(n * size, size)], edge_out_ref.at[pl.ds((n + 1) * size, size)],
            sem_out.at[n],
        )

    ends = [
        pltpu.make_async_copy(
            all_ref.at[pl.ds(at * size, size)], ends_ref.at[pl.ds(n * size, size)],
            sem_in.at[count + n],
        )
        for n, at in enumerate((0, count + 1))
    ]

    @pl.when(step == 0)
    def _():
        for n in range(1, count):
            fetch(n).start()
        for c in ends:
            c.start()
        pool_ref[...] = jnp.zeros_like(pool_ref)

    @pl.when((step > 0) & (step < count))
    def _():
        fetch(step).wait()

    run_stages(
        step, count,
        make_stages(
            lambda s: s + 1, lambda s: (s + 1) * STEP * TILE - HALO, lambda s: s * STEP,
            lambda s: 0,
            (edges_ref, own_ref, cmap_ref, fine_ref) + ready
            + (hid_s, inc_s, pool_ref, size // STEP),
            base_ref,
        ),
    )

    @pl.when((step > 0) & (step < count))
    def _():
        store(step - 1).start()

    @pl.when(step == count + 1)
    def _():
        for n in range(count - 1):
            store(n).wait()
        for c in ends:
            c.wait()


def border_kernel(
    last_block, base_ref, own_ref, across_ref, within_ref, cmap_ref, pool_ref, ws_ref, *refs
):
    ready, refs = refs[:10], refs[12:]
    ends_ref, fine_ref, coarse_ref, win_s, hid_s, inc_s, pool_s = refs
    sent_ref = ready[0]
    rows, lat = sent_ref.shape
    size = ends_ref.shape[0] // 2
    span = STEP * TILE + 2 * HALO
    inside = span - HALO
    even = base_ref[0] % 2 == 0
    across, within = across_ref[...], within_ref[...]
    ws = ws_ref[...]
    win_s[:HALO] = dot(jnp.where(even, across, within), ws).astype(BF)
    win_s[HALO:span] = sent_ref[:inside]
    win_s[span : span + inside] = sent_ref[rows - inside :]
    win_s[span + inside :] = dot(jnp.where(even, within, across), ws).astype(BF)
    pool_s[...] = pool_ref[...]
    first, second, third = make_stages(
        lambda s: s * last_block, lambda s: s * span, lambda s: s * STEP, lambda s: s * STEP,
        (ends_ref, own_ref, cmap_ref, fine_ref, win_s) + ready[1:]
        + (hid_s, inc_s, pool_s, size // STEP),
        base_ref,
    )
    parts = [(s, k, q) for s in range(2) for k in range(STEP) for q in range(PARTS)]
    half = STEP * PARTS
    ticks = [[] for _ in range(2 * half + 8)]
    for n, p in enumerate(parts):
        ticks[n].append(first(*p))
        ticks[n + 3].insert(0, second(*p))
    for s in range(2):
        done = (s + 1) * half + 5
        ticks[done].append(third(s))
    interleave(ticks, [])
    total = pool_s[...]
    coarse_ref[...] = (total[:, :lat] / jnp.maximum(total[:, lat:], 1.0)).astype(BF)


def half_blocks(blocks):
    return (blocks + 1) // 2


def in_halves(row, half):
    hi = row >= half * TILE
    return jnp.where(hi, (row - half * TILE) | jnp.int32(-(2**31)), row)


def near_kernel(
    last_block, partners, base_ref, send_ref, recv_ref, cmap_ref, own_ref, w1_ref, edges_ref,
    ends_ref, _, pre_ref, edge_out_ref, far_ref, spread_ref, sem
):
    size = ends_ref.shape[0] // 2
    copies = [
        pltpu.make_async_copy(
            source.at[pl.ds(row, size)], edge_out_ref.at[pl.ds(at * size, size)], sem.at[n]
        )
        for n, (source, row, at) in enumerate(
            (
                (ends_ref, 0, 0),
                (ends_ref, size, last_block),
                (edges_ref, edges_ref.shape[0] - size, last_block - 1),
            )
        )
    ]
    for c in copies:
        c.start()
    crows, lat = own_ref.shape
    rows = send_ref.shape[0]
    tiles = cmap_ref.shape[0]
    first = base_ref[0] * crows
    blocks = crows // TILE
    half, lows = half_blocks(blocks), half_blocks(blocks * partners)
    send = send_ref[...]
    owner = lax.div(send, jnp.full_like(send, crows))
    other = owner ^ base_ref[0]
    slot = jnp.full_like(send, -1)
    for j in range(partners):
        slot = jnp.where(other == (1 << j), j, slot)
    far = in_halves(jnp.where(slot < 0, 2 * lows * TILE, send - owner * crows + slot * crows), lows)
    far_t = far.T
    spread_t = in_halves(cmap_ref[...] - first, half).T
    send = send - first
    mine = (send >= 0) & (send < crows)
    code_t = (jnp.where(mine, send, crows) | ((recv_ref[...] - first) << 16)).T
    w1 = w1_ref[...] * 0.5
    rhs = dot(own_ref[...], jnp.concatenate([w1[:lat], w1[lat:]], axis=1)).astype(BF)
    rhs = jnp.concatenate([rhs[:, :lat], rhs[:, lat:]], axis=0)
    lane = lax.broadcasted_iota(I16, (TILE, TILE), 1)
    group = 3 if rows % 3 == 0 else 1

    def part(g):
        lhs = []
        for col in range(g, g + group):
            word = column(code_t, col)
            o, r = word.astype(I16), (word >> 16).astype(I16)
            lhs.append(jnp.concatenate(pick(o, lane, blocks) + pick(r, lane, blocks), axis=1))
        out = dot(jnp.concatenate(lhs, axis=0), rhs)
        yield
        pre_ref[g * TILE : (g + group) * TILE] = out
        for col in range(g, g + group):
            far_ref[col * TILE : (col + 1) * TILE] = column(far_t, col)
        for col in range(g * tiles // rows, (g + group) * tiles // rows):
            spread_ref[col * TILE : (col + 1) * TILE] = column(spread_t, col)

    interleave([[part(g)] for g in range(0, rows, group)], [])
    for c in copies:
        c.wait()


def coarse_kernel(
    base_ref, recv_ref, far_ref, spread_ref, fine_ref, pre_ref, w1_ref, w2_ref, gain_ref, *refs
):
    (own_ref, *tables), (out_ref, out_s, sem) = refs[:-3], refs[-3:]
    dev = base_ref[0]
    crows, lat = own_ref.shape
    rows = recv_ref.shape[0]
    nodes = fine_ref.shape[0]
    chunks = crows // TILE
    lows = half_blocks(chunks * len(tables))
    loc = recv_ref[...] - dev * crows
    w1 = twice(w1_ref[:lat] * 0.5)
    proj = jnp.concatenate([t[...] for t in tables], axis=0)
    low, high = proj[: lows * TILE], proj[lows * TILE :]
    if high.shape[0] < low.shape[0]:
        high = jnp.concatenate([high, low[high.shape[0] :]], axis=0)
    rhs = jnp.concatenate([low, high], axis=1)
    lane = lax.broadcasted_iota(I16, (TILE, TILE), 1)
    csub = lax.broadcasted_iota(I16, (crows, TILE), 0)
    w2 = twice(w2_ref[...])
    group = next(g for g in (9, 6, 3, 2, 1) if rows % g == 0)
    total = [own_ref[...].astype(F32)]

    def part(g):
        lhs, upper = [], []
        for col in range(g, g + group):
            word = far_ref[col * TILE : (col + 1) * TILE]
            lhs.append(jnp.concatenate(pick(word.astype(I16), lane, lows), axis=1))
            upper.append(word < 0)
        out = dot(jnp.concatenate(lhs, axis=0), rhs)
        yield
        y = jnp.where(jnp.concatenate(upper, axis=0), out[:, lat:], out[:, :lat])
        y = pair_dot(y.astype(BF), w1)
        yield
        y = half_silu(y + pre_ref[g * TILE : (g + group) * TILE])
        msg = pair_dot(y, w2)
        yield
        back = [one_hot(along_lanes(loc[col : col + 1], crows) == csub) for col in range(g, g + group)]
        total[0] = total[0] + dot(jnp.concatenate(back, axis=1), msg.astype(BF))

    interleave([[part(g)] for g in range(0, rows, group)], [])
    total = total[0]
    centred = total - jnp.mean(total, axis=1, keepdims=True)
    var = jnp.mean(centred * centred, axis=1, keepdims=True)
    delta = (centred * lax.rsqrt(var + 1e-05) * gain_ref[...]).astype(BF)
    half = half_blocks(chunks)
    high = delta[half * TILE :]
    if high.shape[0] < half * TILE:
        high = jnp.concatenate([high, delta[high.shape[0] : half * TILE]], axis=0)
    rhs = jnp.concatenate([delta[: half * TILE], high], axis=1)
    tiles = nodes // TILE
    size = 3 if tiles % 3 == 0 else 1
    copies = []

    def spread(p):
        hot, upper = [], []
        for t in range(p, p + size):
            word = spread_ref[t * TILE : (t + 1) * TILE]
            hot.append(jnp.concatenate(pick(word.astype(I16), lane, half), axis=1))
            upper.append(word < 0)
        out = dot(jnp.concatenate(hot, axis=0), rhs)
        yield
        back = jnp.where(jnp.concatenate(upper, axis=0), out[:, lat:], out[:, :lat])
        sl = pl.ds(p * TILE, size * TILE)
        out_s[sl] = (fine_ref[sl].astype(F32) + back).astype(BF)
        copies.append(pltpu.make_async_copy(out_s.at[sl], out_ref.at[sl], sem.at[p]))
        copies[-1].start()

    interleave([[spread(p)] for p in range(0, tiles, size)], [])
    for c in copies:
        c.wait()


def on_device(
    node_latent, edge_latent, receivers, senders, coarse_map, coarse_recv, coarse_send,
    edge_w1, mod_u, mod_v, edge_w2, edge_gain, node_w1, node_w2, node_gain,
    coarse_w1, coarse_w2, coarse_gain,
):
    axes = ("dom", "sub")
    size = lax.axis_size(axes)
    dev = lax.axis_index(axes).astype(jnp.int32).reshape(1)
    nodes, lat = node_latent.shape
    edges = edge_latent.shape[0]
    tiles = nodes // TILE
    per = edges // tiles
    crows = nodes // COARSEN
    steps = tiles // STEP
    cmap2 = coarse_map.reshape(tiles, TILE)
    vm = pl.BlockSpec(memory_space=pltpu.VMEM)
    sm = pl.BlockSpec(memory_space=pltpu.SMEM)
    hb = pl.BlockSpec(memory_space=pltpu.HBM)
    hbm = (
        node_latent, cmap2, senders.reshape(edges // TILE, TILE),
        receivers.reshape(edges // TILE, TILE), edge_w1, mod_u.T, mod_v, edge_w2, node_w1,
        node_w2, edge_gain.reshape(1, lat), node_gain.reshape(1, lat),
    )
    big = (STEP * per, lat)
    apart = lambda a: pltpu.with_memory_space_constraint(a, pltpu.HBM)
    far = apart(edge_latent)
    count = steps - 2
    full = jax.ShapeDtypeStruct((edges, lat), BF)
    ready = [
        jax.ShapeDtypeStruct(shape, dtype)
        for shape, dtype in [((nodes, lat), BF)] * 2
        + [((2 * lat, 2 * lat), BF)] * 2
        + [((1, lat), F32), ((2 * lat, lat), BF), ((2 * lat, 2 * lat), BF), ((2 * lat, 2 * lat), BF)]
        + [((steps, TILE, PAD), jnp.int32), ((steps, PAD, TILE), jnp.int32)]
    ]
    shape = jax.ShapeDtypeStruct
    params = pltpu.CompilerParams(vmem_limit_bytes=24 * 2**20)
    rows = STEP * per
    across, within, ws, inner_edges, own, cmap2, *ready = pl.pallas_call(
        ready_kernel,
        in_specs=[sm] + [hb] * (1 + len(hbm)),
        out_specs=[vm] * (6 + len(ready)),
        out_shape=[
            shape((HALO, lat), BF),
            shape((HALO, lat), BF),
            shape((lat, lat), BF),
            shape((count * rows, lat), BF),
            shape((nodes, lat), BF),
            shape(cmap2.shape, cmap2.dtype),
        ] + ready,
        scratch_shapes=[pltpu.VMEM(a.shape, a.dtype) for a in hbm[2:]]
        + [pltpu.SemaphoreType.DMA((len(hbm) + 1,))],
        compiler_params=params,
        name="ready",
    )(dev, far, *[apart(a) for a in hbm])
    pairs = [(i, i + 1) for i in range(1, size - 1, 2)]
    across = lax.ppermute(across, axes, pairs + [(j, i) for i, j in pairs])
    pairs = [(i, i + 1) for i in range(0, size, 2)]
    within = lax.ppermute(within, axes, pairs + [(j, i) for i, j in pairs])
    inner_edges, edge_out, fine, pool, ends = pl.pallas_call(
        functools.partial(inner_kernel, count),
        grid=(count + 2,),
        in_specs=[sm, hb] + [vm] * (3 + len(ready)),
        out_specs=[vm, hb, vm, vm, vm],
        out_shape=[
            shape((count * rows, lat), BF),
            full,
            shape((nodes, lat), BF),
            shape((crows, 2 * lat), F32),
            shape((2 * rows, lat), BF),
        ],
        input_output_aliases={4 + len(ready): 0},
        scratch_shapes=[
            pltpu.VMEM((rows, lat), BF),
            pltpu.VMEM((STEP * TILE, lat), BF),
            pltpu.SemaphoreType.DMA((count + 2,)),
            pltpu.SemaphoreType.DMA((count,)),
        ],
        compiler_params=pltpu.CompilerParams(
            dimension_semantics=("arbitrary",), vmem_limit_bytes=24 * 2**20
        ),
        name="inner",
    )(dev, far, own, cmap2, *ready, inner_edges)
    ends, fine, coarse = pl.pallas_call(
        functools.partial(border_kernel, steps - 1),
        in_specs=[sm] + [vm] * (8 + len(ready)),
        out_specs=[vm] * 3,
        out_shape=[shape((2 * rows, lat), BF), shape((nodes, lat), BF), shape((crows, lat), BF)],
        input_output_aliases={7 + len(ready): 0, 8 + len(ready): 1},
        scratch_shapes=[
            pltpu.VMEM((2 * (STEP * TILE + 2 * HALO), lat), BF),
            pltpu.VMEM((2 * rows, lat), BF),
            pltpu.VMEM((2 * STEP * TILE, lat), BF),
            pltpu.VMEM((crows, 2 * lat), F32),
        ],
        compiler_params=params,
        name="border",
    )(dev, own, across, within, cmap2, pool, ws, *ready, ends, fine)
    tables = [coarse]
    bit = 1
    while bit < size:
        tables.append(lax.ppermute(coarse, axes, [(i, i ^ bit) for i in range(size)]))
        bit *= 2
    cedges = coarse_send.shape[0]
    csend2 = coarse_send.reshape(cedges // TILE, TILE)
    crecv2 = coarse_recv.reshape(cedges // TILE, TILE)
    pre, edge_out, far_words, spread_words = pl.pallas_call(
        functools.partial(near_kernel, steps - 1, len(tables) - 1),
        in_specs=[sm] + [vm] * 7 + [hb],
        out_specs=[vm, hb, vm, vm],
        out_shape=[
            shape((cedges, lat), F32),
            full,
            shape((cedges, TILE), jnp.int32),
            shape((nodes, TILE), jnp.int32),
        ],
        input_output_aliases={8: 1},
        scratch_shapes=[pltpu.SemaphoreType.DMA((3,))],
        compiler_params=params,
        name="near",
    )(dev, csend2, crecv2, cmap2, coarse, coarse_w1, inner_edges, ends, edge_out)
    node_out = pl.pallas_call(
        coarse_kernel,
        in_specs=[sm] + [vm] * (8 + len(tables)),
        out_specs=hb,
        out_shape=jax.ShapeDtypeStruct((nodes, lat), BF),
        scratch_shapes=[pltpu.VMEM((nodes, lat), BF), pltpu.SemaphoreType.DMA((tiles,))],
        compiler_params=pltpu.CompilerParams(vmem_limit_bytes=32 * 2**20),
        name="coarse",
    )(
        dev, crecv2, far_words, spread_words, fine, pre, coarse_w1, coarse_w2, coarse_gain.reshape(1, lat),
        *tables,
    )
    return (node_out, edge_out)


def solution(mesh):
    split = P(("groups", "dom", "sub"))
    wide = P(("groups", "dom", "sub"), None)
    return jax.shard_map(
        on_device,
        mesh=mesh,
        in_specs=(wide, wide) + (split,) * 5 + (P(),) * 11,
        out_specs=(wide, wide),
        check_vma=False,
    )
```

```python
import functools

import jax
import jax.numpy as jnp
from jax import lax
from jax.experimental import pallas as pl
from jax.experimental.pallas import tpu as pltpu
from jax.sharding import PartitionSpec as P

TILE = 128
HALO = 256
COARSEN = 8
STEP = 2
PARTS = 2
LOW = 3
HIGH = (TILE + 2 * HALO) // TILE - LOW
PAD = 16
BF = jnp.bfloat16
F32 = jnp.float32
I16 = jnp.int16


def dot(a, b):
    return jnp.dot(a, b, preferred_element_type=F32)


def one_hot(mask):
    return jnp.where(mask, jnp.ones((), BF), jnp.zeros((), BF))


def pick(off, lane, blocks):
    return [one_hot(off == lane + I16(c * TILE)) for c in range(blocks)]


def aligned(row):
    return row if isinstance(row, int) else pl.multiple_of(row, TILE)


def column(rows_t, col):
    return jnp.broadcast_to(rows_t[:, col : col + 1], (TILE, TILE))


def along_lanes(row, count):
    return jnp.broadcast_to(row, (count, TILE)).astype(I16)


def twice(w):
    z = jnp.zeros_like(w)
    return jnp.concatenate(
        [jnp.concatenate([w, z], axis=1), jnp.concatenate([z, w], axis=1)], axis=0
    )


def pair_dot(x, w2):
    half = x.shape[0] // 2
    out = dot(jnp.concatenate([x[:half], x[half:]], axis=1), w2)
    n = out.shape[1] // 2
    return jnp.concatenate([out[:, :n], out[:, n:]], axis=0)


def gained(w, gain):
    w = w.astype(F32)
    return twice(((w - jnp.mean(w, axis=1, keepdims=True)) * gain).astype(BF))


def mean_weight(gain):
    return 1.0 / (gain * gain * gain.shape[1])


def mean_square(gain):
    lat = gain.shape[1]
    return twice(jnp.broadcast_to(mean_weight(gain), (lat, lat)).T.astype(BF))


def scaled(c, weight):
    return c * lax.rsqrt(jnp.sum(c * c * weight, axis=1, keepdims=True) + 1e-05)


def half_silu(y):
    return (y * jnp.tanh(y) + y).astype(BF)


def interleave(queue, active):
    queue = list(queue)
    while active or queue:
        if queue:
            active = list(queue.pop(0)) + active
        alive = []
        for part in active:
            try:
                next(part)
                alive.append(part)
            except StopIteration:
                pass
        active = alive


def make_stages(block, window, base, held, refs, base_ref):
    edge_ref, own_ref, cmap_ref, fine_ref = refs[:4]
    sent_s, recv_s, we_s, w2_s, m_s, nw1_s, nw2_s, nm_s, code_s, loc_s = refs[4:14]
    hid_s, inc_s, pool_s, per = refs[14:]
    lat = sent_s.shape[1]
    crows = pool_s.shape[0]
    groups = per // TILE
    part = per // PARTS
    lane = lax.broadcasted_iota(I16, (TILE, TILE), 1)
    sub = lax.broadcasted_iota(I16, (TILE, TILE), 0)
    csub = lax.broadcasted_iota(I16, (crows, TILE), 0)
    incoming = {}

    def rows_of(s, k, q):
        start = k * per + q * part
        row = held(s) * per + start
        at = pl.ds(aligned(base(s) * per + start), part)
        return at, slice(row, row + part), start // TILE

    def weights(s, k):
        start = aligned(window(s) + k * TILE)
        at = aligned((block(s) * STEP + k) * TILE)
        mine = recv_s[pl.ds(at, TILE)]
        low = jnp.concatenate([sent_s[pl.ds(start, LOW * TILE)], mine], axis=0)
        high = jnp.concatenate(
            [
                sent_s[pl.ds(start + LOW * TILE, HIGH * TILE)],
                sent_s[pl.ds(start, (LOW - HIGH) * TILE)],
                mine,
            ],
            axis=0,
        )
        return jnp.concatenate([low, high], axis=1)

    def first(s, k, q):
        at, held_at, col0 = rows_of(s, k, q)
        code_t = code_s[block(s)]
        lhs, upper = [], []
        for j in range(part // TILE):
            word = column(code_t, col0 + j)
            o = word.astype(I16) & I16(511)
            r = (word >> 16).astype(I16) & I16(TILE - 1)
            lhs.append(jnp.concatenate(pick(o, lane, LOW) + pick(r, lane, 1), axis=1))
            upper.append(word < 0)
        y = pair_dot(edge_ref[at], we_s[...])
        out = dot(jnp.concatenate(lhs, axis=0), weights(s, k))
        yield
        y = y + jnp.where(jnp.concatenate(upper, axis=0), out[:, lat:], out[:, :lat])
        hid_s[held_at] = half_silu(y)

    def second(s, k, q):
        at, held_at, col0 = rows_of(s, k, q)
        c = pair_dot(hid_s[held_at], w2_s[...])
        yield
        new = (edge_ref[at].astype(F32) + scaled(c, m_s[...])).astype(BF)
        edge_ref[at] = new
        loc = loc_s[block(s)]
        back = [
            one_hot(along_lanes(loc[j : j + 1], TILE) == sub)
            for j in range(col0, col0 + part // TILE)
        ]
        incoming.setdefault(k + held(s), []).append((back, new))
        yield
        if q == PARTS - 1:
            backs, news = zip(*incoming.pop(k + held(s)))
            row = (held(s) + k) * TILE
            inc_s[row : row + TILE] = dot(
                jnp.concatenate(sum(backs, []), axis=1), jnp.concatenate(news, axis=0)
            ).astype(BF)

    def third(s):
        here = pl.ds(aligned(block(s) * STEP * TILE), STEP * TILE)
        own = own_ref[here]
        got = inc_s[held(s) * TILE : (held(s) + STEP) * TILE]
        y = dot(jnp.concatenate([own, got], axis=1), nw1_s[...])
        yield
        c = pair_dot(half_silu(y), nw2_s[...])
        yield
        var = pair_dot((c * c).astype(BF), nm_s[...])
        yield
        fine = (own.astype(F32) + c * lax.rsqrt(var + 1e-05)).astype(BF)
        fine_ref[here] = fine
        member = []
        for k in range(STEP):
            local = cmap_ref[pl.ds(block(s) * STEP + k, 1), :] - base_ref[0] * crows
            member.append(one_hot(along_lanes(local, crows) == csub))
        fine = jnp.concatenate([fine, jnp.ones_like(fine)], axis=1)
        pool_s[...] += dot(jnp.concatenate(member, axis=1), fine)

    return first, second, third


def run_stages(step, count, stages):
    first, second, third = stages
    parts = [(k, q) for k in range(STEP) for q in range(PARTS)]

    def run(one, two, three):
        interleave(
            [
                [second(step - 1, k, q)] * two + [first(step, k, q)] * one
                for k, q in (parts if one or two else [])
            ],
            [third(step - 2)] if three else [],
        )

    for when, which in (
        ((step >= 2) & (step < count), (True, True, True)),
        (step == 0, (True, False, False)),
        (step == 1, (True, True, False)),
        (step == count, (False, True, True)),
        (step == count + 1, (False, False, True)),
    ):
        pl.when(when)(functools.partial(run, *which))


def ready_kernel(base_ref, edge_ref, *refs):
    hbm, refs = refs[:12], refs[12:]
    (across_ref, within_ref, ws_ref, edges_ref, own_ref, cmap_ref), refs = refs[:6], refs[6:]
    ready, vmem, sem = refs[:10], refs[10:20], refs[20]
    send_ref, recv_ref, w1_ref, u_ref, v_ref = vmem[:5]
    edge_w2_ref, node_w1_ref, node_w2_ref, gain_ref, ngain_ref = vmem[5:]
    vmem = (own_ref, cmap_ref) + vmem
    sent_s, recv_s, we_s, w2_s, m_s, nw1_s, nw2_s, nm_s, code_s, loc_s = ready
    rows, lat = own_ref.shape
    idx_rows = send_ref.shape[0] // (rows // TILE) * STEP
    size = idx_rows * TILE
    copies = [pltpu.make_async_copy(a, b, sem.at[i]) for i, (a, b) in enumerate(zip(hbm, vmem))]
    order = [4, 5, 6, 0, 2, 3, 10, 11, 7, 9, 8, 1]
    for i in order:
        copies[i].start()
    early = pltpu.make_async_copy(
        edge_ref.at[pl.ds(size, size)], edges_ref.at[pl.ds(0, size)], sem.at[len(hbm)]
    )
    early.start()
    for i in order[:3]:
        copies[i].wait()
    w_eff = w1_ref[...].astype(F32) + lax.dot_general(
        u_ref[...], v_ref[...], (((0,), (0,)), ((), ())), preferred_element_type=F32
    )
    w_eff = (0.5 * w_eff).astype(BF)
    we_s[...] = twice(w_eff[:lat])
    ws = w_eff[lat : 2 * lat]
    ws_ref[...] = ws
    for i in order[3:]:
        copies[i].wait()
    even = base_ref[0] % 2 == 0
    head, tail = own_ref[:HALO], own_ref[rows - HALO :]
    across_ref[...] = jnp.where(even, head, tail)
    within_ref[...] = jnp.where(even, tail, head)
    both = dot(own_ref[...], jnp.concatenate([ws, w_eff[2 * lat :]], axis=1)).astype(BF)
    sent_s[...] = both[:, :lat]
    recv_s[...] = both[:, lat:]
    w2_s[...] = gained(edge_w2_ref[...], gain_ref[...])
    m_s[...] = mean_weight(gain_ref[...])
    nw1_s[...] = node_w1_ref[...] * 0.5
    nw2_s[...] = gained(node_w2_ref[...], ngain_ref[...])
    nm_s[...] = mean_square(ngain_ref[...])
    recv = recv_ref[...]
    loc = recv & (TILE - 1)
    off = send_ref[...] - (recv - loc) + HALO
    hi = off >= LOW * TILE
    lo = jnp.where(hi, off - LOW * TILE, off)
    code = lo | (loc << 16) | jnp.where(hi, jnp.int32(-(2**31)), 0)
    for s in range(rows // TILE // STEP):
        sl = slice(s * idx_rows, (s + 1) * idx_rows)
        code_s[s, :, 0:idx_rows] = code[sl].T
        loc_s[s, 0:idx_rows] = loc[sl]
    early.wait()


def inner_kernel(count, base_ref, all_ref, own_ref, cmap_ref, *refs):
    ready, refs = refs[:10], refs[11:]
    edges_ref, edge_out_ref, fine_ref, pool_ref, ends_ref, hid_s, inc_s, sem_in, sem_out = refs
    step = pl.program_id(0)
    size = hid_s.shape[0]

    def fetch(n):
        return pltpu.make_async_copy(
            all_ref.at[pl.ds((n + 1) * size, size)], edges_ref.at[pl.ds(n * size, size)],
            sem_in.at[n],
        )

    def store(n):
        return pltpu.make_async_copy(
            edges_ref.at[pl.ds(n * size, size)], edge_out_ref.at[pl.ds((n + 1) * size, size)],
            sem_out.at[n],
        )

    ends = [
        pltpu.make_async_copy(
            all_ref.at[pl.ds(at * size, size)], ends_ref.at[pl.ds(n * size, size)],
            sem_in.at[count + n],
        )
        for n, at in enumerate((0, count + 1))
    ]

    @pl.when(step == 0)
    def _():
        for n in range(1, count):
            fetch(n).start()
        for c in ends:
            c.start()
        pool_ref[...] = jnp.zeros_like(pool_ref)

    @pl.when((step > 0) & (step < count))
    def _():
        fetch(step).wait()

    run_stages(
        step, count,
        make_stages(
            lambda s: s + 1, lambda s: (s + 1) * STEP * TILE - HALO, lambda s: s * STEP,
            lambda s: 0,
            (edges_ref, own_ref, cmap_ref, fine_ref) + ready
            + (hid_s, inc_s, pool_ref, size // STEP),
            base_ref,
        ),
    )

    @pl.when((step > 0) & (step < count))
    def _():
        store(step - 1).start()

    @pl.when(step == count + 1)
    def _():
        for n in range(count - 1):
            store(n).wait()
        for c in ends:
            c.wait()


def border_kernel(
    last_block, base_ref, own_ref, across_ref, within_ref, cmap_ref, pool_ref, ws_ref, *refs
):
    ready, refs = refs[:10], refs[12:]
    ends_ref, fine_ref, coarse_ref, win_s, hid_s, inc_s, pool_s = refs
    sent_ref = ready[0]
    rows, lat = sent_ref.shape
    size = ends_ref.shape[0] // 2
    span = STEP * TILE + 2 * HALO
    inside = span - HALO
    even = base_ref[0] % 2 == 0
    across, within = across_ref[...], within_ref[...]
    ws = ws_ref[...]
    win_s[:HALO] = dot(jnp.where(even, across, within), ws).astype(BF)
    win_s[HALO:span] = sent_ref[:inside]
    win_s[span : span + inside] = sent_ref[rows - inside :]
    win_s[span + inside :] = dot(jnp.where(even, within, across), ws).astype(BF)
    pool_s[...] = pool_ref[...]
    first, second, third = make_stages(
        lambda s: s * last_block, lambda s: s * span, lambda s: s * STEP, lambda s: s * STEP,
        (ends_ref, own_ref, cmap_ref, fine_ref, win_s) + ready[1:]
        + (hid_s, inc_s, pool_s, size // STEP),
        base_ref,
    )
    parts = [(s, k, q) for s in range(2) for k in range(STEP) for q in range(PARTS)]
    half = STEP * PARTS
    ticks = [[] for _ in range(2 * half + 8)]
    for n, p in enumerate(parts):
        ticks[n].append(first(*p))
        ticks[n + 3].insert(0, second(*p))
    for s in range(2):
        done = (s + 1) * half + 5
        ticks[done].append(third(s))
    interleave(ticks, [])
    total = pool_s[...]
    coarse_ref[...] = (total[:, :lat] / jnp.maximum(total[:, lat:], 1.0)).astype(BF)


def half_blocks(blocks):
    return (blocks + 1) // 2


def in_halves(row, half):
    hi = row >= half * TILE
    return jnp.where(hi, (row - half * TILE) | jnp.int32(-(2**31)), row)


def near_kernel(
    last_block, partners, base_ref, send_ref, recv_ref, cmap_ref, own_ref, w1_ref, edges_ref,
    ends_ref, _, pre_ref, edge_out_ref, far_ref, spread_ref, sem
):
    size = ends_ref.shape[0] // 2
    copies = [
        pltpu.make_async_copy(
            source.at[pl.ds(row, size)], edge_out_ref.at[pl.ds(at * size, size)], sem.at[n]
        )
        for n, (source, row, at) in enumerate(
            (
                (ends_ref, 0, 0),
                (ends_ref, size, last_block),
                (edges_ref, edges_ref.shape[0] - size, last_block - 1),
            )
        )
    ]
    for c in copies:
        c.start()
    crows, lat = own_ref.shape
    rows = send_ref.shape[0]
    tiles = cmap_ref.shape[0]
    first = base_ref[0] * crows
    blocks = crows // TILE
    half, lows = half_blocks(blocks), half_blocks(blocks * partners)
    send = send_ref[...]
    owner = lax.div(send, jnp.full_like(send, crows))
    other = owner ^ base_ref[0]
    slot = jnp.full_like(send, -1)
    for j in range(partners):
        slot = jnp.where(other == (1 << j), j, slot)
    far = in_halves(jnp.where(slot < 0, 2 * lows * TILE, send - owner * crows + slot * crows), lows)
    far_t = far.T
    spread_t = in_halves(cmap_ref[...] - first, half).T
    send = send - first
    mine = (send >= 0) & (send < crows)
    code_t = (jnp.where(mine, send, crows) | ((recv_ref[...] - first) << 16)).T
    w1 = w1_ref[...] * 0.5
    rhs = dot(own_ref[...], jnp.concatenate([w1[:lat], w1[lat:]], axis=1)).astype(BF)
    rhs = jnp.concatenate([rhs[:, :lat], rhs[:, lat:]], axis=0)
    lane = lax.broadcasted_iota(I16, (TILE, TILE), 1)
    group = 3 if rows % 3 == 0 else 1

    def part(g):
        lhs = []
        for col in range(g, g + group):
            word = column(code_t, col)
            o, r = word.astype(I16), (word >> 16).astype(I16)
            lhs.append(jnp.concatenate(pick(o, lane, blocks) + pick(r, lane, blocks), axis=1))
        out = dot(jnp.concatenate(lhs, axis=0), rhs)
        yield
        pre_ref[g * TILE : (g + group) * TILE] = out
        for col in range(g, g + group):
            far_ref[col * TILE : (col + 1) * TILE] = column(far_t, col)
        for col in range(g * tiles // rows, (g + group) * tiles // rows):
            spread_ref[col * TILE : (col + 1) * TILE] = column(spread_t, col)

    interleave([[part(g)] for g in range(0, rows, group)], [])
    for c in copies:
        c.wait()


def coarse_kernel(
    base_ref, recv_ref, far_ref, spread_ref, fine_ref, pre_ref, w1_ref, w2_ref, gain_ref, *refs
):
    (own_ref, *tables), (out_ref, out_s, sem) = refs[:-3], refs[-3:]
    dev = base_ref[0]
    crows, lat = own_ref.shape
    rows = recv_ref.shape[0]
    nodes = fine_ref.shape[0]
    chunks = crows // TILE
    lows = half_blocks(chunks * len(tables))
    loc = recv_ref[...] - dev * crows
    w1 = twice(w1_ref[:lat] * 0.5)
    proj = jnp.concatenate([t[...] for t in tables], axis=0)
    low, high = proj[: lows * TILE], proj[lows * TILE :]
    if high.shape[0] < low.shape[0]:
        high = jnp.concatenate([high, low[high.shape[0] :]], axis=0)
    rhs = jnp.concatenate([low, high], axis=1)
    lane = lax.broadcasted_iota(I16, (TILE, TILE), 1)
    csub = lax.broadcasted_iota(I16, (crows, TILE), 0)
    w2 = twice(w2_ref[...])
    group = next(g for g in (9, 6, 3, 2, 1) if rows % g == 0)
    total = [own_ref[...].astype(F32)]

    def part(g):
        lhs, upper = [], []
        for col in range(g, g + group):
            word = far_ref[col * TILE : (col + 1) * TILE]
            lhs.append(jnp.concatenate(pick(word.astype(I16), lane, lows), axis=1))
            upper.append(word < 0)
        out = dot(jnp.concatenate(lhs, axis=0), rhs)
        yield
        y = jnp.where(jnp.concatenate(upper, axis=0), out[:, lat:], out[:, :lat])
        y = pair_dot(y.astype(BF), w1)
        yield
        y = half_silu(y + pre_ref[g * TILE : (g + group) * TILE])
        msg = pair_dot(y, w2)
        yield
        back = [one_hot(along_lanes(loc[col : col + 1], crows) == csub) for col in range(g, g + group)]
        total[0] = total[0] + dot(jnp.concatenate(back, axis=1), msg.astype(BF))

    interleave([[part(g)] for g in range(0, rows, group)], [])
    total = total[0]
    centred = total - jnp.mean(total, axis=1, keepdims=True)
    var = jnp.mean(centred * centred, axis=1, keepdims=True)
    delta = (centred * lax.rsqrt(var + 1e-05) * gain_ref[...]).astype(BF)
    half = half_blocks(chunks)
    high = delta[half * TILE :]
    if high.shape[0] < half * TILE:
        high = jnp.concatenate([high, delta[high.shape[0] : half * TILE]], axis=0)
    rhs = jnp.concatenate([delta[: half * TILE], high], axis=1)
    tiles = nodes // TILE
    size = 3 if tiles % 3 == 0 else 1
    copies = []

    def spread(p):
        hot, upper = [], []
        for t in range(p, p + size):
            word = spread_ref[t * TILE : (t + 1) * TILE]
            hot.append(jnp.concatenate(pick(word.astype(I16), lane, half), axis=1))
            upper.append(word < 0)
        out = dot(jnp.concatenate(hot, axis=0), rhs)
        yield
        back = jnp.where(jnp.concatenate(upper, axis=0), out[:, lat:], out[:, :lat])
        sl = pl.ds(p * TILE, size * TILE)
        out_s[sl] = (fine_ref[sl].astype(F32) + back).astype(BF)
        copies.append(pltpu.make_async_copy(out_s.at[sl], out_ref.at[sl], sem.at[p]))
        copies[-1].start()

    interleave([[spread(p)] for p in range(0, tiles, size)], [])
    for c in copies:
        c.wait()


def on_device(
    node_latent, edge_latent, receivers, senders, coarse_map, coarse_recv, coarse_send,
    edge_w1, mod_u, mod_v, edge_w2, edge_gain, node_w1, node_w2, node_gain,
    coarse_w1, coarse_w2, coarse_gain,
):
    axes = ("dom", "sub")
    size = lax.axis_size(axes)
    dev = lax.axis_index(axes).astype(jnp.int32).reshape(1)
    nodes, lat = node_latent.shape
    edges = edge_latent.shape[0]
    tiles = nodes // TILE
    per = edges // tiles
    crows = nodes // COARSEN
    steps = tiles // STEP
    cmap2 = coarse_map.reshape(tiles, TILE)
    vm = pl.BlockSpec(memory_space=pltpu.VMEM)
    sm = pl.BlockSpec(memory_space=pltpu.SMEM)
    hb = pl.BlockSpec(memory_space=pltpu.HBM)
    hbm = (
        node_latent, cmap2, senders.reshape(edges // TILE, TILE),
        receivers.reshape(edges // TILE, TILE), edge_w1, mod_u.T, mod_v, edge_w2, node_w1,
        node_w2, edge_gain.reshape(1, lat), node_gain.reshape(1, lat),
    )
    big = (STEP * per, lat)
    apart = lambda a: pltpu.with_memory_space_constraint(a, pltpu.HBM)
    far = apart(edge_latent)
    count = steps - 2
    full = jax.ShapeDtypeStruct((edges, lat), BF)
    ready = [
        jax.ShapeDtypeStruct(shape, dtype)
        for shape, dtype in [((nodes, lat), BF)] * 2
        + [((2 * lat, 2 * lat), BF)] * 2
        + [((1, lat), F32), ((2 * lat, lat), BF), ((2 * lat, 2 * lat), BF), ((2 * lat, 2 * lat), BF)]
        + [((steps, TILE, PAD), jnp.int32), ((steps, PAD, TILE), jnp.int32)]
    ]
    shape = jax.ShapeDtypeStruct
    params = pltpu.CompilerParams(vmem_limit_bytes=24 * 2**20)
    rows = STEP * per
    across, within, ws, inner_edges, own, cmap2, *ready = pl.pallas_call(
        ready_kernel,
        in_specs=[sm] + [hb] * (1 + len(hbm)),
        out_specs=[vm] * (6 + len(ready)),
        out_shape=[
            shape((HALO, lat), BF),
            shape((HALO, lat), BF),
            shape((lat, lat), BF),
            shape((count * rows, lat), BF),
            shape((nodes, lat), BF),
            shape(cmap2.shape, cmap2.dtype),
        ] + ready,
        scratch_shapes=[pltpu.VMEM(a.shape, a.dtype) for a in hbm[2:]]
        + [pltpu.SemaphoreType.DMA((len(hbm) + 1,))],
        compiler_params=params,
        name="ready",
    )(dev, far, *[apart(a) for a in hbm])
    pairs = [(i, i + 1) for i in range(1, size - 1, 2)]
    across = lax.ppermute(across, axes, pairs + [(j, i) for i, j in pairs])
    pairs = [(i, i + 1) for i in range(0, size, 2)]
    within = lax.ppermute(within, axes, pairs + [(j, i) for i, j in pairs])
    inner_edges, edge_out, fine, pool, ends = pl.pallas_call(
        functools.partial(inner_kernel, count),
        grid=(count + 2,),
        in_specs=[sm, hb] + [vm] * (3 + len(ready)),
        out_specs=[vm, hb, vm, vm, vm],
        out_shape=[
            shape((count * rows, lat), BF),
            full,
            shape((nodes, lat), BF),
            shape((crows, 2 * lat), F32),
            shape((2 * rows, lat), BF),
        ],
        input_output_aliases={4 + len(ready): 0},
        scratch_shapes=[
            pltpu.VMEM((rows, lat), BF),
            pltpu.VMEM((STEP * TILE, lat), BF),
            pltpu.SemaphoreType.DMA((count + 2,)),
            pltpu.SemaphoreType.DMA((count,)),
        ],
        compiler_params=pltpu.CompilerParams(
            dimension_semantics=("arbitrary",), vmem_limit_bytes=24 * 2**20
        ),
        name="inner",
    )(dev, far, own, cmap2, *ready, inner_edges)
    ends, fine, coarse = pl.pallas_call(
        functools.partial(border_kernel, steps - 1),
        in_specs=[sm] + [vm] * (8 + len(ready)),
        out_specs=[vm] * 3,
        out_shape=[shape((2 * rows, lat), BF), shape((nodes, lat), BF), shape((crows, lat), BF)],
        input_output_aliases={7 + len(ready): 0, 8 + len(ready): 1},
        scratch_shapes=[
            pltpu.VMEM((2 * (STEP * TILE + 2 * HALO), lat), BF),
            pltpu.VMEM((2 * rows, lat), BF),
            pltpu.VMEM((2 * STEP * TILE, lat), BF),
            pltpu.VMEM((crows, 2 * lat), F32),
        ],
        compiler_params=params,
        name="border",
    )(dev, own, across, within, cmap2, pool, ws, *ready, ends, fine)
    tables = [coarse]
    bit = 1
    while bit < size:
        tables.append(lax.ppermute(coarse, axes, [(i, i ^ bit) for i in range(size)]))
        bit *= 2
    cedges = coarse_send.shape[0]
    csend2 = coarse_send.reshape(cedges // TILE, TILE)
    crecv2 = coarse_recv.reshape(cedges // TILE, TILE)
    pre, edge_out, far_words, spread_words = pl.pallas_call(
        functools.partial(near_kernel, steps - 1, len(tables) - 1),
        in_specs=[sm] + [vm] * 7 + [hb],
        out_specs=[vm, hb, vm, vm],
        out_shape=[
            shape((cedges, lat), F32),
            full,
            shape((cedges, TILE), jnp.int32),
            shape((nodes, TILE), jnp.int32),
        ],
        input_output_aliases={8: 1},
        scratch_shapes=[pltpu.SemaphoreType.DMA((3,))],
        compiler_params=params,
        name="near",
    )(dev, csend2, crecv2, cmap2, coarse, coarse_w1, inner_edges, ends, edge_out)
    node_out = pl.pallas_call(
        coarse_kernel,
        in_specs=[sm] + [vm] * (8 + len(tables)),
        out_specs=hb,
        out_shape=jax.ShapeDtypeStruct((nodes, lat), BF),
        scratch_shapes=[pltpu.VMEM((nodes, lat), BF), pltpu.SemaphoreType.DMA((tiles,))],
        compiler_params=pltpu.CompilerParams(vmem_limit_bytes=32 * 2**20),
        name="coarse",
    )(
        dev, crecv2, far_words, spread_words, fine, pre, coarse_w1, coarse_w2, coarse_gain.reshape(1, lat),
        *tables,
    )
    return (node_out, edge_out)


def solution(mesh):
    split = P(("groups", "dom", "sub"))
    wide = P(("groups", "dom", "sub"), None)
    return jax.shard_map(
        on_device,
        mesh=mesh,
        in_specs=(wide, wide) + (split,) * 5 + (P(),) * 11,
        out_specs=(wide, wide),
        check_vma=False,
    )
```
